128 devices in a mesh: bis: 16 (over y, z), dom: 8 (over x, core).
Axes of the slice: x: 4, y: 4, z: 4, core: 2. Of those that a mesh axis runs over, the one named last changes fastest.
Arguments:
- positions: float32 [16, 256, 3, 128], P('bis', 'dom'), may hold values from 0 to 1
- velocities: float32 [16, 256, 3, 128], P('bis', 'dom'), may hold values from -3 to 3
- radii: float32 [16, 256, 128], P('bis', 'dom'), may hold values from 0.05 to 0.12
- drag_rates: float32 [16, 256, 128], P('bis', 'dom'), may hold values from 1 to 6
- mig_slots: int32 [16, 24, 16], P('bis', 'dom'), may hold values from 0 to 31, as said below
- mig_counts: int32 [16, 24], P('bis', 'dom'), may hold values from 1 to 16, as said below
- pair_lists: int32 [16, 2, 1536], P('bis', None, 'dom'), may hold values from 0 to 39, as said below
- pair_counts: int32 [16, 8], P('bis', 'dom'), may hold values from 48 to 192, as said below
- owners: int32 [16, 256], P('bis', 'dom'), may hold values from 0 to 2047
- dep_weights: bfloat16 [16, 256, 128, 128], P('bis', 'dom'), may hold values from 0 to 0.015625
- fluid_velocity: float32 [8, 2048, 3, 128], P('dom', 'bis'), may hold values from -6 to 6
Outputs:
- positions_out: float32 [16, 256, 3, 128], P('bis', 'dom')
- velocities_out: float32 [16, 256, 3, 128], P('bis', 'dom')
- fluid_out: float32 [8, 2048, 3, 128], P('dom', 'bis')
- voidage: float32 [8, 2048, 128], P('dom', 'bis')
The draws below stay inside these ranges and needn't reach their ends.
Inputs may be any that keep to these rules, and one draw needn't show every extreme that they name: `mig_slots`: within one device and level the 16 slots are distinct block indices. `mig_counts`: at level l the two devices whose bis indices differ only in bit l, at the same dom index, have equal counts; some such pair has exactly 16. `pair_lists`: row 0 holds blocks below 32; row 1 indexes the 40 extended blocks; entries past a device's count are unused. `pair_counts`: each count is 192 divided by 1, 2, 3 or 4, rounded down; some device has exactly 192.
All inputs are finite; a program needn't handle non-finite values.
Results may differ from the reference program's by a relative error of at most 0.0003.
Values may be sent and summed in bfloat16 or wider, within the bound.
A program may use at most 64 MiB of HBM per device.

```python
import math
import jax
import jax.numpy as jnp
import numpy as np
from jax import lax

BLK = 128
CELLS = 128
NB = 32
G = 4
LEVELS = 3
SUBSTEPS = 2
PAIR_BATCH = 16
CAP = 16
PMAX = 192
GROUPS = 16
DOMAINS = 8
PBLK = 256
FBCOL = 2048


def draw_positions(key, part):
    key = jax.random.fold_in(key, 41)
    spread = jax.random.uniform(key, (GROUPS, PBLK, 3, BLK), jnp.float32)
    return (0.3 + 0.4 * spread).astype(jnp.float32)


def draw_mig_slots(key, part):
    keys = jax.random.split(key, GROUPS * DOMAINS * LEVELS)
    orders = jax.vmap(lambda one_key: jax.random.permutation(one_key, NB))(keys)
    return orders[:, :CAP].astype(jnp.int32).reshape(GROUPS, DOMAINS * LEVELS, CAP)


def draw_mig_counts(key, part):
    base_counts = jax.random.randint(key, (GROUPS, DOMAINS, LEVELS), 1, CAP + 1).astype(jnp.int32)
    group_idx = jnp.arange(GROUPS, dtype=jnp.int32)[:, None, None]
    domain_idx = jnp.arange(DOMAINS, dtype=jnp.int32)[None, :, None]
    level_idx = jnp.arange(LEVELS, dtype=jnp.int32)[None, None, :]
    level_bit = jnp.left_shift(jnp.int32(1), level_idx)
    lower = jnp.bitwise_and(group_idx, jnp.bitwise_not(level_bit))
    lower = jnp.broadcast_to(lower, (GROUPS, DOMAINS, LEVELS))
    counts = jnp.take_along_axis(base_counts, lower, axis=0)
    group_pick = jax.random.randint(jax.random.fold_in(key, 11), (), 0, GROUPS).astype(jnp.int32)
    domain_pick = jax.random.randint(jax.random.fold_in(key, 12), (), 0, DOMAINS).astype(jnp.int32)
    level_pick = jax.random.randint(jax.random.fold_in(key, 13), (), 0, LEVELS).astype(jnp.int32)
    pick_lower = jnp.bitwise_and(group_pick, jnp.bitwise_not(jnp.left_shift(jnp.int32(1), level_pick)))
    chosen = (lower == pick_lower) & (domain_idx == domain_pick) & (level_idx == level_pick)
    counts = jnp.where(chosen, CAP, counts)
    return counts.astype(jnp.int32).reshape(GROUPS, DOMAINS * LEVELS)


def draw_pair_lists(key, part):
    left = jax.random.randint(jax.random.fold_in(key, 21), (GROUPS, 1, DOMAINS * PMAX), 0, NB)
    right = jax.random.randint(jax.random.fold_in(key, 22), (GROUPS, 1, DOMAINS * PMAX), 0, NB + 2 * G)
    return jnp.concatenate([left, right], axis=1).astype(jnp.int32)


def draw_pair_counts(key, part):
    divisor = jax.random.randint(jax.random.fold_in(key, 31), (GROUPS * DOMAINS,), 1, 5).astype(jnp.int32)
    counts = PMAX // divisor
    where_full = jax.random.randint(jax.random.fold_in(key, 32), (), 0, GROUPS * DOMAINS)
    counts = jnp.where(jnp.arange(GROUPS * DOMAINS, dtype=jnp.int32) == where_full, PMAX, counts)
    return counts.astype(jnp.int32).reshape(GROUPS, DOMAINS)


def plant(array, own_key, least, largest):
    longest = array.shape.index(max(array.shape))
    spots = []
    for shift in (0, 1):
        where = [jax.random.randint(jax.random.fold_in(own_key, axis), (), 0, length) for axis, length in enumerate(array.shape)]
        where[longest] = (where[longest] + shift) % array.shape[longest]
        spots.append(tuple(where))
    return array.at[spots[0]].set(least).at[spots[1]].set(largest)


def steps_of(rng, extent, cuts, smallest, largest):
    loudness, own = 1.0, jax.random.fold_in(rng, 6)
    for axis_at, shards_of in cuts:
        draws = jnp.exp(jax.random.uniform(jax.random.fold_in(own, axis_at), (shards_of,), jnp.float32, smallest / len(cuts), largest / len(cuts)))
        loudness = loudness * jnp.repeat(draws, extent[axis_at] // shards_of).reshape([-1 if axis == axis_at else 1 for axis in range(len(extent))])
    return loudness


def rank_table(amount, lean):
    portions = [(1 << 20) // math.isqrt(rank ** lean) + 1 for rank in range(1, amount + 1)]
    deviation = 1 + sum(portions) // (1 << 30)
    return np.cumsum(np.array([max(1, weight // deviation) for weight in portions]))


def skewed_ids(rng, dims, number_of, lean):
    listing = rank_table(number_of, lean)
    lot = jax.random.randint(jax.random.fold_in(rng, 1), dims, 0, int(listing[number_of - 1]))
    rank = jnp.searchsorted(jnp.asarray(listing, jnp.int32), lot, side="right")
    return jax.random.permutation(jax.random.fold_in(rng, 2), number_of)[rank].astype(jnp.int32)


def scatter_about(key, dims, deviation, reach, cuts=(), kind=jnp.bfloat16):
    drawn = jax.random.normal(key, dims, jnp.float32) * deviation
    if len(cuts) > 0:
        drawn = steps_of(key, dims, cuts, -0.22, 0.18) * drawn
    return jnp.clip(drawn, min=-reach, max=reach).astype(kind)


def setup_inputs(seed: int = 0) -> dict:
    key_list = jax.random.split(jax.random.key(seed), 12)
    return {
        "positions": draw_positions(jax.random.fold_in(key_list[11], 71), 0),
        "velocities": scatter_about(key_list[1], (GROUPS, PBLK, 3, BLK), 0.5, 3.0, ((0, 16), (1, 8)), jnp.float32),
        "radii": jnp.clip(jnp.exp(math.log(0.12) - 0.8754687 * jax.random.uniform(key_list[2], (GROUPS, PBLK, BLK), jnp.float32) ** steps_of(key_list[2], (GROUPS, PBLK, BLK), ((0, 16), (1, 8)), -0.2, 0.2)), 0.05, 0.12),
        "drag_rates": jnp.clip(jnp.exp(math.log(6.0) - 1.7917595 * jax.random.uniform(key_list[3], (GROUPS, PBLK, BLK), jnp.float32) ** steps_of(key_list[3], (GROUPS, PBLK, BLK), ((0, 16), (1, 8)), -0.2, 0.2)), 1.0, 6.0),
        "mig_slots": draw_mig_slots(jax.random.fold_in(key_list[11], 71), 0),
        "mig_counts": draw_mig_counts(jax.random.fold_in(key_list[11], 71), 0),
        "pair_lists": draw_pair_lists(jax.random.fold_in(key_list[11], 71), 0),
        "pair_counts": draw_pair_counts(jax.random.fold_in(key_list[11], 71), 0),
        "owners": plant(skewed_ids(key_list[8], (GROUPS, PBLK), FBCOL, 1), jax.random.fold_in(key_list[8], 3), 0, FBCOL - 1).astype(jnp.int32),
        "dep_weights": jnp.clip(0.015625 * jax.random.uniform(key_list[9], (GROUPS, PBLK, BLK, CELLS), jnp.float32) ** steps_of(key_list[9], (GROUPS, PBLK, BLK, CELLS), ((0, 16), (1, 8)), -0.2, 0.2), 0.0, 0.015625).astype(jnp.bfloat16),
        "fluid_velocity": scatter_about(key_list[10], (DOMAINS, FBCOL, 3, CELLS), 1.0, 6.0, ((0, 8), (1, 16)), jnp.float32),
    }


STIFFNESS = 5.0
DAMPING = 1.0
TIME_STEP = 0.05
EPS_DIST = 0.0001
RADIUS_REF = 0.1
FLUID_GAIN = 0.2

def pair_forces(left_blk, right_blk):
    offset = left_blk[:, 0:3, :, None] - right_blk[:, 0:3, None, :]
    distance = jnp.sqrt(lax.optimization_barrier(jnp.sum(offset * offset, axis=1)) + EPS_DIST)
    intersection = jnp.maximum(left_blk[:, 6, :, None] + right_blk[:, 6, None, :] - distance, 0.0)
    rel_vel = left_blk[:, 3:6, :, None] - right_blk[:, 3:6, None, :]
    normal_speed = lax.optimization_barrier(jnp.sum(rel_vel * offset, axis=1)) / distance
    factor = intersection * (STIFFNESS - DAMPING * normal_speed) / distance
    return lax.optimization_barrier(jnp.sum(factor[:, None] * offset, axis=3))

def contact_forces(padded, left_ids, right_ids, pair_total, batches):
    blocks = padded.shape[0] - 2 * G
    empty_sum = jnp.zeros((blocks, 3 * padded.shape[2]), jnp.float32)

    def accumulate(batch_idx, summed):
        first_row = batch_idx * PAIR_BATCH
        left = lax.dynamic_slice_in_dim(left_ids, first_row, PAIR_BATCH)
        right = lax.dynamic_slice_in_dim(right_ids, first_row, PAIR_BATCH)
        is_live = first_row + jnp.arange(PAIR_BATCH, dtype=jnp.int32) < pair_total
        forces = pair_forces(padded[left + G], padded[right])
        forces = jnp.where(is_live[:, None, None], forces, 0.0)
        onehot = (jnp.arange(blocks, dtype=jnp.int32)[:, None] == left[None, :]).astype(jnp.float32)
        return summed + jnp.dot(onehot, forces.reshape(PAIR_BATCH, -1), precision=lax.Precision.HIGHEST)
    return lax.fori_loop(0, batches, accumulate, empty_sum)

def reference(positions, velocities, radii, drag_rates, mig_slots, mig_counts, pair_lists, pair_counts, owners, dep_weights, fluid_velocity):
    particle_state = jnp.concatenate([positions, velocities, radii[:, :, None], drag_rates[:, :, None]], axis=2)
    particle_state = particle_state.reshape(GROUPS, DOMAINS, NB, 8, BLK)
    slot_table = mig_slots.reshape(GROUPS, DOMAINS, LEVELS, CAP)
    count_table = mig_counts.reshape(GROUPS, DOMAINS, LEVELS)
    group_idx = jnp.arange(GROUPS, dtype=jnp.int32)
    slot_idx = jnp.arange(CAP, dtype=jnp.int32)
    take_rows = jax.vmap(jax.vmap(lambda blocks, where_at: blocks[where_at]))
    put_rows = jax.vmap(jax.vmap(lambda blocks, where_at, values: blocks.at[where_at].set(values)))
    for bit_level in range(LEVELS):
        slot_list = slot_table[:, :, bit_level]
        outgoing = take_rows(particle_state, slot_list)
        partner = jnp.bitwise_xor(group_idx, 1 << bit_level)
        incoming = outgoing[partner]
        is_live = slot_idx[None, None, :] < count_table[:, :, bit_level][:, :, None]
        chosen = jnp.where(is_live[..., None, None], incoming, outgoing)
        particle_state = put_rows(particle_state, slot_list, chosen)
    fluid_bf = fluid_velocity.astype(jnp.bfloat16)
    owner_map = owners.reshape(GROUPS, DOMAINS, NB)
    weights = dep_weights.reshape(GROUPS, DOMAINS, NB, BLK, CELLS)

    def interpolate(inputs):
        owner_group, weight_group = inputs
        fluid_blk = jax.vmap(lambda field, which: field[which])(fluid_bf, owner_group)
        return jnp.einsum('dnpc,dnkc->dnkp', weight_group.astype(jnp.float32), fluid_blk.astype(jnp.float32))
    sampled = lax.map(interpolate, (owner_map, weights))
    pair_table = jnp.transpose(pair_lists.reshape(GROUPS, 2, DOMAINS, PMAX), (0, 2, 1, 3)).reshape(GROUPS * DOMAINS, 2, PMAX)
    totals_pairs = pair_counts.reshape(GROUPS * DOMAINS)

    def device_force(inputs):
        padded, pair_rows, pair_total = inputs
        return contact_forces(padded, pair_rows[0], pair_rows[1], pair_total, PMAX // PAIR_BATCH)
    for substep in range(SUBSTEPS):
        before = jnp.roll(particle_state, 1, axis=1)[:, :, NB - G:]
        after = jnp.roll(particle_state, -1, axis=1)[:, :, :G]
        extended = jnp.concatenate([before, particle_state, after], axis=2)
        extended = extended.reshape(GROUPS * DOMAINS, NB + 2 * G, 8, BLK)
        contact = lax.map(device_force, (extended, pair_table, totals_pairs))
        contact = contact.reshape(GROUPS, DOMAINS, NB, 3, BLK)
        masses = (particle_state[:, :, :, 6] / RADIUS_REF) ** 3
        beta = particle_state[:, :, :, 7]
        velocity = particle_state[:, :, :, 3:6]
        velocity = velocity + TIME_STEP * (contact / masses[:, :, :, None] + beta[:, :, :, None] * (sampled - velocity))
        position = particle_state[:, :, :, 0:3] + TIME_STEP * velocity
        particle_state = jnp.concatenate([position, velocity, particle_state[:, :, :, 6:8]], axis=3)
    masses = (particle_state[:, :, :, 6] / RADIUS_REF) ** 3
    beta = particle_state[:, :, :, 7]
    velocity = particle_state[:, :, :, 3:6]
    payload = jnp.concatenate([(masses * beta)[:, :, :, None] * (sampled - velocity), masses[:, :, :, None]], axis=3).astype(jnp.bfloat16)

    def deposit(inputs):
        payload_group, weight_group = inputs
        return jnp.einsum('dnkp,dnpc->dnkc', payload_group.astype(jnp.float32), weight_group.astype(jnp.float32))
    deposits = lax.map(deposit, (payload, weights))
    deposits = jnp.transpose(deposits, (1, 0, 2, 3, 4)).reshape(DOMAINS, GROUPS * NB, 4 * CELLS)
    owner_cols = jnp.transpose(owner_map, (1, 0, 2)).reshape(DOMAINS, GROUPS * NB)
    totals = jax.vmap(lambda rows, which: jax.ops.segment_sum(rows, which, num_segments=FBCOL))(deposits, owner_cols)
    totals = totals.reshape(DOMAINS, FBCOL, 4, CELLS)
    solid = totals[:, :, 3]
    voidage = 1.0 / (1.0 + solid)
    fluid_out = fluid_velocity - FLUID_GAIN * totals[:, :, 0:3] / (1.0 + solid)[:, :, None]
    final = particle_state.reshape(GROUPS, PBLK, 8, BLK)
    return (final[:, :, 0:3], final[:, :, 3:6], fluid_out, voidage)
```

```python
import jax
import jax.numpy as jnp
from jax import lax
from jax.experimental import pallas as pl
from jax.experimental.pallas import tpu as pltpu

from jax.sharding import PartitionSpec as P

G = 4
SUBSTEPS = 2
PAIR_BATCH = 16


STIFFNESS = 5.0
DAMPING = 1.0
TIME_STEP = 0.05
EPS_DIST = 0.0001
RADIUS_REF = 0.1
FLUID_GAIN = 0.2


def from_partner(value, axis, stride):
    mask = 2**stride
    pairs = [(source, source ^ mask) for source in range(lax.axis_size(axis))]
    return lax.ppermute(value, axis, pairs)


def with_halo(block, sides, width):
    for axis, dim in sides:
        count = lax.axis_size(axis)
        forward = [(i, i + 1) for i in range(count - 1)]
        forward.append((count - 1, 0))
        backward = [(target, source) for source, target in forward]
        low = lax.ppermute(
            lax.slice_in_dim(block, block.shape[dim] - width, None, axis=dim), axis, forward
        )
        high = lax.ppermute(lax.slice_in_dim(block, 0, width, axis=dim), axis, backward)
        block = jnp.concatenate([low, block, high], axis=dim)
    return block


PAIRS = 192

def rowsel(rows, zero):
    row = lax.broadcasted_iota(jnp.int32, (8, 128), 0)
    out = zero
    for k, r in enumerate(rows):
        if r is not None:
            out = jnp.where(row == k, r, out)
    return out

def bf(x):
    return x.astype(jnp.bfloat16).astype(jnp.float32)

def split3(x):
    s1 = bf(x)
    r = x - s1
    s2 = bf(r)
    return s1, s2, bf(r - s2)

def centered(blk):
    row = lax.broadcasted_iota(jnp.int32, (8, 128), 0)
    return jnp.where(row < 3, blk - 0.5, blk)

def partner_features(blk):
    row = lax.broadcasted_iota(jnp.int32, (8, 128), 0)
    y = centered(blk)
    sq = jnp.sum(y[0:3] * y[0:3], axis=0, keepdims=True)
    sv = jnp.sum(y[0:3] * y[3:6], axis=0, keepdims=True)
    s1, s2, s3 = split3(jnp.where(row < 6, y, 1.0))
    n = split3(sq)
    s = split3(sv)
    e = rowsel([n[0], n[1], n[2], s[0], s[1], s[2]], jnp.zeros((8, 128), jnp.float32))
    return jnp.concatenate([y, s1, s1, s1, s2, s2, s3, e], axis=0)

def local_features(blk):
    row = lax.broadcasted_iota(jnp.int32, (8, 128), 0)
    zero = jnp.zeros((8, 128), jnp.float32)
    y = centered(blk)
    sq = jnp.sum(y[0:3] * y[0:3], axis=0, keepdims=True) + EPS_DIST
    sv = jnp.sum(y[0:3] * y[3:6], axis=0, keepdims=True)
    wd = jnp.where(row < 3, -2.0 * y, jnp.where(row == 6, sq, 0.0))
    wv = jnp.concatenate([-y[3:6], -y[0:3], sv, jnp.zeros((1, 128), jnp.float32)], axis=0)
    p1, p2, p3 = split3(wd)
    v1, v2, v3 = split3(wv)
    ed = jnp.where(row < 3, 1.0, 0.0)
    ev = jnp.where((row >= 3) & (row < 6), 1.0, 0.0)
    d = jnp.concatenate([zero, p1, p2, p3, p1, p2, p1, ed], axis=0)
    v = jnp.concatenate([zero, v1, v2, v3, v1, v2, v1, ev], axis=0)
    return jnp.concatenate([d, v], axis=1).astype(jnp.bfloat16)

def prep_partner(blk, j, a_ref, xb_ref):
    t = partner_features(blk).T
    a_ref[j] = t.astype(jnp.bfloat16)
    for k, ch in enumerate((0, 1, 2, 6)):
        xb_ref[j, k] = jnp.broadcast_to(t[:, ch:ch + 1], (128, 128))

def pair_sums(a, b, a_ref, xb_ref, b_ref, rad_row):
    z = jnp.dot(a_ref[b], b_ref[a], preferred_element_type=jnp.float32)
    inv = lax.rsqrt(jnp.maximum(z[:, :128], EPS_DIST))
    rs = xb_ref[b, 3] + rad_row
    w = jnp.maximum(rs * inv - 1.0, 0.0)
    f = w * (STIFFNESS - DAMPING * z[:, 128:] * inv)
    rows = []
    for k in range(3):
        rows.append(jnp.sum(f * xb_ref[b, k], axis=0, keepdims=True))
    rows.append(jnp.sum(f, axis=0, keepdims=True))
    return rows

def contact_kernel(ext_ref, ids_ref, left_ref, cnt_ref, out_ref, a_ref, xb_ref, b_ref, f_ref):
    def prep(j, _):
        prep_partner(ext_ref[j], j, a_ref, xb_ref)
        return 0
    lax.fori_loop(0, 40, prep, 0, unroll=4)
    def prepl(j, _):
        b_ref[j] = local_features(ext_ref[j + 4])
        return 0
    lax.fori_loop(0, 32, prepl, 0, unroll=4)
    zero = jnp.zeros((8, 128), jnp.float32)
    def body(i, _):
        a = ids_ref[0, i]
        b = ids_ref[1, i]
        blk = centered(ext_ref[a + 4])
        rows = pair_sums(a, b, a_ref, xb_ref, b_ref, blk[6:7])
        f_ref[i] = rowsel([blk[k:k + 1] * rows[3] - rows[k] for k in range(3)], zero)
        return 0
    lax.fori_loop(0, PAIRS, body, 0, unroll=UNROLL)
    lane = lax.broadcasted_iota(jnp.int32, (32, PAIRS), 1)
    blkid = lax.broadcasted_iota(jnp.int32, (32, PAIRS), 0)
    oh = jnp.where((left_ref[0:1] == blkid) & (lane < cnt_ref[0, 0]), 1.0, 0.0).astype(jnp.bfloat16)
    for k in range(3):
        s1, s2, s3 = split3(f_ref[:, k, :])
        acc = jnp.zeros((32, 128), jnp.float32)
        for s in (s3, s2, s1):
            acc = acc + jnp.dot(oh, s.astype(jnp.bfloat16), preferred_element_type=jnp.float32)
        out_ref[k] = acc

UNROLL = 8

def contact_forces(ext, pairs, count):
    ids = pairs
    return pl.pallas_call(
        contact_kernel,
        out_shape=jax.ShapeDtypeStruct((3, 32, 128), jnp.float32),
        in_specs=[pl.BlockSpec(memory_space=pltpu.VMEM), pl.BlockSpec(memory_space=pltpu.SMEM),
                  pl.BlockSpec(memory_space=pltpu.VMEM), pl.BlockSpec(memory_space=pltpu.SMEM)],
        out_specs=pl.BlockSpec(memory_space=pltpu.VMEM),
        scratch_shapes=[pltpu.VMEM((40, 128, 64), jnp.bfloat16), pltpu.VMEM((40, 4, 128, 128), jnp.float32),
                        pltpu.VMEM((32, 64, 256), jnp.bfloat16), pltpu.VMEM((PAIRS, 8, 128), jnp.float32)],
        compiler_params=pltpu.CompilerParams(vmem_limit_bytes=48 * 1024 * 1024),
    )(ext, ids, pairs, count)


def local(
    positions,
    velocities,
    radii,
    drag_rates,
    mig_slots,
    mig_counts,
    pair_lists,
    pair_counts,
    owners,
    dep_weights,
    fluid_velocity,
):
    particle_state = jnp.concatenate(
        [positions[0], velocities[0], radii[0][:, None], drag_rates[0][:, None]], axis=1
    )
    blocks = particle_state.shape[0]
    blk_width = particle_state.shape[2]
    capacity = mig_slots.shape[2]
    slot_idx = jnp.arange(capacity, dtype=jnp.int32)
    for bit_level in range(mig_slots.shape[1]):
        slot_list = mig_slots[0, bit_level]
        outgoing = particle_state[slot_list]
        incoming = from_partner(outgoing, "bis", bit_level)
        is_live = slot_idx < mig_counts[0, bit_level]
        chosen = jnp.where(is_live[:, None, None], incoming, outgoing)
        particle_state = particle_state.at[slot_list].set(chosen)
    fb_dev = fluid_velocity.shape[1]
    cells = fluid_velocity.shape[3]
    fluid_bf = fluid_velocity[0].astype(jnp.bfloat16).reshape(fb_dev, 3 * cells)
    owner_map = owners[0]
    weights = dep_weights[0]
    shard_piece = lax.all_gather(fluid_bf, "bis", axis=0, tiled=True)
    onehot = (
        owner_map[:, None] == jnp.arange(shard_piece.shape[0], dtype=jnp.int32)[None, :]
    ).astype(jnp.bfloat16)
    carried = jnp.dot(onehot, shard_piece, preferred_element_type=jnp.float32)
    fluid_blk = carried.astype(jnp.bfloat16).reshape(blocks, 3, cells)
    sampled = jnp.einsum("npc,nkc->nkp", weights, fluid_blk, preferred_element_type=jnp.float32)
    for substep in range(SUBSTEPS):
        padded = with_halo(particle_state, (("dom", 0),), G)
        contact = jnp.transpose(contact_forces(padded, pair_lists[0], pair_counts), (1, 0, 2))
        masses = (particle_state[:, 6] / RADIUS_REF) ** 3
        beta = particle_state[:, 7]
        velocity = particle_state[:, 3:6]
        velocity = velocity + TIME_STEP * (
            contact / masses[:, None] + beta[:, None] * (sampled - velocity)
        )
        position = particle_state[:, 0:3] + TIME_STEP * velocity
        particle_state = jnp.concatenate([position, velocity, particle_state[:, 6:8]], axis=1)
    masses = (particle_state[:, 6] / RADIUS_REF) ** 3
    beta = particle_state[:, 7]
    velocity = particle_state[:, 3:6]
    payload = jnp.concatenate(
        [(masses * beta)[:, None] * (sampled - velocity), masses[:, None]], axis=1
    ).astype(jnp.bfloat16)
    deposits = jnp.einsum(
        "nkp,npc->nkc", payload, weights, preferred_element_type=jnp.float32
    ).reshape(blocks, 4 * cells)
    fluid_rows = jnp.arange(fb_dev * lax.axis_size("bis"), dtype=jnp.int32)
    onehot = (fluid_rows[:, None] == owner_map[None, :]).astype(jnp.float32)
    totals = lax.psum_scatter(
        jnp.dot(onehot, deposits, precision=lax.Precision.HIGHEST),
        "bis",
        scatter_dimension=0,
        tiled=True,
    )
    totals = totals.reshape(fb_dev, 4, cells)
    solid = totals[:, 3]
    voidage = 1.0 / (1.0 + solid)
    fluid_out = fluid_velocity[0] - FLUID_GAIN * totals[:, 0:3] / (1.0 + solid)[:, None]
    return (
        particle_state[None, :, 0:3],
        particle_state[None, :, 3:6],
        fluid_out[None],
        voidage[None],
    )


def solution(mesh):
    in_specs = (
        P("bis", "dom", None, None),
        P("bis", "dom", None, None),
        P("bis", "dom", None),
        P("bis", "dom", None),
        P("bis", "dom", None),
        P("bis", "dom"),
        P("bis", None, "dom"),
        P("bis", "dom"),
        P("bis", "dom"),
        P("bis", "dom", None, None),
        P("dom", "bis", None, None),
    )
    out_specs = (
        P("bis", "dom", None, None),
        P("bis", "dom", None, None),
        P("dom", "bis", None, None),
        P("dom", "bis", None),
    )
    return jax.shard_map(local, mesh=mesh, in_specs=in_specs, out_specs=out_specs, check_vma=False)
```

```python
import functools

import jax
import jax.numpy as jnp
from jax import lax
from jax.experimental import pallas as pl
from jax.experimental.pallas import tpu as pltpu
from jax.sharding import PartitionSpec as P

G = 4
SUBSTEPS = 2
BLK = 128

STIFFNESS = 5.0
DAMPING = 1.0
TIME_STEP = 0.05
EPS_DIST = 0.0001
RADIUS_REF = 0.1
FLUID_GAIN = 0.2

F32 = jnp.float32
BF16 = jnp.bfloat16
MESH = pl.DeviceIdType.MESH


def row_ids():
    return lax.broadcasted_iota(jnp.int32, (8, BLK), 0)


def stack_rows(rows):
    row = row_ids()
    out = jnp.zeros((8, BLK), F32)
    for k, value in enumerate(rows):
        out = jnp.where(row == k, value, out)
    return out


def split(x, parts=3):
    out = []
    for _ in range(parts):
        piece = x.astype(BF16).astype(F32)
        out.append(piece)
        x = x - piece
    return out


def centered(blk):
    return jnp.where(row_ids() < 3, blk - 0.5, blk)


def partner_features(blk):
    row = row_ids()
    y = centered(blk)
    sq = jnp.sum(y[0:3] * y[0:3], axis=0, keepdims=True)
    sv = jnp.sum(y[0:3] * y[3:6], axis=0, keepdims=True)
    base = jnp.where(row < 6, y, jnp.where(row == 6, 1.0, y[6:7]))
    s1, s2, s3 = split(base)
    e = stack_rows(split(sq) + split(sv))
    zero = jnp.zeros((8, BLK), F32)
    return jnp.concatenate([zero, s1, s1, s1, s2, s2, s3, e], axis=0)


def local_features(blk):
    row = row_ids()
    zero = jnp.zeros((8, BLK), F32)
    y = centered(blk)
    sq = jnp.sum(y[0:3] * y[0:3], axis=0, keepdims=True) + EPS_DIST
    sv = jnp.sum(y[0:3] * y[3:6], axis=0, keepdims=True)
    wd = jnp.where(row < 3, -2.0 * y, jnp.where(row == 6, sq, 0.0))
    wv = jnp.concatenate([-y[3:6], -y[0:3], sv, jnp.zeros((1, BLK), F32)], axis=0)
    p1, p2, p3 = split(wd)
    v1, v2, v3 = split(wv)
    ed = jnp.where(row < 3, 1.0, 0.0)
    ev = jnp.where((row >= 3) & (row < 6), 1.0, 0.0)
    d = jnp.concatenate([zero, p1, p2, p3, p1, p2, p1, ed], axis=0)
    v = jnp.concatenate([zero, v1, v2, v3, v1, v2, v1, ev], axis=0)
    return jnp.concatenate([d, v], axis=1).astype(BF16)


def kernel(
    bis, dom, pmax,
    pos_ref, vel_ref, rad_ref, drag_ref, slots_ref, inv_ref, pairs_ref, left_ref, cnt_ref, own_ref, w_hbm, fluid_ref,
    pos_out, vel_out, fluid_out, void_out,
    st0, st1, mig_s, mig_r, halo_r, own_s, own_r, fl_s, fl_r, w_v, flrow, samp,
    a_ref, xb_ref, b_ref, f_ref, sel_ref, oh_ref, dep, dep_s, dep_r,
    w_sem, mig_ss, mig_rs, halo_ss, halo_rs, own_ss, own_rs, fl_ss, fl_rs, dep_ss, dep_rs,
):
    nb = st0.shape[0]
    per = BLK // nb
    tiles = bis // per
    me = lax.axis_index("bis")
    mine = lax.axis_index("dom")
    right, left = lax.rem(mine + 1, dom), lax.rem(mine + dom - 1, dom)

    weights_copy = pltpu.make_async_copy(w_hbm, w_v, w_sem)
    weights_copy.start()

    barrier = pltpu.get_barrier_semaphore()

    def greet(r, _):
        pl.semaphore_signal(barrier, inc=1, device_id={"bis": lax.rem(me + r, bis)}, device_id_type=MESH)
        return 0

    lax.fori_loop(1, bis, greet, 0)
    for side in (left, right):
        pl.semaphore_signal(barrier, inc=1, device_id={"dom": side}, device_id_type=MESH)

    def to_peer(r, source, target, ss, rs):
        peer = lax.rem(me + r, bis)
        return pltpu.make_async_remote_copy(
            src_ref=source(peer), dst_ref=target.at[me], send_sem=ss.at[r], recv_sem=rs.at[r],
            device_id={"bis": peer}, device_id_type=MESH,
        )

    def start_all(source, target, ss, rs):
        def step(r, _):
            to_peer(r, source, target, ss, rs).start()
            return 0

        lax.fori_loop(1, bis, step, 0)

    def wait_all(source, target, ss, rs):
        def step(r, _):
            to_peer(r, source, target, ss, rs).wait()
            return 0

        lax.fori_loop(1, bis, step, 0)

    for k in range(3):
        st0[:, k, :] = pos_ref[k]
        st0[:, 3 + k, :] = vel_ref[k]
    st0[:, 6, :] = rad_ref[...]
    st0[:, 7, :] = drag_ref[...]
    lane8 = lax.broadcasted_iota(jnp.int32, (8, BLK), 1)
    quarter = lax.rem(me, per)
    own_s[...] = jnp.where(lane8 // nb == quarter, own_ref[...], 0)
    own_r[me] = own_s[...]

    capacity = mig_s.shape[1]

    def gather(level):
        def step(j, _):
            mig_s[level, j] = st0[slots_ref[level, j]]
            return 0

        lax.fori_loop(0, capacity, step, 0, unroll=4)

    def migrate_copy(level):
        stride = 2**level
        bit = lax.rem(me // stride, 2)
        partner = me + stride - 2 * stride * bit
        return pltpu.make_async_remote_copy(
            src_ref=mig_s.at[level], dst_ref=mig_r[level], send_sem=mig_ss.at[level], recv_sem=mig_rs.at[level],
            device_id={"bis": partner}, device_id_type=MESH,
        )

    def scatter(level):
        def step(n, _):
            j = inv_ref[level, n]
            st0[n] = jnp.where(j >= 0, mig_r[level][jnp.maximum(j, 0)], st0[n])
            return 0

        lax.fori_loop(0, nb, step, 0, unroll=4)

    gather(0)
    pl.semaphore_wait(barrier, bis - 1 + 2)
    migrate_copy(0).start()
    own_source = lambda peer: own_s
    start_all(own_source, own_r, own_ss, own_rs)
    srow = lax.broadcasted_iota(jnp.int32, (64, BLK), 0)
    part = (srow >= 8) & (srow < 56)
    first = (srow // 8 == 1) | (srow // 8 == 4) | (srow // 8 == 6)
    for c, ch in enumerate((0, 1, 2, 7)):
        sel_ref[:, c * BLK:(c + 1) * BLK] = jnp.where(first & part & (lax.rem(srow, 8) == ch), 1.0, 0.0).astype(BF16)
    migrate_copy(0).wait()
    scatter(0)
    gather(1)
    migrate_copy(1).start()

    wait_all(own_source, own_r, own_ss, own_rs)
    fluid_bf = jnp.concatenate([fluid_ref[k].astype(BF16) for k in range(3)], axis=1)
    rows = []
    for t in range(tiles):
        row = own_r[per * t, 0:1, :]
        for i in range(1, per):
            row = row + own_r[per * t + i, 0:1, :]
        rows.append(row - BLK * me)
    sub = lax.broadcasted_iota(jnp.int32, (BLK, BLK), 0)
    for t in range(tiles):
        hot = jnp.where(sub == rows[t], 1.0, 0.0)
        oh_ref[t] = hot.astype(BF16)
        chosen = jnp.dot(hot.T.astype(BF16), fluid_bf, preferred_element_type=F32).astype(BF16)
        for i in range(per):
            fl_s[per * t + i] = chosen[nb * i:nb * (i + 1)]
    fl_r[me] = fl_s[me]

    migrate_copy(1).wait()
    scatter(1)
    gather(2)
    migrate_copy(2).start()
    migrate_copy(2).wait()
    scatter(2)

    def halo_copies(step, state):
        return [
            pltpu.make_async_remote_copy(
                src_ref=state.at[pl.ds(nb - G, G)], dst_ref=halo_r.at[step, pl.ds(0, G)],
                send_sem=halo_ss.at[step, 0], recv_sem=halo_rs.at[step, 0],
                device_id={"dom": right}, device_id_type=MESH,
            ),
            pltpu.make_async_remote_copy(
                src_ref=state.at[pl.ds(0, G)], dst_ref=halo_r.at[step, pl.ds(G, G)],
                send_sem=halo_ss.at[step, 1], recv_sem=halo_rs.at[step, 1],
                device_id={"dom": left}, device_id_type=MESH,
            ),
        ]

    fl_source = lambda peer: fl_s.at[peer]

    def prepare(blk, j):
        t = partner_features(blk).T.astype(BF16)
        a_ref[j] = t
        wide = jnp.dot(t, sel_ref[...], preferred_element_type=F32)
        for c in range(4):
            xb_ref[j, c] = wide[:, c * BLK:(c + 1) * BLK]

    def contacts(step, state):
        for copy in halo_copies(step, state):
            copy.start()
        if step == 0:
            start_all(fl_source, fl_r, fl_ss, fl_rs)

        def own_blocks(n, _):
            blk = state[n]
            prepare(blk, n + G)
            b_ref[n] = local_features(blk)
            return 0

        lax.fori_loop(0, nb, own_blocks, 0, unroll=4)
        for copy in halo_copies(step, state):
            copy.wait()

        def rim(n, _):
            prepare(halo_r[step, n], n)
            prepare(halo_r[step, n + G], n + nb + G)
            return 0

        lax.fori_loop(0, G, rim, 0, unroll=2)

        def pair(i, _):
            a = jnp.minimum(pairs_ref[0, i], nb - 1)
            b = pairs_ref[1, i]
            blk = centered(state[a])
            z = jnp.dot(a_ref[b], b_ref[a], preferred_element_type=F32)
            inv = lax.rsqrt(jnp.maximum(z[:, :BLK], EPS_DIST))
            depth = jnp.maximum((xb_ref[b, 3] + blk[6:7]) * inv - 1.0, 0.0)
            f = depth * (STIFFNESS - DAMPING * z[:, BLK:] * inv)
            total = jnp.sum(f, axis=0, keepdims=True)
            f_ref[i] = stack_rows([
                blk[k:k + 1] * total - jnp.sum(f * xb_ref[b, k], axis=0, keepdims=True) for k in range(3)
            ])
            return 0

        lax.fori_loop(0, pmax, pair, 0, unroll=min(16, pmax))
        lane = lax.broadcasted_iota(jnp.int32, (nb, pmax), 1)
        blk_id = lax.broadcasted_iota(jnp.int32, (nb, pmax), 0)
        hot = jnp.where((left_ref[...] == blk_id) & (lane < cnt_ref[0, 0]), 1.0, 0.0).astype(BF16)
        out = []
        for k in range(3):
            acc = jnp.zeros((nb, BLK), F32)
            for piece in split(f_ref[:, k, :])[::-1]:
                acc = acc + jnp.dot(hot, piece.astype(BF16), preferred_element_type=F32)
            out.append(acc)
        return out

    def sample():
        wait_all(fl_source, fl_r, fl_ss, fl_rs)
        total = fl_r[0].astype(F32)
        for g in range(1, bis):
            total = total + fl_r[g].astype(F32)
        flrow[...] = jnp.zeros(flrow.shape, F32)
        for k in range(3):
            flrow[:, k, :] = total[:, k * BLK:(k + 1) * BLK]
        weights_copy.wait()

        def step(n, _):
            samp[n] = lax.dot_general(
                flrow[n].astype(BF16), w_v[n], (((1,), (1,)), ((), ())), preferred_element_type=F32
            )
            return 0

        lax.fori_loop(0, nb, step, 0, unroll=8)

    radius, beta = None, None
    for substep in range(SUBSTEPS):
        state = (st0, st1)[substep]
        contact = contacts(substep, state)
        if substep == 0:
            sample()
            sampled = [samp[:, k, :] for k in range(3)]
            radius, beta = st0[:, 6, :], st0[:, 7, :]
            masses = (radius / RADIUS_REF) ** 3
        speed, place = [], []
        for k in range(3):
            v = state[:, 3 + k, :]
            v = v + TIME_STEP * (contact[k] / masses + beta * (sampled[k] - v))
            speed.append(v)
            place.append(state[:, k, :] + TIME_STEP * v)
        if substep + 1 < SUBSTEPS:
            for k in range(3):
                st1[:, k, :] = place[k]
                st1[:, 3 + k, :] = speed[k]
            st1[:, 6, :] = radius
            st1[:, 7, :] = beta
    for k in range(3):
        pos_out[k] = place[k]
        vel_out[k] = speed[k]

    flrow[...] = jnp.zeros(flrow.shape, F32)
    for k in range(3):
        flrow[:, k, :] = (masses * beta) * (sampled[k] - speed[k])
    flrow[:, 3, :] = masses

    def deposit(n, _):
        dep[n] = jnp.dot(flrow[n].astype(BF16), w_v[n], preferred_element_type=F32)
        return 0

    lax.fori_loop(0, nb, deposit, 0, unroll=8)
    for k in range(4):
        dep_s[k] = dep[:, k, :]
    dep_source = lambda peer: dep_s
    start_all(dep_source, dep_r, dep_ss, dep_rs)
    dep_r[me] = dep_s[...]
    wait_all(dep_source, dep_r, dep_ss, dep_rs)
    totals = []
    for k in (3, 0, 1, 2):
        acc = jnp.zeros((BLK, BLK), F32)
        for t in range(tiles):
            values = dep_r[per * t:per * (t + 1), k].reshape(BLK, BLK)
            for piece in split(values)[::-1]:
                acc = acc + jnp.dot(oh_ref[t], piece.astype(BF16), preferred_element_type=F32)
        totals.append(acc)
    void = 1.0 / (1.0 + totals[0])
    void_out[...] = void
    for k in range(3):
        fluid_out[k] = fluid_ref[k] - FLUID_GAIN * totals[1 + k] * void


def local(
    bis, dom, positions, velocities, radii, drag_rates, mig_slots, mig_counts, pair_lists, pair_counts, owners, dep_weights, fluid_velocity,
):
    nb = positions.shape[1]
    levels, capacity = mig_slots.shape[1:]
    pmax = pair_lists.shape[2]
    fb = fluid_velocity.shape[1]
    j = jnp.arange(capacity, dtype=jnp.int32)
    hit = mig_slots[0][:, None, :] == jnp.arange(nb, dtype=jnp.int32)[None, :, None]
    hit = hit & (j[None, None, :] < mig_counts[0][:, None, None])
    inverse = jnp.max(jnp.where(hit, j[None, None, :], -1), axis=2)
    vmem = pl.BlockSpec(memory_space=pltpu.VMEM)
    smem = pl.BlockSpec(memory_space=pltpu.SMEM)
    dma = pltpu.SemaphoreType.DMA
    tiles = bis * nb // BLK
    outs = pl.pallas_call(
        functools.partial(kernel, bis, dom, pmax),
        out_shape=(
            jax.ShapeDtypeStruct((3, nb, BLK), F32),
            jax.ShapeDtypeStruct((3, nb, BLK), F32),
            jax.ShapeDtypeStruct((3, fb, BLK), F32),
            jax.ShapeDtypeStruct((fb, BLK), F32),
        ),
        in_specs=[vmem] * 4 + [smem] * 3 + [vmem, smem, vmem, pl.BlockSpec(memory_space=pl.ANY), vmem],
        out_specs=(vmem,) * 4,
        scratch_shapes=[
            pltpu.VMEM((nb, 8, BLK), F32),
            pltpu.VMEM((nb, 8, BLK), F32),
            pltpu.VMEM((levels, capacity, 8, BLK), F32),
            [pltpu.VMEM((capacity, 8, BLK), F32)] * levels,
            pltpu.VMEM((SUBSTEPS, 2 * G, 8, BLK), F32),
            pltpu.VMEM((8, BLK), jnp.int32),
            pltpu.VMEM((bis, 8, BLK), jnp.int32),
            pltpu.VMEM((bis, nb, 3 * BLK), BF16),
            pltpu.VMEM((bis, nb, 3 * BLK), BF16),
            pltpu.VMEM((nb, BLK, BLK), BF16),
            pltpu.VMEM((nb, 8, BLK), F32),
            pltpu.VMEM((nb, 8, BLK), F32),
            pltpu.VMEM((nb + 2 * G, BLK, 64), BF16),
            pltpu.VMEM((nb + 2 * G, 4, BLK, BLK), F32),
            pltpu.VMEM((nb, 64, 2 * BLK), BF16),
            pltpu.VMEM((pmax, 8, BLK), F32),
            pltpu.VMEM((64, 4 * BLK), BF16),
            pltpu.VMEM((tiles, BLK, BLK), BF16),
            pltpu.VMEM((nb, 8, BLK), F32),
            pltpu.VMEM((4, nb, BLK), F32),
            pltpu.VMEM((bis, 4, nb, BLK), F32),
            dma,
            dma((levels,)),
            dma((levels,)),
            dma((SUBSTEPS, 2)),
            dma((SUBSTEPS, 2)),
            dma((bis,)),
            dma((bis,)),
            dma((bis,)),
            dma((bis,)),
            dma((bis,)),
            dma((bis,)),
        ],
        compiler_params=pltpu.CompilerParams(
            collective_id=0, has_side_effects=True, vmem_limit_bytes=48 * 1024 * 1024
        ),
    )(
        jnp.transpose(positions[0], (1, 0, 2)),
        jnp.transpose(velocities[0], (1, 0, 2)),
        radii[0],
        drag_rates[0],
        mig_slots[0],
        inverse,
        pair_lists[0],
        pair_lists[0, 0:1],
        pair_counts,
        jnp.tile(owners, (1, BLK // nb)),
        dep_weights[0],
        jnp.transpose(fluid_velocity[0], (1, 0, 2)),
    )
    pos, vel, fluid, void = outs
    return (
        jnp.transpose(pos, (1, 0, 2))[None],
        jnp.transpose(vel, (1, 0, 2))[None],
        jnp.transpose(fluid, (1, 0, 2))[None],
        void[None],
    )


def solution(mesh):
    in_specs = (
        P("bis", "dom", None, None),
        P("bis", "dom", None, None),
        P("bis", "dom", None),
        P("bis", "dom", None),
        P("bis", "dom", None),
        P("bis", "dom"),
        P("bis", None, "dom"),
        P("bis", "dom"),
        P("bis", "dom"),
        P("bis", "dom", None, None),
        P("dom", "bis", None, None),
    )
    out_specs = (
        P("bis", "dom", None, None),
        P("bis", "dom", None, None),
        P("dom", "bis", None, None),
        P("dom", "bis", None),
    )
    body = functools.partial(local, mesh.shape["bis"], mesh.shape["dom"])
    return jax.shard_map(body, mesh=mesh, in_specs=in_specs, out_specs=out_specs, check_vma=False)
```

```python
import functools

import jax
import jax.numpy as jnp
from jax import lax
from jax.experimental import pallas as pl
from jax.experimental.pallas import tpu as pltpu
from jax.sharding import PartitionSpec as P

G = 4
SUBSTEPS = 2
BLK = 128

STIFFNESS = 5.0
DAMPING = 1.0
TIME_STEP = 0.05
EPS_DIST = 0.0001
RADIUS_REF = 0.1
FLUID_GAIN = 0.2

F32 = jnp.float32
BF16 = jnp.bfloat16
MESH = pl.DeviceIdType.MESH


def row_ids():
    return lax.broadcasted_iota(jnp.int32, (8, BLK), 0)


def stack_rows(rows):
    row = row_ids()
    out = jnp.zeros((8, BLK), F32)
    for k, value in enumerate(rows):
        out = jnp.where(row == k, value, out)
    return out


def split(x, parts=3):
    out = []
    for _ in range(parts):
        piece = x.astype(BF16).astype(F32)
        out.append(piece)
        x = x - piece
    return out


def centered(blk):
    return jnp.where(row_ids() < 3, blk - 0.5, blk)


def partner_features(blk):
    row = row_ids()
    y = centered(blk)
    sq = jnp.sum(y[0:3] * y[0:3], axis=0, keepdims=True)
    sv = jnp.sum(y[0:3] * y[3:6], axis=0, keepdims=True)
    base = jnp.where(row < 6, y, jnp.where(row == 6, 1.0, y[6:7]))
    s1, s2, s3 = split(base)
    e = stack_rows(split(sq) + split(sv))
    zero = jnp.zeros((8, BLK), F32)
    return jnp.concatenate([zero, s1, s1, s1, s2, s2, s3, e], axis=0)


def local_features(blk):
    row = row_ids()
    zero = jnp.zeros((8, BLK), F32)
    y = centered(blk)
    sq = jnp.sum(y[0:3] * y[0:3], axis=0, keepdims=True) + EPS_DIST
    sv = jnp.sum(y[0:3] * y[3:6], axis=0, keepdims=True)
    wd = jnp.where(row < 3, -2.0 * y, jnp.where(row == 6, sq, 0.0))
    wv = jnp.concatenate([-y[3:6], -y[0:3], sv, jnp.zeros((1, BLK), F32)], axis=0)
    p1, p2, p3 = split(wd)
    v1, v2, v3 = split(wv)
    ed = jnp.where(row < 3, 1.0, 0.0)
    ev = jnp.where((row >= 3) & (row < 6), 1.0, 0.0)
    d = jnp.concatenate([zero, p1, p2, p3, p1, p2, p1, ed], axis=0)
    v = jnp.concatenate([zero, v1, v2, v3, v1, v2, v1, ev], axis=0)
    return jnp.concatenate([d, v], axis=1).astype(BF16)


def kernel(
    bis, dom, pmax,
    pos_hbm, vel_hbm, rad_hbm, drag_hbm, slots_ref, inv_ref, pairs_ref, left_ref, cnt_ref, own_ref, w_hbm, fluid_hbm,
    pos_out, vel_out, fluid_out, void_out,
    pos_ref, vel_ref, rad_ref, drag_ref, fluid_ref,
    st0, st1, mig_s, mig_r, halo_r, own_s, own_r, fl_s, fl_r, w_v, flrow, samp,
    a_ref, xb_ref, b_ref, f_ref, sel_ref, oh_ref, dep, mass_s, mass_r, da, db,
    in_sem, w_sem, mig_ss, mig_rs, halo_ss, halo_rs, own_ss, own_rs, fl_ss, fl_rs, mass_ss, mass_rs, dep_ss, dep_rs,
):
    nb = st0.shape[0]
    per = BLK // nb
    tiles = bis // per
    me = lax.axis_index("bis")
    mine = lax.axis_index("dom")
    right, left = lax.rem(mine + 1, dom), lax.rem(mine + dom - 1, dom)

    barrier = pltpu.get_barrier_semaphore()

    def greet(r, _):
        pl.semaphore_signal(barrier, inc=1, device_id={"bis": lax.rem(me + r, bis)}, device_id_type=MESH)
        return 0

    lax.fori_loop(1, bis, greet, 0)
    for side in (left, right):
        pl.semaphore_signal(barrier, inc=1, device_id={"dom": side}, device_id_type=MESH)

    inputs = [
        pltpu.make_async_copy(src, dst, in_sem.at[k])
        for k, (src, dst) in enumerate((
            (pos_hbm, pos_ref), (vel_hbm, vel_ref), (rad_hbm, rad_ref), (drag_hbm, drag_ref), (fluid_hbm, fluid_ref)
        ))
    ]
    for copy in inputs:
        copy.start()
    weights_copy = pltpu.make_async_copy(w_hbm, w_v, w_sem)
    weights_copy.start()

    def to_peer(r, source, target, ss, rs):
        peer = lax.rem(me + r, bis)
        return pltpu.make_async_remote_copy(
            src_ref=source(peer), dst_ref=target.at[me], send_sem=ss.at[r], recv_sem=rs.at[r],
            device_id={"bis": peer}, device_id_type=MESH,
        )

    def start_all(source, target, ss, rs):
        def step(r, _):
            to_peer(r, source, target, ss, rs).start()
            return 0

        lax.fori_loop(1, bis, step, 0)

    def wait_all(source, target, ss, rs):
        def step(r, _):
            to_peer(r, source, target, ss, rs).wait()
            return 0

        lax.fori_loop(1, bis, step, 0)

    own_s[...] = jnp.zeros((8, BLK), jnp.int32)
    own_s[:, 0:nb] = jnp.broadcast_to(own_ref[...], (8, nb))
    lane8 = lax.broadcasted_iota(jnp.int32, (8, BLK), 1)
    quarter = lax.rem(me, per)
    half = nb // 2
    owners = own_s[...]
    low = pltpu.roll(jnp.where(lane8 < half, owners, 0), half * quarter, 1)
    high = pltpu.roll(jnp.where((lane8 >= half) & (lane8 < nb), owners, 0), BLK // 2 - half + half * quarter, 1)
    own_s[...] = low + high
    for copy in inputs[:4]:
        copy.wait()
    for k in range(3):
        st0[:, k, :] = pos_ref[k]
        st0[:, 3 + k, :] = vel_ref[k]
    st0[:, 6, :] = rad_ref[...]
    st0[:, 7, :] = drag_ref[...]
    own_r[me] = own_s[...]

    capacity = mig_s.shape[1]

    def gather(level):
        def step(j, _):
            mig_s[level, j] = st0[slots_ref[level, j]]
            return 0

        lax.fori_loop(0, capacity, step, 0, unroll=4)

    def migrate_copy(level):
        stride = 2**level
        bit = lax.rem(me // stride, 2)
        partner = me + stride - 2 * stride * bit
        return pltpu.make_async_remote_copy(
            src_ref=mig_s.at[level], dst_ref=mig_r[level], send_sem=mig_ss.at[level], recv_sem=mig_rs.at[level],
            device_id={"bis": partner}, device_id_type=MESH,
        )

    def scatter(level):
        def step(n, _):
            j = inv_ref[level, n]
            st0[n] = jnp.where(j >= 0, mig_r[level][jnp.maximum(j, 0)], st0[n])
            return 0

        lax.fori_loop(0, nb, step, 0, unroll=4)

    gather(0)
    pl.semaphore_wait(barrier, bis - 1 + 2)
    migrate_copy(0).start()
    own_source = lambda peer: own_s
    start_all(own_source, own_r, own_ss, own_rs)
    srow = lax.broadcasted_iota(jnp.int32, (64, BLK), 0)
    part = (srow >= 8) & (srow < 56)
    first = (srow // 8 == 1) | (srow // 8 == 4) | (srow // 8 == 6)
    for c, ch in enumerate((0, 1, 2, 7)):
        sel_ref[:, c * BLK:(c + 1) * BLK] = jnp.where(first & part & (lax.rem(srow, 8) == ch), 1.0, 0.0).astype(BF16)
    migrate_copy(0).wait()
    scatter(0)
    gather(1)
    migrate_copy(1).start()

    wait_all(own_source, own_r, own_ss, own_rs)
    inputs[4].wait()
    fluid_bf = jnp.concatenate([fluid_ref[k].astype(BF16) for k in range(3)], axis=1)
    rows = []
    for t in range(tiles):
        row = own_r[per * t, 0:1, :]
        for i in range(1, per):
            row = row + own_r[per * t + i, 0:1, :]
        rows.append(row - BLK * me)
    sub = lax.broadcasted_iota(jnp.int32, (BLK, BLK), 0)
    for t in range(tiles):
        hot = jnp.where(sub == rows[t], 1.0, 0.0)
        oh_ref[t] = hot.astype(BF16)
        chosen = jnp.dot(hot.T.astype(BF16), fluid_bf, preferred_element_type=F32).astype(BF16)
        for i in range(per):
            for h in range(2):
                first_row = BLK // 2 * h + half * i
                fl_s[per * t + i, half * h:half * (h + 1)] = chosen[first_row:first_row + half]
    fl_r[me] = fl_s[me]

    migrate_copy(1).wait()
    scatter(1)
    gather(2)
    migrate_copy(2).start()
    migrate_copy(2).wait()
    scatter(2)

    def halo_copies(step, state):
        return [
            pltpu.make_async_remote_copy(
                src_ref=state.at[pl.ds(nb - G, G)], dst_ref=halo_r.at[step, pl.ds(0, G)],
                send_sem=halo_ss.at[step, 0], recv_sem=halo_rs.at[step, 0],
                device_id={"dom": right}, device_id_type=MESH,
            ),
            pltpu.make_async_remote_copy(
                src_ref=state.at[pl.ds(0, G)], dst_ref=halo_r.at[step, pl.ds(G, G)],
                send_sem=halo_ss.at[step, 1], recv_sem=halo_rs.at[step, 1],
                device_id={"dom": left}, device_id_type=MESH,
            ),
        ]

    fl_source = lambda peer: fl_s.at[peer]

    def prepare(blk, j):
        t = partner_features(blk).T.astype(BF16)
        a_ref[j] = t
        wide = jnp.dot(t, sel_ref[...], preferred_element_type=F32)
        for c in range(4):
            xb_ref[j, c] = wide[:, c * BLK:(c + 1) * BLK]

    mass_source = lambda peer: mass_s

    def deposit(n, _):
        dep[n] = jnp.dot(flrow[n].astype(BF16), w_v[n], preferred_element_type=F32)
        return 0

    def deposit_mass():
        flrow[...] = jnp.zeros(flrow.shape, F32)
        flrow[:, 0, :] = (st0[:, 6, :] / RADIUS_REF) ** 3
        weights_copy.wait()
        lax.fori_loop(0, nb, deposit, 0, unroll=8)
        mass_s[...] = dep[:, 0, :]
        mass_r[me] = mass_s[...]
        start_all(mass_source, mass_r, mass_ss, mass_rs)

    def solid_volume():
        wait_all(mass_source, mass_r, mass_ss, mass_rs)
        solid = jnp.zeros((BLK, BLK), F32)
        for t in range(tiles):
            values = jnp.concatenate([
                mass_r[per * t:per * (t + 1), half * h:half * (h + 1)].reshape(BLK // 2, BLK) for h in range(2)
            ], axis=0)
            for piece in split(values)[::-1]:
                solid = solid + jnp.dot(oh_ref[t], piece.astype(BF16), preferred_element_type=F32)
        void_out[...] = 1.0 / (1.0 + solid)

    def contacts(step, state):
        for copy in halo_copies(step, state):
            copy.start()
        if step == 0:
            start_all(fl_source, fl_r, fl_ss, fl_rs)

        def own_blocks(n, _):
            blk = state[n]
            prepare(blk, n + G)
            b_ref[n] = local_features(blk)
            return 0

        lax.fori_loop(0, nb, own_blocks, 0, unroll=4)
        if step == 0:
            deposit_mass()
        if step == 1:
            solid_volume()
        for copy in halo_copies(step, state):
            copy.wait()

        def rim(n, _):
            prepare(halo_r[step, n], n)
            prepare(halo_r[step, n + G], n + nb + G)
            return 0

        lax.fori_loop(0, G, rim, 0, unroll=2)

        def pair(i, _):
            a = jnp.minimum(pairs_ref[0, i], nb - 1)
            b = pairs_ref[1, i]
            blk = centered(state[a])
            z = jnp.dot(a_ref[b], b_ref[a], preferred_element_type=F32)
            inv = lax.rsqrt(jnp.maximum(z[:, :BLK], EPS_DIST))
            depth = jnp.maximum((xb_ref[b, 3] + blk[6:7]) * inv - 1.0, 0.0)
            f = depth * (STIFFNESS - DAMPING * z[:, BLK:] * inv)
            total = jnp.sum(f, axis=0, keepdims=True)
            f_ref[i] = stack_rows([
                blk[k:k + 1] * total - jnp.sum(f * xb_ref[b, k], axis=0, keepdims=True) for k in range(3)
            ])
            return 0

        lax.fori_loop(0, pmax, pair, 0, unroll=min(16, pmax))
        lane = lax.broadcasted_iota(jnp.int32, (nb, pmax), 1)
        blk_id = lax.broadcasted_iota(jnp.int32, (nb, pmax), 0)
        hot = jnp.where((left_ref[0:1] == blk_id) & (lane < cnt_ref[0, 0]), 1.0, 0.0).astype(BF16)
        out = []
        for k in range(3):
            acc = jnp.zeros((nb, BLK), F32)
            for piece in split(f_ref[:, k, :])[::-1]:
                acc = acc + jnp.dot(hot, piece.astype(BF16), preferred_element_type=F32)
            out.append(acc)
        return out

    def sample():
        wait_all(fl_source, fl_r, fl_ss, fl_rs)
        total = fl_r[0].astype(F32)
        for g in range(1, bis):
            total = total + fl_r[g].astype(F32)
        for k in range(3):
            flrow[:, k, :] = total[:, k * BLK:(k + 1) * BLK]

        def step(n, _):
            samp[n] = lax.dot_general(
                flrow[n].astype(BF16), w_v[n], (((1,), (1,)), ((), ())), preferred_element_type=F32
            )
            return 0

        lax.fori_loop(0, nb, step, 0, unroll=8)

    radius, beta = None, None
    for substep in range(SUBSTEPS):
        state = (st0, st1)[substep]
        contact = contacts(substep, state)
        if substep == 0:
            sample()
            sampled = [samp[:, k, :] for k in range(3)]
            radius, beta = st0[:, 6, :], st0[:, 7, :]
            masses = (radius / RADIUS_REF) ** 3
        speed, place = [], []
        for k in range(3):
            v = state[:, 3 + k, :]
            v = v + TIME_STEP * (contact[k] / masses + beta * (sampled[k] - v))
            speed.append(v)
            place.append(state[:, k, :] + TIME_STEP * v)
        if substep + 1 < SUBSTEPS:
            for k in range(3):
                st1[:, k, :] = place[k]
                st1[:, 3 + k, :] = speed[k]
            st1[:, 6, :] = radius
            st1[:, 7, :] = beta
    for k in range(3):
        pos_out[k] = place[k]
        vel_out[k] = speed[k]

    ring = 4
    cols = bis // ring
    my_y, my_z = me // ring, lax.rem(me, ring)
    steps_z = (1, 3, 2)
    steps_y = (1, 3, 2)[:cols - 1] if cols > 2 else (1,)
    along_z = lambda i: my_y * ring + lax.rem(my_z + i, ring)
    along_y = lambda i: lax.rem(my_y + i, cols) * ring + my_z

    def relay(h, slot, sem, peer):
        buffer = (da, db)[h]
        return pltpu.make_async_remote_copy(
            src_ref=buffer.at[slot], dst_ref=buffer.at[slot], send_sem=dep_ss.at[h, sem], recv_sem=dep_rs.at[h, slot],
            device_id={"bis": peer}, device_id_type=MESH,
        )

    for k in range(3):
        flrow[:, k, :] = (masses * beta) * (sampled[k] - speed[k])
    sent = []

    def send(h, slot, peer):
        copy = relay(h, slot, sum(1 for g, _ in sent if g == h), peer)
        copy.start()
        sent.append((h, copy))

    routes = ((along_z, steps_z, along_y, steps_y), (along_y, steps_y, along_z, steps_z))
    for h in range(2):
        lax.fori_loop(half * h, half * (h + 1), deposit, 0, unroll=8)
        buffer = (da, db)[h]
        for k in range(3):
            buffer[me, k] = dep[half * h:half * (h + 1), k, :]
        first, steps, _, _ = routes[h]
        for i in steps:
            send(h, me, first(i))
    for h in range(2):
        _, _, second, steps = routes[h]
        for i in steps:
            send(h, me, second(i))
    for h, i in [(h, i) for i in range(3) for h in range(2)]:
        first, steps, second, others = routes[h]
        if i >= len(steps):
            continue
        slot = first(-steps[i] + (ring if h == 0 else cols))
        relay(h, slot, 0, lax.rem(me + 1, bis)).wait_recv()
        for i in others:
            send(h, slot, second(i))
    for y in range(1, cols):
        for z in range(ring):
            relay(0, lax.rem(my_y + y, cols) * ring + z, 0, lax.rem(me + 1, bis)).wait_recv()
    for y in range(cols):
        for z in range(1, ring):
            relay(1, y * ring + lax.rem(my_z + z, ring), 0, lax.rem(me + 1, bis)).wait_recv()

    def reduce(values_of):
        acc = jnp.zeros((BLK, BLK), F32)
        for t in range(tiles):
            values = jnp.concatenate([values_of(t, h).reshape(BLK // 2, BLK) for h in range(2)], axis=0)
            for piece in split(values)[::-1]:
                acc = acc + jnp.dot(oh_ref[t], piece.astype(BF16), preferred_element_type=F32)
        return acc

    void = void_out[...]
    for k in range(3):
        total = reduce(lambda t, h: (da, db)[h][per * t:per * (t + 1), k])
        fluid_out[k] = fluid_ref[k] - FLUID_GAIN * total * void
    for _, copy in sent:
        copy.wait_send()


def copy_out(*refs):
    sem = refs[-1]
    count = len(refs) // 2
    copies = [pltpu.make_async_copy(refs[k], refs[count + k], sem.at[k]) for k in range(count)]
    for copy in copies:
        copy.start()
    for copy in copies:
        copy.wait()


def local(
    bis, dom, positions, velocities, radii, drag_rates, mig_slots, mig_counts, pair_lists, pair_counts, owners, dep_weights, fluid_velocity,
):
    nb = positions.shape[1]
    levels, capacity = mig_slots.shape[1:]
    pmax = pair_lists.shape[2]
    fb = fluid_velocity.shape[1]
    j = jnp.arange(capacity, dtype=jnp.int32)
    hit = mig_slots[0][:, None, :] == jnp.arange(nb, dtype=jnp.int32)[None, :, None]
    hit = hit & (j[None, None, :] < mig_counts[0][:, None, None])
    inverse = jnp.max(jnp.where(hit, j[None, None, :], -1), axis=2)
    vmem = pl.BlockSpec(memory_space=pltpu.VMEM)
    smem = pl.BlockSpec(memory_space=pltpu.SMEM)
    hbm = pl.BlockSpec(memory_space=pl.ANY)
    dma = pltpu.SemaphoreType.DMA
    tiles = bis * nb // BLK
    outs = pl.pallas_call(
        functools.partial(kernel, bis, dom, pmax),
        out_shape=(
            jax.ShapeDtypeStruct((3, nb, BLK), F32),
            jax.ShapeDtypeStruct((3, nb, BLK), F32),
            jax.ShapeDtypeStruct((3, fb, BLK), F32),
            jax.ShapeDtypeStruct((fb, BLK), F32),
        ),
        in_specs=[hbm] * 4 + [smem] * 3 + [vmem, smem, vmem, hbm, hbm],
        out_specs=(vmem,) * 4,
        scratch_shapes=[
            pltpu.VMEM((3, nb, BLK), F32),
            pltpu.VMEM((3, nb, BLK), F32),
            pltpu.VMEM((nb, BLK), F32),
            pltpu.VMEM((nb, BLK), F32),
            pltpu.VMEM((3, fb, BLK), F32),
            pltpu.VMEM((nb, 8, BLK), F32),
            pltpu.VMEM((nb, 8, BLK), F32),
            pltpu.VMEM((levels, capacity, 8, BLK), F32),
            [pltpu.VMEM((capacity, 8, BLK), F32)] * levels,
            pltpu.VMEM((SUBSTEPS, 2 * G, 8, BLK), F32),
            pltpu.VMEM((8, BLK), jnp.int32),
            pltpu.VMEM((bis, 8, BLK), jnp.int32),
            pltpu.VMEM((bis, nb, 3 * BLK), BF16),
            pltpu.VMEM((bis, nb, 3 * BLK), BF16),
            pltpu.VMEM((nb, BLK, BLK), BF16),
            pltpu.VMEM((nb, 8, BLK), F32),
            pltpu.VMEM((nb, 8, BLK), F32),
            pltpu.VMEM((nb + 2 * G, BLK, 64), BF16),
            pltpu.VMEM((nb + 2 * G, 4, BLK, BLK), F32),
            pltpu.VMEM((nb, 64, 2 * BLK), BF16),
            pltpu.VMEM((pmax, 8, BLK), F32),
            pltpu.VMEM((64, 4 * BLK), BF16),
            pltpu.VMEM((tiles, BLK, BLK), BF16),
            pltpu.VMEM((nb, 8, BLK), F32),
            pltpu.VMEM((nb, BLK), F32),
            pltpu.VMEM((bis, nb, BLK), F32),
            pltpu.VMEM((bis, 3, nb // 2, BLK), F32),
            pltpu.VMEM((bis, 3, nb // 2, BLK), F32),
            dma((5,)),
            dma,
            dma((levels,)),
            dma((levels,)),
            dma((SUBSTEPS, 2)),
            dma((SUBSTEPS, 2)),
            dma((bis,)),
            dma((bis,)),
            dma((bis,)),
            dma((bis,)),
            dma((bis,)),
            dma((bis,)),
            dma((2, bis)),
            dma((2, bis)),
        ],
        compiler_params=pltpu.CompilerParams(
            collective_id=0, has_side_effects=True, vmem_limit_bytes=48 * 1024 * 1024
        ),
    )(
        jnp.transpose(positions[0], (1, 0, 2)),
        jnp.transpose(velocities[0], (1, 0, 2)),
        radii[0],
        drag_rates[0],
        mig_slots[0],
        inverse,
        pair_lists[0],
        pair_lists[0],
        pair_counts,
        owners,
        dep_weights[0],
        jnp.transpose(fluid_velocity[0], (1, 0, 2)),
    )
    pos, vel, fluid, void = pl.pallas_call(
        copy_out,
        out_shape=tuple(jax.ShapeDtypeStruct(out.shape, out.dtype) for out in outs),
        in_specs=[hbm] * 4,
        out_specs=(hbm,) * 4,
        scratch_shapes=[dma((4,))],
    )(*outs)
    return (
        jnp.transpose(pos, (1, 0, 2))[None],
        jnp.transpose(vel, (1, 0, 2))[None],
        jnp.transpose(fluid, (1, 0, 2))[None],
        void[None],
    )


def solution(mesh):
    in_specs = (
        P("bis", "dom", None, None),
        P("bis", "dom", None, None),
        P("bis", "dom", None),
        P("bis", "dom", None),
        P("bis", "dom", None),
        P("bis", "dom"),
        P("bis", None, "dom"),
        P("bis", "dom"),
        P("bis", "dom"),
        P("bis", "dom", None, None),
        P("dom", "bis", None, None),
    )
    out_specs = (
        P("bis", "dom", None, None),
        P("bis", "dom", None, None),
        P("dom", "bis", None, None),
        P("dom", "bis", None),
    )
    body = functools.partial(local, mesh.shape["bis"], mesh.shape["dom"])
    return jax.shard_map(body, mesh=mesh, in_specs=in_specs, out_specs=out_specs, check_vma=False)
```

```python
import functools

import jax
import jax.numpy as jnp
from jax import lax
from jax.experimental import pallas as pl
from jax.experimental.pallas import tpu as pltpu
from jax.sharding import PartitionSpec as P

G = 4
SUBSTEPS = 2
BLK = 128

STIFFNESS = 5.0
DAMPING = 1.0
TIME_STEP = 0.05
EPS_DIST = 0.0001
RADIUS_REF = 0.1
FLUID_GAIN = 0.2

F32 = jnp.float32
BF16 = jnp.bfloat16
MESH = pl.DeviceIdType.MESH


def row_ids():
    return lax.broadcasted_iota(jnp.int32, (8, BLK), 0)


def stack_rows(rows):
    row = row_ids()
    out = jnp.zeros((8, BLK), F32)
    for k, value in enumerate(rows):
        out = jnp.where(row == k, value, out)
    return out


def split(x, parts=3):
    out = []
    for _ in range(parts):
        piece = x.astype(BF16).astype(F32)
        out.append(piece)
        x = x - piece
    return out


def centered(blk):
    return jnp.where(row_ids() < 3, blk - 0.5, blk)


def partner_features(blk):
    row = row_ids()
    y = centered(blk)
    sq = jnp.sum(y[0:3] * y[0:3], axis=0, keepdims=True)
    sv = jnp.sum(y[0:3] * y[3:6], axis=0, keepdims=True)
    base = jnp.where(row < 6, y, jnp.where(row == 6, 1.0, y[6:7]))
    s1, s2, s3 = split(base)
    e = stack_rows(split(sq) + split(sv))
    zero = jnp.zeros((8, BLK), F32)
    return jnp.concatenate([zero, s1, s1, s1, s2, s2, s3, e], axis=0)


def local_features(blk):
    row = row_ids()
    zero = jnp.zeros((8, BLK), F32)
    y = centered(blk)
    sq = jnp.sum(y[0:3] * y[0:3], axis=0, keepdims=True) + EPS_DIST
    sv = jnp.sum(y[0:3] * y[3:6], axis=0, keepdims=True)
    wd = jnp.where(row < 3, -2.0 * y, jnp.where(row == 6, sq, 0.0))
    wv = jnp.concatenate([-y[3:6], -y[0:3], sv, jnp.zeros((1, BLK), F32)], axis=0)
    p1, p2, p3 = split(wd)
    v1, v2, v3 = split(wv)
    ed = jnp.where(row < 3, 1.0, 0.0)
    ev = jnp.where((row >= 3) & (row < 6), 1.0, 0.0)
    d = jnp.concatenate([zero, p1, p2, p3, p1, p2, p1, ed], axis=0)
    v = jnp.concatenate([zero, v1, v2, v3, v1, v2, v1, ev], axis=0)
    return jnp.concatenate([d, v], axis=1).astype(BF16)


def kernel(
    bis, dom, pmax,
    pos_hbm, vel_hbm, rad_hbm, drag_hbm, slots_ref, moved_ref, pairs_ref, cnt_ref, left_hbm, own_hbm, w_hbm, fluid_hbm,
    pos_out, vel_out, fluid_out, void_out,
    pos_ref, vel_ref, rad_ref, drag_ref, left_ref, own_ref, fluid_ref, inv_v, inv_ref,
    st0, st1, mig_s, mig_r, halo_r, own_s, own_r, fl_s, fl_r, w_v, flrow, samp,
    a_ref, xb_ref, b_ref, f_ref, sel_ref, oh_ref, dep, mass_s, mass_r, da, db,
    in_sem, inv_sem, w_sem, mig_ss, mig_rs, halo_ss, halo_rs, own_ss, own_rs, fl_ss, fl_rs, mass_ss, mass_rs, dep_ss, dep_rs,
):
    nb = st0.shape[0]
    per = BLK // nb
    tiles = bis // per
    me = lax.axis_index("bis")
    mine = lax.axis_index("dom")
    right, left = lax.rem(mine + 1, dom), lax.rem(mine + dom - 1, dom)

    barrier = pltpu.get_barrier_semaphore()

    def greet(r, _):
        pl.semaphore_signal(barrier, inc=1, device_id={"bis": lax.rem(me + r, bis)}, device_id_type=MESH)
        return 0

    lax.fori_loop(1, bis, greet, 0)
    for side in (left, right):
        pl.semaphore_signal(barrier, inc=1, device_id={"dom": side}, device_id_type=MESH)

    inputs = [
        pltpu.make_async_copy(src, dst, in_sem.at[k])
        for k, (src, dst) in enumerate((
            (pos_hbm, pos_ref), (vel_hbm, vel_ref), (rad_hbm, rad_ref), (drag_hbm, drag_ref),
            (own_hbm, own_ref), (left_hbm, left_ref), (fluid_hbm, fluid_ref),
        ))
    ]
    for copy in inputs:
        copy.start()
    weights_copy = pltpu.make_async_copy(w_hbm, w_v, w_sem)
    weights_copy.start()

    def to_peer(r, source, target, ss, rs):
        peer = lax.rem(me + r, bis)
        return pltpu.make_async_remote_copy(
            src_ref=source(peer), dst_ref=target.at[me], send_sem=ss.at[r], recv_sem=rs.at[r],
            device_id={"bis": peer}, device_id_type=MESH,
        )

    def start_all(source, target, ss, rs):
        def step(r, _):
            to_peer(r, source, target, ss, rs).start()
            return 0

        lax.fori_loop(1, bis, step, 0)

    def wait_all(source, target, ss, rs):
        def step(r, _):
            to_peer(r, source, target, ss, rs).wait()
            return 0

        lax.fori_loop(1, bis, step, 0)

    lane8 = lax.broadcasted_iota(jnp.int32, (8, BLK), 1)
    capacity = mig_s.shape[1]
    places = jnp.full((8, BLK), -1, jnp.int32)
    for level in range(mig_s.shape[0]):
        for j in range(capacity):
            here = (lane8 == slots_ref[level, j]) & (row_ids() == level) & (moved_ref[0, level] > j)
            places = jnp.where(here, j, places)
    inv_v[...] = places
    inv_copy = pltpu.make_async_copy(inv_v, inv_ref, inv_sem)
    inv_copy.start()
    for copy in inputs[:6]:
        copy.wait()
    own_s[...] = jnp.zeros((8, BLK), jnp.int32)
    own_s[:, 0:nb] = jnp.broadcast_to(own_ref[...], (8, nb))
    quarter = lax.rem(me, per)
    half = nb // 2
    owners = own_s[...]
    low = pltpu.roll(jnp.where(lane8 < half, owners, 0), half * quarter, 1)
    high = pltpu.roll(jnp.where((lane8 >= half) & (lane8 < nb), owners, 0), BLK // 2 - half + half * quarter, 1)
    own_s[...] = low + high
    for k in range(3):
        st0[:, k, :] = pos_ref[k]
        st0[:, 3 + k, :] = vel_ref[k]
    st0[:, 6, :] = rad_ref[...]
    st0[:, 7, :] = drag_ref[...]
    own_r[me] = own_s[...]

    def gather(level):
        def step(j, _):
            mig_s[level, j] = st0[slots_ref[level, j]]
            return 0

        lax.fori_loop(0, capacity, step, 0, unroll=4)

    def migrate_copy(level):
        stride = 2**level
        bit = lax.rem(me // stride, 2)
        partner = me + stride - 2 * stride * bit
        return pltpu.make_async_remote_copy(
            src_ref=mig_s.at[level], dst_ref=mig_r[level], send_sem=mig_ss.at[level], recv_sem=mig_rs.at[level],
            device_id={"bis": partner}, device_id_type=MESH,
        )

    def scatter(level):
        def step(n, _):
            j = inv_ref[level, n]
            st0[n] = jnp.where(j >= 0, mig_r[level][jnp.maximum(j, 0)], st0[n])
            return 0

        lax.fori_loop(0, nb, step, 0, unroll=4)

    gather(0)
    inv_copy.wait()
    pl.semaphore_wait(barrier, bis - 1 + 2)
    migrate_copy(0).start()
    own_source = lambda peer: own_s
    start_all(own_source, own_r, own_ss, own_rs)
    srow = lax.broadcasted_iota(jnp.int32, (64, BLK), 0)
    part = (srow >= 8) & (srow < 56)
    first = (srow // 8 == 1) | (srow // 8 == 4) | (srow // 8 == 6)
    for c, ch in enumerate((0, 1, 2, 7)):
        sel_ref[:, c * BLK:(c + 1) * BLK] = jnp.where(first & part & (lax.rem(srow, 8) == ch), 1.0, 0.0).astype(BF16)
    migrate_copy(0).wait()
    scatter(0)
    gather(1)
    migrate_copy(1).start()

    wait_all(own_source, own_r, own_ss, own_rs)
    inputs[6].wait()
    fluid_bf = jnp.concatenate([fluid_ref[k].astype(BF16) for k in range(3)], axis=1)
    rows = []
    for t in range(tiles):
        row = own_r[per * t, 0:1, :]
        for i in range(1, per):
            row = row + own_r[per * t + i, 0:1, :]
        rows.append(row - BLK * me)
    sub = lax.broadcasted_iota(jnp.int32, (BLK, BLK), 0)
    for t in range(tiles):
        hot = jnp.where(sub == rows[t], 1.0, 0.0)
        oh_ref[t] = hot.astype(BF16)
        chosen = jnp.dot(hot.T.astype(BF16), fluid_bf, preferred_element_type=F32).astype(BF16)
        for i in range(per):
            for h in range(2):
                first_row = BLK // 2 * h + half * i
                fl_s[per * t + i, half * h:half * (h + 1)] = chosen[first_row:first_row + half]
    fl_r[me] = fl_s[me]

    migrate_copy(1).wait()
    scatter(1)
    gather(2)
    migrate_copy(2).start()
    migrate_copy(2).wait()
    scatter(2)

    def halo_copies(step, state):
        return [
            pltpu.make_async_remote_copy(
                src_ref=state.at[pl.ds(nb - G, G)], dst_ref=halo_r.at[step, pl.ds(0, G)],
                send_sem=halo_ss.at[step, 0], recv_sem=halo_rs.at[step, 0],
                device_id={"dom": right}, device_id_type=MESH,
            ),
            pltpu.make_async_remote_copy(
                src_ref=state.at[pl.ds(0, G)], dst_ref=halo_r.at[step, pl.ds(G, G)],
                send_sem=halo_ss.at[step, 1], recv_sem=halo_rs.at[step, 1],
                device_id={"dom": left}, device_id_type=MESH,
            ),
        ]

    fl_source = lambda peer: fl_s.at[peer]

    def prepare(blk, j):
        t = partner_features(blk).T.astype(BF16)
        a_ref[j] = t
        wide = jnp.dot(t, sel_ref[...], preferred_element_type=F32)
        for c in range(4):
            xb_ref[j, c] = wide[:, c * BLK:(c + 1) * BLK]

    mass_source = lambda peer: mass_s

    def deposit(n, _):
        dep[n] = jnp.dot(flrow[n].astype(BF16), w_v[n], preferred_element_type=F32)
        return 0

    def deposit_mass():
        flrow[...] = jnp.zeros(flrow.shape, F32)
        flrow[:, 0, :] = (st0[:, 6, :] / RADIUS_REF) ** 3
        weights_copy.wait()
        lax.fori_loop(0, nb, deposit, 0, unroll=8)
        mass_s[...] = dep[:, 0, :]
        mass_r[me] = mass_s[...]
        start_all(mass_source, mass_r, mass_ss, mass_rs)

    def solid_volume():
        wait_all(mass_source, mass_r, mass_ss, mass_rs)
        solid = jnp.zeros((BLK, BLK), F32)
        for t in range(tiles):
            values = jnp.concatenate([
                mass_r[per * t:per * (t + 1), half * h:half * (h + 1)].reshape(BLK // 2, BLK) for h in range(2)
            ], axis=0)
            for piece in split(values)[::-1]:
                solid = solid + jnp.dot(oh_ref[t], piece.astype(BF16), preferred_element_type=F32)
        void_out[...] = 1.0 / (1.0 + solid)

    def contacts(step, state):
        for copy in halo_copies(step, state):
            copy.start()
        if step == 0:
            start_all(fl_source, fl_r, fl_ss, fl_rs)

        def own_blocks(n, _):
            blk = state[n]
            prepare(blk, n + G)
            b_ref[n] = local_features(blk)
            return 0

        lax.fori_loop(0, nb, own_blocks, 0, unroll=4)
        if step == 0:
            deposit_mass()
        if step == 1:
            solid_volume()
        for copy in halo_copies(step, state):
            copy.wait()

        def rim(n, _):
            prepare(halo_r[step, n], n)
            prepare(halo_r[step, n + G], n + nb + G)
            return 0

        lax.fori_loop(0, G, rim, 0, unroll=2)

        def pair(i, _):
            a = jnp.minimum(pairs_ref[0, i], nb - 1)
            b = pairs_ref[1, i]
            blk = centered(state[a])
            z = jnp.dot(a_ref[b], b_ref[a], preferred_element_type=F32)
            inv = lax.rsqrt(jnp.maximum(z[:, :BLK], EPS_DIST))
            depth = jnp.maximum((xb_ref[b, 3] + blk[6:7]) * inv - 1.0, 0.0)
            f = depth * (STIFFNESS - DAMPING * z[:, BLK:] * inv)
            total = jnp.sum(f, axis=0, keepdims=True)
            f_ref[i] = stack_rows([
                blk[k:k + 1] * total - jnp.sum(f * xb_ref[b, k], axis=0, keepdims=True) for k in range(3)
            ])
            return 0

        lax.fori_loop(0, pmax, pair, 0, unroll=min(16, pmax))
        lane = lax.broadcasted_iota(jnp.int32, (nb, pmax), 1)
        blk_id = lax.broadcasted_iota(jnp.int32, (nb, pmax), 0)
        hot = jnp.where((left_ref[0:1] == blk_id) & (lane < cnt_ref[0, 0]), 1.0, 0.0).astype(BF16)
        out = []
        for k in range(3):
            acc = jnp.zeros((nb, BLK), F32)
            for piece in split(f_ref[:, k, :])[::-1]:
                acc = acc + jnp.dot(hot, piece.astype(BF16), preferred_element_type=F32)
            out.append(acc)
        return out

    def sample():
        wait_all(fl_source, fl_r, fl_ss, fl_rs)
        total = fl_r[0].astype(F32)
        for g in range(1, bis):
            total = total + fl_r[g].astype(F32)
        for k in range(3):
            flrow[:, k, :] = total[:, k * BLK:(k + 1) * BLK]

        def step(n, _):
            samp[n] = lax.dot_general(
                flrow[n].astype(BF16), w_v[n], (((1,), (1,)), ((), ())), preferred_element_type=F32
            )
            return 0

        lax.fori_loop(0, nb, step, 0, unroll=8)

    radius, beta = None, None
    for substep in range(SUBSTEPS):
        state = (st0, st1)[substep]
        contact = contacts(substep, state)
        if substep == 0:
            sample()
            sampled = [samp[:, k, :] for k in range(3)]
            radius, beta = st0[:, 6, :], st0[:, 7, :]
            masses = (radius / RADIUS_REF) ** 3
        speed, place = [], []
        for k in range(3):
            v = state[:, 3 + k, :]
            v = v + TIME_STEP * (contact[k] / masses + beta * (sampled[k] - v))
            speed.append(v)
            place.append(state[:, k, :] + TIME_STEP * v)
        if substep + 1 < SUBSTEPS:
            for k in range(3):
                st1[:, k, :] = place[k]
                st1[:, 3 + k, :] = speed[k]
            st1[:, 6, :] = radius
            st1[:, 7, :] = beta
    for k in range(3):
        pos_out[k] = place[k]
        vel_out[k] = speed[k]

    ring = 4
    cols = bis // ring
    my_y, my_z = me // ring, lax.rem(me, ring)
    steps_z = (1, 3, 2)
    steps_y = (1, 3, 2)[:cols - 1] if cols > 2 else (1,)
    along_z = lambda i: my_y * ring + lax.rem(my_z + i, ring)
    along_y = lambda i: lax.rem(my_y + i, cols) * ring + my_z

    def relay(h, slot, sem, peer):
        buffer = (da, db)[h]
        return pltpu.make_async_remote_copy(
            src_ref=buffer.at[slot], dst_ref=buffer.at[slot], send_sem=dep_ss.at[h, sem], recv_sem=dep_rs.at[h, slot],
            device_id={"bis": peer}, device_id_type=MESH,
        )

    for k in range(3):
        flrow[:, k, :] = (masses * beta) * (sampled[k] - speed[k])
    sent = []

    def send(h, slot, peer):
        copy = relay(h, slot, sum(1 for g, _ in sent if g == h), peer)
        copy.start()
        sent.append((h, copy))

    routes = ((along_z, steps_z, along_y, steps_y), (along_y, steps_y, along_z, steps_z))
    for h in range(2):
        lax.fori_loop(half * h, half * (h + 1), deposit, 0, unroll=8)
        buffer = (da, db)[h]
        for k in range(3):
            buffer[me, k] = dep[half * h:half * (h + 1), k, :]
        first, steps, _, _ = routes[h]
        for i in steps:
            send(h, me, first(i))
    for h in range(2):
        _, _, second, steps = routes[h]
        for i in steps:
            send(h, me, second(i))
    for h, i in [(h, i) for i in range(3) for h in range(2)]:
        first, steps, second, others = routes[h]
        if i >= len(steps):
            continue
        slot = first(-steps[i] + (ring if h == 0 else cols))
        relay(h, slot, 0, lax.rem(me + 1, bis)).wait_recv()
        for i in others:
            send(h, slot, second(i))
    for y in range(1, cols):
        for z in range(ring):
            relay(0, lax.rem(my_y + y, cols) * ring + z, 0, lax.rem(me + 1, bis)).wait_recv()
    for y in range(cols):
        for z in range(1, ring):
            relay(1, y * ring + lax.rem(my_z + z, ring), 0, lax.rem(me + 1, bis)).wait_recv()

    def reduce(values_of):
        acc = jnp.zeros((BLK, BLK), F32)
        for t in range(tiles):
            values = jnp.concatenate([values_of(t, h).reshape(BLK // 2, BLK) for h in range(2)], axis=0)
            for piece in split(values)[::-1]:
                acc = acc + jnp.dot(oh_ref[t], piece.astype(BF16), preferred_element_type=F32)
        return acc

    void = void_out[...]
    for k in range(3):
        total = reduce(lambda t, h: (da, db)[h][per * t:per * (t + 1), k])
        fluid_out[k] = fluid_ref[k] - FLUID_GAIN * total * void
    for _, copy in sent:
        copy.wait_send()


def copy_out(*refs):
    sem = refs[-1]
    count = len(refs) // 2
    copies = [pltpu.make_async_copy(refs[k], refs[count + k], sem.at[k]) for k in range(count)]
    for copy in copies:
        copy.start()
    for copy in copies:
        copy.wait()


def local(
    bis, dom, positions, velocities, radii, drag_rates, mig_slots, mig_counts, pair_lists, pair_counts, owners, dep_weights, fluid_velocity,
):
    nb = positions.shape[1]
    levels, capacity = mig_slots.shape[1:]
    pmax = pair_lists.shape[2]
    fb = fluid_velocity.shape[1]
    vmem = pl.BlockSpec(memory_space=pltpu.VMEM)
    smem = pl.BlockSpec(memory_space=pltpu.SMEM)
    hbm = pl.BlockSpec(memory_space=pltpu.HBM)
    dma = pltpu.SemaphoreType.DMA
    tiles = bis * nb // BLK
    outs = pl.pallas_call(
        functools.partial(kernel, bis, dom, pmax),
        out_shape=(
            jax.ShapeDtypeStruct((3, nb, BLK), F32),
            jax.ShapeDtypeStruct((3, nb, BLK), F32),
            jax.ShapeDtypeStruct((3, fb, BLK), F32),
            jax.ShapeDtypeStruct((fb, BLK), F32),
        ),
        in_specs=[hbm] * 4 + [smem] * 4 + [hbm] * 4,
        out_specs=(vmem,) * 4,
        scratch_shapes=[
            pltpu.VMEM((3, nb, BLK), F32),
            pltpu.VMEM((3, nb, BLK), F32),
            pltpu.VMEM((nb, BLK), F32),
            pltpu.VMEM((nb, BLK), F32),
            pltpu.VMEM((2, pmax), jnp.int32),
            pltpu.VMEM((1, nb), jnp.int32),
            pltpu.VMEM((3, fb, BLK), F32),
            pltpu.VMEM((8, BLK), jnp.int32),
            pltpu.SMEM((8, BLK), jnp.int32),
            pltpu.VMEM((nb, 8, BLK), F32),
            pltpu.VMEM((nb, 8, BLK), F32),
            pltpu.VMEM((levels, capacity, 8, BLK), F32),
            [pltpu.VMEM((capacity, 8, BLK), F32)] * levels,
            pltpu.VMEM((SUBSTEPS, 2 * G, 8, BLK), F32),
            pltpu.VMEM((8, BLK), jnp.int32),
            pltpu.VMEM((bis, 8, BLK), jnp.int32),
            pltpu.VMEM((bis, nb, 3 * BLK), BF16),
            pltpu.VMEM((bis, nb, 3 * BLK), BF16),
            pltpu.VMEM((nb, BLK, BLK), BF16),
            pltpu.VMEM((nb, 8, BLK), F32),
            pltpu.VMEM((nb, 8, BLK), F32),
            pltpu.VMEM((nb + 2 * G, BLK, 64), BF16),
            pltpu.VMEM((nb + 2 * G, 4, BLK, BLK), F32),
            pltpu.VMEM((nb, 64, 2 * BLK), BF16),
            pltpu.VMEM((pmax, 8, BLK), F32),
            pltpu.VMEM((64, 4 * BLK), BF16),
            pltpu.VMEM((tiles, BLK, BLK), BF16),
            pltpu.VMEM((nb, 8, BLK), F32),
            pltpu.VMEM((nb, BLK), F32),
            pltpu.VMEM((bis, nb, BLK), F32),
            pltpu.VMEM((bis, 3, nb // 2, BLK), F32),
            pltpu.VMEM((bis, 3, nb // 2, BLK), F32),
            dma((7,)),
            dma,
            dma,
            dma((levels,)),
            dma((levels,)),
            dma((SUBSTEPS, 2)),
            dma((SUBSTEPS, 2)),
            dma((bis,)),
            dma((bis,)),
            dma((bis,)),
            dma((bis,)),
            dma((bis,)),
            dma((bis,)),
            dma((2, bis)),
            dma((2, bis)),
        ],
        compiler_params=pltpu.CompilerParams(
            collective_id=0, has_side_effects=True, vmem_limit_bytes=64 * 1024 * 1024
        ),
    )(
        jnp.transpose(positions[0], (1, 0, 2)),
        jnp.transpose(velocities[0], (1, 0, 2)),
        radii[0],
        drag_rates[0],
        mig_slots[0],
        mig_counts,
        pair_lists[0],
        pair_counts,
        pair_lists[0],
        owners,
        dep_weights[0],
        jnp.transpose(fluid_velocity[0], (1, 0, 2)),
    )
    pos, vel, fluid, void = pl.pallas_call(
        copy_out,
        out_shape=tuple(jax.ShapeDtypeStruct(out.shape, out.dtype) for out in outs),
        in_specs=[vmem] * 4,
        out_specs=(hbm,) * 4,
        scratch_shapes=[dma((4,))],
        compiler_params=pltpu.CompilerParams(vmem_limit_bytes=64 * 1024 * 1024),
    )(*outs)
    return (
        jnp.transpose(pos, (1, 0, 2))[None],
        jnp.transpose(vel, (1, 0, 2))[None],
        jnp.transpose(fluid, (1, 0, 2))[None],
        void[None],
    )


def solution(mesh):
    in_specs = (
        P("bis", "dom", None, None),
        P("bis", "dom", None, None),
        P("bis", "dom", None),
        P("bis", "dom", None),
        P("bis", "dom", None),
        P("bis", "dom"),
        P("bis", None, "dom"),
        P("bis", "dom"),
        P("bis", "dom"),
        P("bis", "dom", None, None),
        P("dom", "bis", None, None),
    )
    out_specs = (
        P("bis", "dom", None, None),
        P("bis", "dom", None, None),
        P("dom", "bis", None, None),
        P("dom", "bis", None),
    )
    body = functools.partial(local, mesh.shape["bis"], mesh.shape["dom"])
    return jax.shard_map(body, mesh=mesh, in_specs=in_specs, out_specs=out_specs, check_vma=False)
```

```python
import functools

import jax
import jax.numpy as jnp
from jax import lax
from jax.experimental import pallas as pl
from jax.experimental.pallas import tpu as pltpu
from jax.sharding import PartitionSpec as P

G = 4
SUBSTEPS = 2
BLK = 128

STIFFNESS = 5.0
DAMPING = 1.0
TIME_STEP = 0.05
EPS_DIST = 0.0001
RADIUS_REF = 0.1
FLUID_GAIN = 0.2

F32 = jnp.float32
BF16 = jnp.bfloat16
MESH = pl.DeviceIdType.MESH


def row_ids():
    return lax.broadcasted_iota(jnp.int32, (8, BLK), 0)


def stack_rows(rows):
    row = row_ids()
    out = jnp.zeros((8, BLK), F32)
    for k, value in enumerate(rows):
        out = jnp.where(row == k, value, out)
    return out


def split(x, parts=3):
    out = []
    for _ in range(parts):
        piece = x.astype(BF16).astype(F32)
        out.append(piece)
        x = x - piece
    return out


def centered(blk):
    return jnp.where(row_ids() < 3, blk - 0.5, blk)


def partner_features(blk):
    row = row_ids()
    y = centered(blk)
    sq = jnp.sum(y[0:3] * y[0:3], axis=0, keepdims=True)
    sv = jnp.sum(y[0:3] * y[3:6], axis=0, keepdims=True)
    base = jnp.where(row < 6, y, jnp.where(row == 6, 1.0, y[6:7]))
    s1, s2, s3 = split(base)
    e = stack_rows(split(sq) + split(sv))
    zero = jnp.zeros((8, BLK), F32)
    return jnp.concatenate([zero, s1, s1, s1, s2, s2, s3, e], axis=0)


def local_features(blk):
    row = row_ids()
    zero = jnp.zeros((8, BLK), F32)
    y = centered(blk)
    sq = jnp.sum(y[0:3] * y[0:3], axis=0, keepdims=True) + EPS_DIST
    sv = jnp.sum(y[0:3] * y[3:6], axis=0, keepdims=True)
    wd = jnp.where(row < 3, -2.0 * y, jnp.where(row == 6, sq, 0.0))
    wv = jnp.concatenate([-y[3:6], -y[0:3], sv, jnp.zeros((1, BLK), F32)], axis=0)
    p1, p2, p3 = split(wd)
    v1, v2, v3 = split(wv)
    ed = jnp.where(row < 3, 1.0, 0.0)
    ev = jnp.where((row >= 3) & (row < 6), 1.0, 0.0)
    d = jnp.concatenate([zero, p1, p2, p3, p1, p2, p1, ed], axis=0)
    v = jnp.concatenate([zero, v1, v2, v3, v1, v2, v1, ev], axis=0)
    return jnp.concatenate([d, v], axis=1).astype(BF16)


def kernel(
    bis, dom, pmax,
    pos_hbm, vel_hbm, rad_hbm, drag_hbm, slots_hbm, moved_hbm, pairs_hbm, cnt_hbm, left_hbm, own_hbm, w_hbm, fluid_hbm,
    pos_hbm_out, vel_hbm_out, fluid_hbm_out, void_hbm_out,
    slots_ref, moved_ref, pairs_ref, cnt_ref,
    pos_out, vel_out, fluid_out, void_out, pos_ref, vel_ref, rad_ref, drag_ref, left_ref, own_ref, fluid_ref, inv_v, inv_ref,
    st0, st1, mig_s, mig_r, from_s, from_near, from_far, halo_r, own_s, own_r, fl_s, fl_r, w_v, flrow, samp,
    a_ref, xb_ref, b_ref, f_ref, sel_ref, oh_ref, dep, mass_s, mass_r, da, db,
    in_sem, inv_sem, out_sem, w_sem, mig_ss, mig_rs, halo_ss, halo_rs, own_ss, own_rs, fl_ss, fl_rs, mass_ss, mass_rs, dep_ss, dep_rs,
):
    nb = st0.shape[0]
    per = BLK // nb
    tiles = bis // per
    me = lax.axis_index("bis")
    mine = lax.axis_index("dom")
    right, left = lax.rem(mine + 1, dom), lax.rem(mine + dom - 1, dom)

    barrier = pltpu.get_barrier_semaphore()

    def greet(r, _):
        pl.semaphore_signal(barrier, inc=1, device_id={"bis": lax.rem(me + r, bis)}, device_id_type=MESH)
        return 0

    lax.fori_loop(1, bis, greet, 0)
    for side in (left, right):
        pl.semaphore_signal(barrier, inc=1, device_id={"dom": side}, device_id_type=MESH)

    inputs = [
        pltpu.make_async_copy(src, dst, in_sem.at[k])
        for k, (src, dst) in enumerate((
            (pos_hbm, pos_ref), (vel_hbm, vel_ref), (rad_hbm, rad_ref), (drag_hbm, drag_ref),
            (own_hbm, own_ref), (left_hbm, left_ref), (fluid_hbm, fluid_ref),
            (slots_hbm, slots_ref), (moved_hbm, moved_ref), (pairs_hbm, pairs_ref), (cnt_hbm, cnt_ref),
        ))
    ]
    for copy in inputs:
        copy.start()
    weights_copy = pltpu.make_async_copy(w_hbm, w_v, w_sem)
    weights_copy.start()

    def to_peer(r, source, target, ss, rs):
        peer = lax.rem(me + r, bis)
        return pltpu.make_async_remote_copy(
            src_ref=source(peer), dst_ref=target.at[me], send_sem=ss.at[r], recv_sem=rs.at[r],
            device_id={"bis": peer}, device_id_type=MESH,
        )

    def start_all(source, target, ss, rs):
        def step(r, _):
            to_peer(r, source, target, ss, rs).start()
            return 0

        lax.fori_loop(1, bis, step, 0)

    def wait_all(source, target, ss, rs):
        def step(r, _):
            to_peer(r, source, target, ss, rs).wait()
            return 0

        lax.fori_loop(1, bis, step, 0)

    for copy in inputs[7:]:
        copy.wait()
    lane8 = lax.broadcasted_iota(jnp.int32, (8, BLK), 1)
    capacity = slots_ref.shape[1]
    places = jnp.full((8, BLK), -1, jnp.int32)
    for level in range(slots_ref.shape[0]):
        for j in range(capacity):
            here = (lane8 == slots_ref[level, j]) & (row_ids() == level) & (moved_ref[0, level] > j)
            places = jnp.where(here, j, places)
    inv_v[...] = places
    inv_copy = pltpu.make_async_copy(inv_v, inv_ref, inv_sem)
    inv_copy.start()
    for copy in inputs[:6]:
        copy.wait()
    own_s[...] = jnp.zeros((8, BLK), jnp.int32)
    own_s[:, 0:nb] = jnp.broadcast_to(own_ref[...], (8, nb))
    quarter = lax.rem(me, per)
    half = nb // 2
    owners = own_s[...]
    low = pltpu.roll(jnp.where(lane8 < half, owners, 0), half * quarter, 1)
    high = pltpu.roll(jnp.where((lane8 >= half) & (lane8 < nb), owners, 0), BLK // 2 - half + half * quarter, 1)
    own_s[...] = low + high
    for k in range(3):
        st0[:, k, :] = pos_ref[k]
        st0[:, 3 + k, :] = vel_ref[k]
    st0[:, 6, :] = rad_ref[...]
    st0[:, 7, :] = drag_ref[...]
    own_r[me] = own_s[...]

    def gather(level, target):
        def step(j, _):
            target[j] = st0[slots_ref[level, j]]
            return 0

        lax.fori_loop(0, capacity, step, 0, unroll=8)

    def flip(level):
        stride = 2**level
        return stride - 2 * stride * lax.rem(me // stride, 2)

    def migrate_copy(k, source, target, partner):
        return pltpu.make_async_remote_copy(
            src_ref=source, dst_ref=target, send_sem=mig_ss.at[k], recv_sem=mig_rs.at[k],
            device_id={"bis": partner}, device_id_type=MESH,
        )

    def scatter(level, arrived):
        def step(n, _):
            j = inv_ref[level, n]
            st0[n] = jnp.where(j >= 0, arrived[jnp.maximum(j, 0)], st0[n])
            return 0

        lax.fori_loop(0, nb, step, 0, unroll=8)

    near, far = me + flip(1), me + flip(2)
    both = far + flip(1)
    level0 = migrate_copy(0, mig_s[0], mig_r[0], me + flip(0))
    table_near = migrate_copy(1, from_s, from_near, near)
    table_far = migrate_copy(2, from_s, from_far, far)
    level1 = migrate_copy(3, mig_s[1], mig_r[1], near)
    level2 = migrate_copy(4, mig_s[2], mig_r[2], far)
    level12 = migrate_copy(5, mig_s[3], mig_r[3], both)

    def make_table():
        row = lax.broadcasted_iota(jnp.int32, (capacity, BLK), 0)
        table = jnp.zeros((capacity, BLK), jnp.int32)
        for j in range(capacity):
            table = jnp.where(row == j, inv_ref[1, slots_ref[2, j]], table)
        from_s[...] = table

    def pick_for_both():
        def step(j, _):
            want = from_near[pl.ds(j, 1), :]
            block = jnp.zeros((8, BLK), F32)
            for k in range(capacity):
                block = jnp.where(want == k, mig_s[1][k], block)
            mig_s[3][j] = block
            return 0

        lax.fori_loop(0, capacity, step, 0, unroll=4)

    def merge_level2():
        def step(j, _):
            mig_r[2][j] = jnp.where(from_far[pl.ds(j, 1), :] >= 0, mig_r[3][j], mig_r[2][j])
            return 0

        lax.fori_loop(0, capacity, step, 0, unroll=8)

    gather(0, mig_s[0])
    inv_copy.wait()
    make_table()
    pl.semaphore_wait(barrier, bis - 1 + 2)
    level0.start()
    table_near.start()
    table_far.start()
    own_source = lambda peer: own_s
    start_all(own_source, own_r, own_ss, own_rs)
    srow = lax.broadcasted_iota(jnp.int32, (64, BLK), 0)
    part = (srow >= 8) & (srow < 56)
    first = (srow // 8 == 1) | (srow // 8 == 4) | (srow // 8 == 6)
    for c, ch in enumerate((0, 1, 2, 7)):
        sel_ref[:, c * BLK:(c + 1) * BLK] = jnp.where(first & part & (lax.rem(srow, 8) == ch), 1.0, 0.0).astype(BF16)
    level0.wait()
    scatter(0, mig_r[0])
    gather(1, mig_s[1])
    level1.start()
    gather(2, mig_s[2])
    level2.start()
    table_near.wait()
    pick_for_both()
    level12.start()

    wait_all(own_source, own_r, own_ss, own_rs)
    inputs[6].wait()
    fluid_bf = jnp.concatenate([fluid_ref[k].astype(BF16) for k in range(3)], axis=1)
    rows = []
    for t in range(tiles):
        row = own_r[per * t, 0:1, :]
        for i in range(1, per):
            row = row + own_r[per * t + i, 0:1, :]
        rows.append(row - BLK * me)
    sub = lax.broadcasted_iota(jnp.int32, (BLK, BLK), 0)
    for t in range(tiles):
        hot = jnp.where(sub == rows[t], 1.0, 0.0)
        oh_ref[t] = hot.astype(BF16)
        chosen = jnp.dot(hot.T.astype(BF16), fluid_bf, preferred_element_type=F32).astype(BF16)
        for i in range(per):
            for h in range(2):
                first_row = BLK // 2 * h + half * i
                fl_s[per * t + i, half * h:half * (h + 1)] = chosen[first_row:first_row + half]
    fl_r[me] = fl_s[me]

    level1.wait()
    scatter(1, mig_r[1])
    table_far.wait()
    level2.wait()
    level12.wait()
    merge_level2()
    scatter(2, mig_r[2])

    def halo_copies(step, state):
        return [
            pltpu.make_async_remote_copy(
                src_ref=state.at[pl.ds(nb - G, G)], dst_ref=halo_r.at[step, pl.ds(0, G)],
                send_sem=halo_ss.at[step, 0], recv_sem=halo_rs.at[step, 0],
                device_id={"dom": right}, device_id_type=MESH,
            ),
            pltpu.make_async_remote_copy(
                src_ref=state.at[pl.ds(0, G)], dst_ref=halo_r.at[step, pl.ds(G, G)],
                send_sem=halo_ss.at[step, 1], recv_sem=halo_rs.at[step, 1],
                device_id={"dom": left}, device_id_type=MESH,
            ),
        ]

    fl_source = lambda peer: fl_s.at[peer]

    def prepare(step, blk, j):
        t = partner_features(blk).T.astype(BF16)
        a_ref[j] = t
        count = 4 - step
        wide = jnp.dot(t, sel_ref[:, 0:count * BLK], preferred_element_type=F32)
        for c in range(count):
            xb_ref[j, c] = wide[:, c * BLK:(c + 1) * BLK]

    mass_source = lambda peer: mass_s

    def deposit(n, _):
        dep[n] = jnp.dot(flrow[n].astype(BF16), w_v[n], preferred_element_type=F32)
        return 0

    def deposit_mass():
        flrow[...] = jnp.zeros(flrow.shape, F32)
        flrow[:, 0, :] = (st0[:, 6, :] / RADIUS_REF) ** 3
        weights_copy.wait()
        lax.fori_loop(0, nb, deposit, 0, unroll=8)
        mass_s[...] = dep[:, 0, :]
        mass_r[me] = mass_s[...]
        start_all(mass_source, mass_r, mass_ss, mass_rs)

    def solid_volume():
        wait_all(mass_source, mass_r, mass_ss, mass_rs)
        solid = jnp.zeros((BLK, BLK), F32)
        for t in range(tiles):
            values = jnp.concatenate([
                mass_r[per * t:per * (t + 1), half * h:half * (h + 1)].reshape(BLK // 2, BLK) for h in range(2)
            ], axis=0)
            for piece in split(values, 2)[::-1]:
                solid = solid + jnp.dot(oh_ref[t], piece.astype(BF16), preferred_element_type=F32)
        void_out[...] = 1.0 / (1.0 + solid)

    def contacts(step, state):
        for copy in halo_copies(step, state):
            copy.start()
        if step == 0:
            start_all(fl_source, fl_r, fl_ss, fl_rs)

        def own_blocks(n, _):
            blk = state[n]
            prepare(step, blk, n + G)
            b_ref[n] = local_features(blk)
            return 0

        lax.fori_loop(0, nb, own_blocks, 0, unroll=4)
        if step == 0:
            deposit_mass()
        if step == 1:
            solid_volume()
        for copy in halo_copies(step, state):
            copy.wait()

        def rim(n, _):
            prepare(step, halo_r[step, n], n)
            prepare(step, halo_r[step, n + G], n + nb + G)
            return 0

        lax.fori_loop(0, G, rim, 0, unroll=2)

        def pair(i, _):
            a = jnp.minimum(pairs_ref[0, i], nb - 1)
            b = pairs_ref[1, i]
            blk = centered(state[a])
            z = jnp.dot(a_ref[b], b_ref[a], preferred_element_type=F32)
            inv = lax.rsqrt(jnp.maximum(z[:, :BLK], EPS_DIST))
            depth = jnp.maximum((xb_ref[b, 3] + blk[6:7]) * inv - 1.0, 0.0)
            f = depth * (STIFFNESS - DAMPING * z[:, BLK:] * inv)
            total = jnp.sum(f, axis=0, keepdims=True)
            f_ref[i] = stack_rows([
                blk[k:k + 1] * total - jnp.sum(f * xb_ref[b, k], axis=0, keepdims=True) for k in range(3)
            ])
            return 0

        lax.fori_loop(0, pmax, pair, 0, unroll=min(32, pmax))
        lane = lax.broadcasted_iota(jnp.int32, (nb, pmax), 1)
        blk_id = lax.broadcasted_iota(jnp.int32, (nb, pmax), 0)
        hot = jnp.where((left_ref[0:1] == blk_id) & (lane < cnt_ref[0, 0]), 1.0, 0.0).astype(BF16)
        out = []
        for k in range(3):
            acc = jnp.zeros((nb, BLK), F32)
            for piece in split(f_ref[:, k, :], 2)[::-1]:
                acc = acc + jnp.dot(hot, piece.astype(BF16), preferred_element_type=F32)
            out.append(acc)
        return out

    def sample():
        wait_all(fl_source, fl_r, fl_ss, fl_rs)
        total = fl_r[0].astype(F32)
        for g in range(1, bis):
            total = total + fl_r[g].astype(F32)
        for k in range(3):
            flrow[:, k, :] = total[:, k * BLK:(k + 1) * BLK]

        def step(n, _):
            samp[n] = lax.dot_general(
                flrow[n].astype(BF16), w_v[n], (((1,), (1,)), ((), ())), preferred_element_type=F32
            )
            return 0

        lax.fori_loop(0, nb, step, 0, unroll=8)

    radius, beta = None, None
    for substep in range(SUBSTEPS):
        state = (st0, st1)[substep]
        contact = contacts(substep, state)
        if substep == 0:
            sample()
            sampled = [samp[:, k, :] for k in range(3)]
            radius, beta = st0[:, 6, :], st0[:, 7, :]
            masses = (radius / RADIUS_REF) ** 3
        speed, place = [], []
        for k in range(3):
            v = state[:, 3 + k, :]
            v = v + TIME_STEP * (contact[k] / masses + beta * (sampled[k] - v))
            speed.append(v)
            place.append(state[:, k, :] + TIME_STEP * v)
        if substep + 1 < SUBSTEPS:
            for k in range(3):
                st1[:, k, :] = place[k]
                st1[:, 3 + k, :] = speed[k]
            st1[:, 6, :] = radius
            st1[:, 7, :] = beta
    for k in range(3):
        pos_out[k] = place[k]
        vel_out[k] = speed[k]
    results = [
        pltpu.make_async_copy(src, dst, out_sem.at[k])
        for k, (src, dst) in enumerate(
            [(pos_out, pos_hbm_out), (vel_out, vel_hbm_out), (void_out, void_hbm_out)]
            + [(fluid_out.at[k], fluid_hbm_out.at[k]) for k in range(3)]
        )
    ]
    for copy in results[:3]:
        copy.start()

    ring = 4
    cols = bis // ring
    my_y, my_z = me // ring, lax.rem(me, ring)
    steps_z = (1, 3, 2)
    steps_y = (1, 3, 2)[:cols - 1] if cols > 2 else (1,)
    along_z = lambda i: my_y * ring + lax.rem(my_z + i, ring)
    along_y = lambda i: lax.rem(my_y + i, cols) * ring + my_z

    def relay(h, slot, sem, peer):
        buffer = (da, db)[h]
        return pltpu.make_async_remote_copy(
            src_ref=buffer.at[slot], dst_ref=buffer.at[slot], send_sem=dep_ss.at[h, sem], recv_sem=dep_rs.at[h, slot],
            device_id={"bis": peer}, device_id_type=MESH,
        )

    for k in range(3):
        flrow[:, k, :] = (masses * beta) * (sampled[k] - speed[k])
    sent = []

    def send(h, slot, peer):
        copy = relay(h, slot, sum(1 for g, _ in sent if g == h), peer)
        copy.start()
        sent.append((h, copy))

    routes = ((along_z, steps_z, along_y, steps_y), (along_y, steps_y, along_z, steps_z))
    for h in range(2):
        lax.fori_loop(half * h, half * (h + 1), deposit, 0, unroll=8)
        buffer = (da, db)[h]
        for k in range(3):
            buffer[me, k] = dep[half * h:half * (h + 1), k, :]
        first, steps, _, _ = routes[h]
        for i in steps:
            send(h, me, first(i))
    for h in range(2):
        _, _, second, steps = routes[h]
        for i in steps:
            send(h, me, second(i))
    for h, i in [(h, i) for i in range(3) for h in range(2)]:
        first, steps, second, others = routes[h]
        if i >= len(steps):
            continue
        slot = first(-steps[i] + (ring if h == 0 else cols))
        relay(h, slot, 0, lax.rem(me + 1, bis)).wait_recv()
        for i in others:
            send(h, slot, second(i))
    for y in range(1, cols):
        for z in range(ring):
            relay(0, lax.rem(my_y + y, cols) * ring + z, 0, lax.rem(me + 1, bis)).wait_recv()
    for y in range(cols):
        for z in range(1, ring):
            relay(1, y * ring + lax.rem(my_z + z, ring), 0, lax.rem(me + 1, bis)).wait_recv()

    def reduce(values_of):
        acc = jnp.zeros((BLK, BLK), F32)
        for t in range(tiles):
            values = jnp.concatenate([values_of(t, h).reshape(BLK // 2, BLK) for h in range(2)], axis=0)
            for piece in split(values, 2)[::-1]:
                acc = acc + jnp.dot(oh_ref[t], piece.astype(BF16), preferred_element_type=F32)
        return acc

    void = void_out[...]
    for k in range(3):
        total = reduce(lambda t, h: (da, db)[h][per * t:per * (t + 1), k])
        fluid_out[k] = fluid_ref[k] - FLUID_GAIN * total * void
        results[3 + k].start()
    for _, copy in sent:
        copy.wait_send()
    for copy in results:
        copy.wait()


def copy_out(*refs):
    sem = refs[-1]
    count = len(refs) // 2
    copies = [pltpu.make_async_copy(refs[k], refs[count + k], sem.at[k]) for k in range(count)]
    for copy in copies:
        copy.start()
    for copy in copies:
        copy.wait()


def local(
    bis, dom, positions, velocities, radii, drag_rates, mig_slots, mig_counts, pair_lists, pair_counts, owners, dep_weights, fluid_velocity,
):
    nb = positions.shape[1]
    levels, capacity = mig_slots.shape[1:]
    pmax = pair_lists.shape[2]
    fb = fluid_velocity.shape[1]
    vmem = pl.BlockSpec(memory_space=pltpu.VMEM)
    smem = pl.BlockSpec(memory_space=pltpu.SMEM)
    hbm = pl.BlockSpec(memory_space=pltpu.HBM)
    dma = pltpu.SemaphoreType.DMA
    tiles = bis * nb // BLK
    outs = pl.pallas_call(
        functools.partial(kernel, bis, dom, pmax),
        out_shape=(
            jax.ShapeDtypeStruct((3, nb, BLK), F32),
            jax.ShapeDtypeStruct((3, nb, BLK), F32),
            jax.ShapeDtypeStruct((3, fb, BLK), F32),
            jax.ShapeDtypeStruct((fb, BLK), F32),
        ),
        in_specs=[hbm] * 12,
        out_specs=(hbm,) * 4,
        scratch_shapes=[
            pltpu.SMEM((levels, capacity), jnp.int32),
            pltpu.SMEM((1, levels), jnp.int32),
            pltpu.SMEM((2, pmax), jnp.int32),
            pltpu.SMEM((1, 1), jnp.int32),
            pltpu.VMEM((3, nb, BLK), F32),
            pltpu.VMEM((3, nb, BLK), F32),
            pltpu.VMEM((3, fb, BLK), F32),
            pltpu.VMEM((fb, BLK), F32),
            pltpu.VMEM((3, nb, BLK), F32),
            pltpu.VMEM((3, nb, BLK), F32),
            pltpu.VMEM((nb, BLK), F32),
            pltpu.VMEM((nb, BLK), F32),
            pltpu.VMEM((2, pmax), jnp.int32),
            pltpu.VMEM((1, nb), jnp.int32),
            pltpu.VMEM((3, fb, BLK), F32),
            pltpu.VMEM((8, BLK), jnp.int32),
            pltpu.SMEM((8, BLK), jnp.int32),
            pltpu.VMEM((nb, 8, BLK), F32),
            pltpu.VMEM((nb, 8, BLK), F32),
            [pltpu.VMEM((capacity, 8, BLK), F32)] * (levels + 1),
            [pltpu.VMEM((capacity, 8, BLK), F32)] * (levels + 1),
            pltpu.VMEM((capacity, BLK), jnp.int32),
            pltpu.VMEM((capacity, BLK), jnp.int32),
            pltpu.VMEM((capacity, BLK), jnp.int32),
            pltpu.VMEM((SUBSTEPS, 2 * G, 8, BLK), F32),
            pltpu.VMEM((8, BLK), jnp.int32),
            pltpu.VMEM((bis, 8, BLK), jnp.int32),
            pltpu.VMEM((bis, nb, 3 * BLK), BF16),
            pltpu.VMEM((bis, nb, 3 * BLK), BF16),
            pltpu.VMEM((nb, BLK, BLK), BF16),
            pltpu.VMEM((nb, 8, BLK), F32),
            pltpu.VMEM((nb, 8, BLK), F32),
            pltpu.VMEM((nb + 2 * G, BLK, 64), BF16),
            pltpu.VMEM((nb + 2 * G, 4, BLK, BLK), F32),
            pltpu.VMEM((nb, 64, 2 * BLK), BF16),
            pltpu.VMEM((pmax, 8, BLK), F32),
            pltpu.VMEM((64, 4 * BLK), BF16),
            pltpu.VMEM((tiles, BLK, BLK), BF16),
            pltpu.VMEM((nb, 8, BLK), F32),
            pltpu.VMEM((nb, BLK), F32),
            pltpu.VMEM((bis, nb, BLK), F32),
            pltpu.VMEM((bis, 3, nb // 2, BLK), F32),
            pltpu.VMEM((bis, 3, nb // 2, BLK), F32),
            dma((11,)),
            dma,
            dma((6,)),
            dma,
            dma((6,)),
            dma((6,)),
            dma((SUBSTEPS, 2)),
            dma((SUBSTEPS, 2)),
            dma((bis,)),
            dma((bis,)),
            dma((bis,)),
            dma((bis,)),
            dma((bis,)),
            dma((bis,)),
            dma((2, bis)),
            dma((2, bis)),
        ],
        compiler_params=pltpu.CompilerParams(
            collective_id=0, has_side_effects=True, vmem_limit_bytes=64 * 1024 * 1024
        ),
    )(
        jnp.transpose(positions[0], (1, 0, 2)),
        jnp.transpose(velocities[0], (1, 0, 2)),
        radii[0],
        drag_rates[0],
        mig_slots[0],
        mig_counts,
        pair_lists[0],
        pair_counts,
        pair_lists[0],
        owners,
        dep_weights[0],
        jnp.transpose(fluid_velocity[0], (1, 0, 2)),
    )
    pos, vel, fluid, void = pl.pallas_call(
        copy_out,
        out_shape=tuple(jax.ShapeDtypeStruct(out.shape, out.dtype) for out in outs),
        in_specs=[vmem] * 4,
        out_specs=(hbm,) * 4,
        scratch_shapes=[dma((4,))],
        compiler_params=pltpu.CompilerParams(vmem_limit_bytes=64 * 1024 * 1024),
    )(*outs)
    return (
        jnp.transpose(pos, (1, 0, 2))[None],
        jnp.transpose(vel, (1, 0, 2))[None],
        jnp.transpose(fluid, (1, 0, 2))[None],
        void[None],
    )


def solution(mesh):
    in_specs = (
        P("bis", "dom", None, None),
        P("bis", "dom", None, None),
        P("bis", "dom", None),
        P("bis", "dom", None),
        P("bis", "dom", None),
        P("bis", "dom"),
        P("bis", None, "dom"),
        P("bis", "dom"),
        P("bis", "dom"),
        P("bis", "dom", None, None),
        P("dom", "bis", None, None),
    )
    out_specs = (
        P("bis", "dom", None, None),
        P("bis", "dom", None, None),
        P("dom", "bis", None, None),
        P("dom", "bis", None),
    )
    body = functools.partial(local, mesh.shape["bis"], mesh.shape["dom"])
    return jax.shard_map(body, mesh=mesh, in_specs=in_specs, out_specs=out_specs, check_vma=False)
```

```python
import functools

import jax
import jax.numpy as jnp
from jax import lax
from jax.experimental import pallas as pl
from jax.experimental.pallas import tpu as pltpu
from jax.sharding import PartitionSpec as P

G = 4
SUBSTEPS = 2
BLK = 128

STIFFNESS = 5.0
DAMPING = 1.0
TIME_STEP = 0.05
EPS_DIST = 0.0001
RADIUS_REF = 0.1
FLUID_GAIN = 0.2

F32 = jnp.float32
BF16 = jnp.bfloat16
MESH = pl.DeviceIdType.MESH


def row_ids():
    return lax.broadcasted_iota(jnp.int32, (8, BLK), 0)


def stack_rows(rows):
    row = row_ids()
    out = jnp.zeros((8, BLK), F32)
    for k, value in enumerate(rows):
        out = jnp.where(row == k, value, out)
    return out


def split(x, parts=3):
    out = []
    for _ in range(parts):
        piece = x.astype(BF16).astype(F32)
        out.append(piece)
        x = x - piece
    return out


def centered(blk):
    return jnp.where(row_ids() < 3, blk - 0.5, blk)


def partner_features(blk):
    row = row_ids()
    y = centered(blk)
    sq = jnp.sum(y[0:3] * y[0:3], axis=0, keepdims=True)
    sv = jnp.sum(y[0:3] * y[3:6], axis=0, keepdims=True)
    base = jnp.where(row < 6, y, jnp.where(row == 6, 1.0, y[6:7]))
    s1, s2, s3 = split(base)
    e = stack_rows(split(sq) + split(sv))
    zero = jnp.zeros((8, BLK), F32)
    return jnp.concatenate([zero, s1, s1, s1, s2, s2, s3, e], axis=0)


def local_features(blk):
    row = row_ids()
    zero = jnp.zeros((8, BLK), F32)
    y = centered(blk)
    sq = jnp.sum(y[0:3] * y[0:3], axis=0, keepdims=True) + EPS_DIST
    sv = jnp.sum(y[0:3] * y[3:6], axis=0, keepdims=True)
    wd = jnp.where(row < 3, -2.0 * y, jnp.where(row == 6, sq, 0.0))
    wv = jnp.concatenate([-y[3:6], -y[0:3], sv, jnp.zeros((1, BLK), F32)], axis=0)
    p1, p2, p3 = split(wd)
    v1, v2, v3 = split(wv)
    ed = jnp.where(row < 3, 1.0, 0.0)
    ev = jnp.where((row >= 3) & (row < 6), 1.0, 0.0)
    d = jnp.concatenate([zero, p1, p2, p3, p1, p2, p1, ed], axis=0)
    v = jnp.concatenate([zero, v1, v2, v3, v1, v2, v1, ev], axis=0)
    return jnp.concatenate([d, v], axis=1).astype(BF16)


def kernel(
    bis, dom, pmax,
    pos_hbm, vel_hbm, rad_hbm, drag_hbm, slots_hbm, moved_hbm, pairs_hbm, cnt_hbm, left_hbm, own_hbm, w_hbm, fluid_hbm,
    pos_hbm_out, vel_hbm_out, fluid_hbm_out, void_hbm_out,
    slots_ref, moved_ref, pairs_ref, cnt_ref,
    pos_out, vel_out, fluid_out, void_out, pos_ref, vel_ref, rad_ref, drag_ref, left_ref, own_ref, fluid_ref, inv_v, inv_ref,
    st0, st1, mig_s, mig_r, from_s, from_near, from_far, halo_r, own_s, own_r, fl_s, fl_r, w_v, flrow, samp,
    a_ref, xb_ref, b_ref, f_ref, sel_ref, oh_ref, dep, mass_s, mass_r, da, db,
    in_sem, inv_sem, out_sem, w_sem, mig_ss, mig_rs, halo_ss, halo_rs, own_ss, own_rs, fl_ss, fl_rs, mass_ss, mass_rs, dep_ss, dep_rs,
):
    nb = st0.shape[0]
    per = BLK // nb
    tiles = bis // per
    me = lax.axis_index("bis")
    mine = lax.axis_index("dom")
    right, left = lax.rem(mine + 1, dom), lax.rem(mine + dom - 1, dom)

    barrier = pltpu.get_barrier_semaphore()

    def greet(r, _):
        pl.semaphore_signal(barrier, inc=1, device_id={"bis": lax.rem(me + r, bis)}, device_id_type=MESH)
        return 0

    lax.fori_loop(1, bis, greet, 0)
    for side in (left, right):
        pl.semaphore_signal(barrier, inc=1, device_id={"dom": side}, device_id_type=MESH)

    inputs = [
        pltpu.make_async_copy(src, dst, in_sem.at[k])
        for k, (src, dst) in enumerate((
            (pos_hbm, pos_ref), (vel_hbm, vel_ref), (rad_hbm, rad_ref), (drag_hbm, drag_ref),
            (own_hbm, own_ref), (left_hbm, left_ref), (fluid_hbm, fluid_ref),
            (slots_hbm, slots_ref), (moved_hbm, moved_ref), (pairs_hbm, pairs_ref), (cnt_hbm, cnt_ref),
        ))
    ]
    for copy in inputs:
        copy.start()
    weights_copy = pltpu.make_async_copy(w_hbm, w_v, w_sem)
    weights_copy.start()

    def to_peer(r, source, target, ss, rs):
        peer = lax.rem(me + r, bis)
        return pltpu.make_async_remote_copy(
            src_ref=source(peer), dst_ref=target.at[me], send_sem=ss.at[r], recv_sem=rs.at[r],
            device_id={"bis": peer}, device_id_type=MESH,
        )

    def start_all(source, target, ss, rs):
        def step(r, _):
            to_peer(r, source, target, ss, rs).start()
            return 0

        lax.fori_loop(1, bis, step, 0)

    def wait_all(source, target, ss, rs):
        def step(r, _):
            to_peer(r, source, target, ss, rs).wait()
            return 0

        lax.fori_loop(1, bis, step, 0)

    for copy in inputs[7:]:
        copy.wait()
    lane8 = lax.broadcasted_iota(jnp.int32, (8, BLK), 1)
    capacity = slots_ref.shape[2]
    places = jnp.full((8, BLK), -1, jnp.int32)
    for level in range(slots_ref.shape[0]):
        for j in range(capacity):
            here = (lane8 == slots_ref[level, 0, j]) & (row_ids() == level) & (moved_ref[0, level] > j)
            places = jnp.where(here, j, places)
    inv_v[...] = places
    inv_copy = pltpu.make_async_copy(inv_v, inv_ref, inv_sem)
    inv_copy.start()
    for copy in inputs[:6]:
        copy.wait()
    own_s[...] = jnp.zeros((8, BLK), jnp.int32)
    own_s[:, 0:nb] = jnp.broadcast_to(own_ref[...], (8, nb))
    quarter = lax.rem(me, per)
    half = nb // 2
    owners = own_s[...]
    low = pltpu.roll(jnp.where(lane8 < half, owners, 0), half * quarter, 1)
    high = pltpu.roll(jnp.where((lane8 >= half) & (lane8 < nb), owners, 0), BLK // 2 - half + half * quarter, 1)
    own_s[...] = low + high
    for k in range(3):
        st0[:, k, :] = pos_ref[k]
        st0[:, 3 + k, :] = vel_ref[k]
    st0[:, 6, :] = rad_ref[...]
    st0[:, 7, :] = drag_ref[...]
    own_r[me] = own_s[...]

    def gather(level, target):
        def step(j, _):
            target[j] = st0[slots_ref[level, 0, j]]
            return 0

        lax.fori_loop(0, capacity, step, 0, unroll=8)

    def flip(level):
        stride = 2**level
        return stride - 2 * stride * lax.rem(me // stride, 2)

    def migrate_copy(k, source, target, partner):
        return pltpu.make_async_remote_copy(
            src_ref=source, dst_ref=target, send_sem=mig_ss.at[k], recv_sem=mig_rs.at[k],
            device_id={"bis": partner}, device_id_type=MESH,
        )

    def scatter(level, arrived):
        def step(n, _):
            j = inv_ref[level, n]
            st0[n] = jnp.where(j >= 0, arrived[jnp.maximum(j, 0)], st0[n])
            return 0

        lax.fori_loop(0, nb, step, 0, unroll=8)

    near, far = me + flip(1), me + flip(2)
    both = far + flip(1)
    level0 = migrate_copy(0, mig_s[0], mig_r[0], me + flip(0))
    table_near = migrate_copy(1, from_s, from_near, near)
    table_far = migrate_copy(2, from_s, from_far, far)
    level1 = migrate_copy(3, mig_s[1], mig_r[1], near)
    level2 = migrate_copy(4, mig_s[2], mig_r[2], far)
    level12 = migrate_copy(5, mig_s[3], mig_r[3], both)

    def make_table():
        row = lax.broadcasted_iota(jnp.int32, (capacity, BLK), 0)
        table = jnp.zeros((capacity, BLK), jnp.int32)
        for j in range(capacity):
            table = jnp.where(row == j, inv_ref[1, slots_ref[2, 0, j]], table)
        from_s[...] = table

    def pick_for_both():
        def step(j, _):
            want = from_near[pl.ds(j, 1), :]
            block = jnp.zeros((8, BLK), F32)
            for k in range(capacity):
                block = jnp.where(want == k, mig_s[1][k], block)
            mig_s[3][j] = block
            return 0

        lax.fori_loop(0, capacity, step, 0, unroll=4)

    def merge_level2():
        def step(j, _):
            mig_r[2][j] = jnp.where(from_far[pl.ds(j, 1), :] >= 0, mig_r[3][j], mig_r[2][j])
            return 0

        lax.fori_loop(0, capacity, step, 0, unroll=8)

    gather(0, mig_s[0])
    inv_copy.wait()
    make_table()
    pl.semaphore_wait(barrier, bis - 1 + 2)
    level0.start()
    table_near.start()
    table_far.start()
    own_source = lambda peer: own_s
    start_all(own_source, own_r, own_ss, own_rs)
    srow = lax.broadcasted_iota(jnp.int32, (64, BLK), 0)
    part = (srow >= 8) & (srow < 56)
    first = (srow // 8 == 1) | (srow // 8 == 4) | (srow // 8 == 6)
    for c, ch in enumerate((0, 1, 2, 7)):
        sel_ref[:, c * BLK:(c + 1) * BLK] = jnp.where(first & part & (lax.rem(srow, 8) == ch), 1.0, 0.0).astype(BF16)
    level0.wait()
    scatter(0, mig_r[0])
    gather(1, mig_s[1])
    level1.start()
    gather(2, mig_s[2])
    level2.start()
    table_near.wait()
    pick_for_both()
    level12.start()

    wait_all(own_source, own_r, own_ss, own_rs)
    inputs[6].wait()
    fluid_bf = jnp.concatenate([fluid_ref[k].astype(BF16) for k in range(3)], axis=1)
    rows = []
    for t in range(tiles):
        row = own_r[per * t, 0:1, :]
        for i in range(1, per):
            row = row + own_r[per * t + i, 0:1, :]
        rows.append(row - BLK * me)
    sub = lax.broadcasted_iota(jnp.int32, (BLK, BLK), 0)
    for t in range(tiles):
        hot = jnp.where(sub == rows[t], 1.0, 0.0)
        oh_ref[t] = hot.astype(BF16)
        chosen = jnp.dot(hot.T.astype(BF16), fluid_bf, preferred_element_type=F32).astype(BF16)
        for i in range(per):
            for h in range(2):
                first_row = BLK // 2 * h + half * i
                fl_s[per * t + i, half * h:half * (h + 1)] = chosen[first_row:first_row + half]
    fl_r[me] = fl_s[me]
    fl_source = lambda peer: fl_s.at[peer]

    level1.wait()
    scatter(1, mig_r[1])
    table_far.wait()
    level2.wait()
    level12.wait()
    merge_level2()
    scatter(2, mig_r[2])

    def halo_copies(step, state):
        return [
            pltpu.make_async_remote_copy(
                src_ref=state.at[pl.ds(nb - G, G)], dst_ref=halo_r.at[step, pl.ds(0, G)],
                send_sem=halo_ss.at[step, 0], recv_sem=halo_rs.at[step, 0],
                device_id={"dom": right}, device_id_type=MESH,
            ),
            pltpu.make_async_remote_copy(
                src_ref=state.at[pl.ds(0, G)], dst_ref=halo_r.at[step, pl.ds(G, G)],
                send_sem=halo_ss.at[step, 1], recv_sem=halo_rs.at[step, 1],
                device_id={"dom": left}, device_id_type=MESH,
            ),
        ]


    def prepare(step, blk, j):
        t = partner_features(blk).T.astype(BF16)
        a_ref[j] = t
        count = 4 - step
        wide = jnp.dot(t, sel_ref[:, 0:count * BLK], preferred_element_type=F32)
        for c in range(count):
            xb_ref[j, c] = wide[:, c * BLK:(c + 1) * BLK]

    mass_source = lambda peer: mass_s

    def deposit(n, _):
        dep[n] = jnp.dot(flrow[n].astype(BF16), w_v[n], preferred_element_type=F32)
        return 0

    def deposit_mass():
        flrow[...] = jnp.zeros(flrow.shape, F32)
        flrow[:, 0, :] = (st0[:, 6, :] / RADIUS_REF) ** 3
        weights_copy.wait()
        lax.fori_loop(0, nb, deposit, 0, unroll=16)
        mass_s[...] = dep[:, 0, :]
        mass_r[me] = mass_s[...]
        start_all(mass_source, mass_r, mass_ss, mass_rs)

    def solid_volume():
        wait_all(mass_source, mass_r, mass_ss, mass_rs)
        solid = jnp.zeros((BLK, BLK), F32)
        for t in range(tiles):
            values = jnp.concatenate([
                mass_r[per * t:per * (t + 1), half * h:half * (h + 1)].reshape(BLK // 2, BLK) for h in range(2)
            ], axis=0)
            for piece in split(values, 2)[::-1]:
                solid = solid + jnp.dot(oh_ref[t], piece.astype(BF16), preferred_element_type=F32)
        void_out[...] = 1.0 / (1.0 + solid)

    def gather_fluid():
        wait_all(fl_source, fl_r, fl_ss, fl_rs)
        total = fl_r[0].astype(F32)
        for g in range(1, bis):
            total = total + fl_r[g].astype(F32)
        for k in range(3):
            flrow[:, k, :] = total[:, k * BLK:(k + 1) * BLK]

    def sample(n):
        samp[n] = lax.dot_general(
            flrow[n].astype(BF16), w_v[n], (((1,), (1,)), ((), ())), preferred_element_type=F32
        )

    def contacts(step, state):
        for copy in halo_copies(step, state):
            copy.start()
        if step == 0:
            start_all(fl_source, fl_r, fl_ss, fl_rs)

        def own_blocks(n, _):
            blk = state[n]
            prepare(step, blk, n + G)
            b_ref[n] = local_features(blk)
            return 0

        lax.fori_loop(0, nb, own_blocks, 0, unroll=8)
        if step == 0:
            deposit_mass()
        if step == 1:
            solid_volume()
        for copy in halo_copies(step, state):
            copy.wait()

        def rim(n, _):
            prepare(step, halo_r[step, n], n)
            prepare(step, halo_r[step, n + G], n + nb + G)
            return 0

        lax.fori_loop(0, G, rim, 0, unroll=4)

        def pair(i, _):
            a = jnp.minimum(pairs_ref[0, i], nb - 1)
            b = pairs_ref[1, i]
            blk = centered(state[a])
            z = jnp.dot(a_ref[b], b_ref[a], preferred_element_type=F32)
            inv = lax.rsqrt(jnp.maximum(z[:, :BLK], EPS_DIST))
            depth = jnp.maximum((xb_ref[b, 3] + blk[6:7]) * inv - 1.0, 0.0)
            f = depth * (STIFFNESS - DAMPING * z[:, BLK:] * inv)
            total = jnp.sum(f, axis=0, keepdims=True)
            f_ref[i] = stack_rows([
                blk[k:k + 1] * total - jnp.sum(f * xb_ref[b, k], axis=0, keepdims=True) for k in range(3)
            ])
            return 0

        if step == 0:
            first = pmax * 2 // 3
            lax.fori_loop(0, first, pair, 0, unroll=min(32, first))
            gather_fluid()
            turns = 2
            pairs_each, blocks_each = (pmax - first) // turns, nb // turns

            def mixed(turn, _):
                for u in range(pairs_each):
                    pair(first + turn * pairs_each + u, 0)
                    for v in range(blocks_each * u // pairs_each, blocks_each * (u + 1) // pairs_each):
                        sample(turn * blocks_each + v)
                return 0

            lax.fori_loop(0, turns, mixed, 0)
        else:
            lax.fori_loop(0, pmax, pair, 0, unroll=min(32, pmax))
        lane = lax.broadcasted_iota(jnp.int32, (nb, pmax), 1)
        blk_id = lax.broadcasted_iota(jnp.int32, (nb, pmax), 0)
        hot = jnp.where((left_ref[0:1] == blk_id) & (lane < cnt_ref[0, 0]), 1.0, 0.0).astype(BF16)
        out = []
        for k in range(3):
            acc = jnp.zeros((nb, BLK), F32)
            for piece in split(f_ref[:, k, :], 2)[::-1]:
                acc = acc + jnp.dot(hot, piece.astype(BF16), preferred_element_type=F32)
            out.append(acc)
        return out

    radius, beta = None, None
    for substep in range(SUBSTEPS):
        state = (st0, st1)[substep]
        contact = contacts(substep, state)
        if substep == 0:
            sampled = [samp[:, k, :] for k in range(3)]
            radius, beta = st0[:, 6, :], st0[:, 7, :]
            masses = (radius / RADIUS_REF) ** 3
        speed, place = [], []
        for k in range(3):
            v = state[:, 3 + k, :]
            v = v + TIME_STEP * (contact[k] / masses + beta * (sampled[k] - v))
            speed.append(v)
            place.append(state[:, k, :] + TIME_STEP * v)
        if substep + 1 < SUBSTEPS:
            for k in range(3):
                st1[:, k, :] = place[k]
                st1[:, 3 + k, :] = speed[k]
            st1[:, 6, :] = radius
            st1[:, 7, :] = beta
    for k in range(3):
        pos_out[k] = place[k]
        vel_out[k] = speed[k]
    results = [
        pltpu.make_async_copy(src, dst, out_sem.at[k])
        for k, (src, dst) in enumerate(
            [(pos_out, pos_hbm_out), (vel_out, vel_hbm_out), (void_out, void_hbm_out)]
            + [(fluid_out.at[k], fluid_hbm_out.at[k]) for k in range(3)]
        )
    ]
    for copy in results[:3]:
        copy.start()

    ring = 4
    cols = bis // ring
    my_y, my_z = me // ring, lax.rem(me, ring)
    steps_z = (1, 3, 2)
    steps_y = (1, 3, 2)[:cols - 1] if cols > 2 else (1,)
    along_z = lambda i: my_y * ring + lax.rem(my_z + i, ring)
    along_y = lambda i: lax.rem(my_y + i, cols) * ring + my_z

    def relay(h, slot, sem, peer):
        buffer = (da, db)[h]
        return pltpu.make_async_remote_copy(
            src_ref=buffer.at[slot], dst_ref=buffer.at[slot], send_sem=dep_ss.at[h, sem], recv_sem=dep_rs.at[h, slot],
            device_id={"bis": peer}, device_id_type=MESH,
        )

    for k in range(3):
        flrow[:, k, :] = (masses * beta) * (sampled[k] - speed[k])
    sent = []

    def send(h, slot, peer):
        copy = relay(h, slot, sum(1 for g, _ in sent if g == h), peer)
        copy.start()
        sent.append((h, copy))

    routes = ((along_z, steps_z, along_y, steps_y), (along_y, steps_y, along_z, steps_z))
    for h in range(2):
        lax.fori_loop(half * h, half * (h + 1), deposit, 0, unroll=16)
        buffer = (da, db)[h]
        for k in range(3):
            buffer[me, k] = dep[half * h:half * (h + 1), k, :]
        first, steps, _, _ = routes[h]
        for i in steps:
            send(h, me, first(i))
    for h in range(2):
        _, _, second, steps = routes[h]
        for i in steps:
            send(h, me, second(i))
    for h, i in [(h, i) for i in range(3) for h in range(2)]:
        first, steps, second, others = routes[h]
        if i >= len(steps):
            continue
        slot = first(-steps[i] + (ring if h == 0 else cols))
        relay(h, slot, 0, lax.rem(me + 1, bis)).wait_recv()
        for i in others:
            send(h, slot, second(i))
    for y in range(1, cols):
        for z in range(ring):
            relay(0, lax.rem(my_y + y, cols) * ring + z, 0, lax.rem(me + 1, bis)).wait_recv()
    for y in range(cols):
        for z in range(1, ring):
            relay(1, y * ring + lax.rem(my_z + z, ring), 0, lax.rem(me + 1, bis)).wait_recv()

    def reduce(values_of):
        acc = jnp.zeros((BLK, BLK), F32)
        for t in range(tiles):
            values = jnp.concatenate([values_of(t, h).reshape(BLK // 2, BLK) for h in range(2)], axis=0)
            for piece in split(values, 2)[::-1]:
                acc = acc + jnp.dot(oh_ref[t], piece.astype(BF16), preferred_element_type=F32)
        return acc

    void = void_out[...]
    for k in range(3):
        total = reduce(lambda t, h: (da, db)[h][per * t:per * (t + 1), k])
        fluid_out[k] = fluid_ref[k] - FLUID_GAIN * total * void
        results[3 + k].start()
    for _, copy in sent:
        copy.wait_send()
    for copy in results:
        copy.wait()


def copy_out(*refs):
    sem = refs[-1]
    count = len(refs) // 2
    copies = [pltpu.make_async_copy(refs[k], refs[count + k], sem.at[k]) for k in range(count)]
    for copy in copies:
        copy.start()
    for copy in copies:
        copy.wait()


def local(
    bis, dom, positions, velocities, radii, drag_rates, mig_slots, mig_counts, pair_lists, pair_counts, owners, dep_weights, fluid_velocity,
):
    nb = positions.shape[1]
    levels, capacity = mig_slots.shape[1:]
    pmax = pair_lists.shape[2]
    fb = fluid_velocity.shape[1]
    vmem = pl.BlockSpec(memory_space=pltpu.VMEM)
    smem = pl.BlockSpec(memory_space=pltpu.SMEM)
    hbm = pl.BlockSpec(memory_space=pltpu.HBM)
    dma = pltpu.SemaphoreType.DMA
    tiles = bis * nb // BLK
    outs = pl.pallas_call(
        functools.partial(kernel, bis, dom, pmax),
        out_shape=(
            jax.ShapeDtypeStruct((3, nb, BLK), F32),
            jax.ShapeDtypeStruct((3, nb, BLK), F32),
            jax.ShapeDtypeStruct((3, fb, BLK), F32),
            jax.ShapeDtypeStruct((fb, BLK), F32),
        ),
        in_specs=[hbm] * 12,
        out_specs=(hbm,) * 4,
        scratch_shapes=[
            pltpu.SMEM((levels, 1, capacity), jnp.int32),
            pltpu.SMEM((1, levels), jnp.int32),
            pltpu.SMEM((2, pmax), jnp.int32),
            pltpu.SMEM((1, 1), jnp.int32),
            pltpu.VMEM((3, nb, BLK), F32),
            pltpu.VMEM((3, nb, BLK), F32),
            pltpu.VMEM((3, fb, BLK), F32),
            pltpu.VMEM((fb, BLK), F32),
            pltpu.VMEM((3, nb, BLK), F32),
            pltpu.VMEM((3, nb, BLK), F32),
            pltpu.VMEM((nb, BLK), F32),
            pltpu.VMEM((nb, BLK), F32),
            pltpu.VMEM((2, pmax), jnp.int32),
            pltpu.VMEM((1, nb), jnp.int32),
            pltpu.VMEM((3, fb, BLK), F32),
            pltpu.VMEM((8, BLK), jnp.int32),
            pltpu.SMEM((8, BLK), jnp.int32),
            pltpu.VMEM((nb, 8, BLK), F32),
            pltpu.VMEM((nb, 8, BLK), F32),
            [pltpu.VMEM((capacity, 8, BLK), F32)] * (levels + 1),
            [pltpu.VMEM((capacity, 8, BLK), F32)] * (levels + 1),
            pltpu.VMEM((capacity, BLK), jnp.int32),
            pltpu.VMEM((capacity, BLK), jnp.int32),
            pltpu.VMEM((capacity, BLK), jnp.int32),
            pltpu.VMEM((SUBSTEPS, 2 * G, 8, BLK), F32),
            pltpu.VMEM((8, BLK), jnp.int32),
            pltpu.VMEM((bis, 8, BLK), jnp.int32),
            pltpu.VMEM((bis, nb, 3 * BLK), BF16),
            pltpu.VMEM((bis, nb, 3 * BLK), BF16),
            pltpu.VMEM((nb, BLK, BLK), BF16),
            pltpu.VMEM((nb, 8, BLK), F32),
            pltpu.VMEM((nb, 8, BLK), F32),
            pltpu.VMEM((nb + 2 * G, BLK, 64), BF16),
            pltpu.VMEM((nb + 2 * G, 4, BLK, BLK), F32),
            pltpu.VMEM((nb, 64, 2 * BLK), BF16),
            pltpu.VMEM((pmax, 8, BLK), F32),
            pltpu.VMEM((64, 4 * BLK), BF16),
            pltpu.VMEM((tiles, BLK, BLK), BF16),
            pltpu.VMEM((nb, 8, BLK), F32),
            pltpu.VMEM((nb, BLK), F32),
            pltpu.VMEM((bis, nb, BLK), F32),
            pltpu.VMEM((bis, 3, nb // 2, BLK), F32),
            pltpu.VMEM((bis, 3, nb // 2, BLK), F32),
            dma((11,)),
            dma,
            dma((6,)),
            dma,
            dma((6,)),
            dma((6,)),
            dma((SUBSTEPS, 2)),
            dma((SUBSTEPS, 2)),
            dma((bis,)),
            dma((bis,)),
            dma((bis,)),
            dma((bis,)),
            dma((bis,)),
            dma((bis,)),
            dma((2, bis)),
            dma((2, bis)),
        ],
        compiler_params=pltpu.CompilerParams(
            collective_id=0, has_side_effects=True, vmem_limit_bytes=64 * 1024 * 1024
        ),
    )(
        jnp.transpose(positions[0], (1, 0, 2)),
        jnp.transpose(velocities[0], (1, 0, 2)),
        radii[0],
        drag_rates[0],
        jnp.transpose(mig_slots, (1, 0, 2)),
        mig_counts,
        pair_lists[0],
        pair_counts,
        pair_lists[0],
        owners,
        dep_weights[0],
        jnp.transpose(fluid_velocity[0], (1, 0, 2)),
    )
    pos, vel, fluid, void = pl.pallas_call(
        copy_out,
        out_shape=tuple(jax.ShapeDtypeStruct(out.shape, out.dtype) for out in outs),
        in_specs=[vmem] * 4,
        out_specs=(hbm,) * 4,
        scratch_shapes=[dma((4,))],
        compiler_params=pltpu.CompilerParams(vmem_limit_bytes=64 * 1024 * 1024),
    )(*outs)
    return (
        jnp.transpose(pos, (1, 0, 2))[None],
        jnp.transpose(vel, (1, 0, 2))[None],
        jnp.transpose(fluid, (1, 0, 2))[None],
        void[None],
    )


def solution(mesh):
    in_specs = (
        P("bis", "dom", None, None),
        P("bis", "dom", None, None),
        P("bis", "dom", None),
        P("bis", "dom", None),
        P("bis", "dom", None),
        P("bis", "dom"),
        P("bis", None, "dom"),
        P("bis", "dom"),
        P("bis", "dom"),
        P("bis", "dom", None, None),
        P("dom", "bis", None, None),
    )
    out_specs = (
        P("bis", "dom", None, None),
        P("bis", "dom", None, None),
        P("dom", "bis", None, None),
        P("dom", "bis", None),
    )
    body = functools.partial(local, mesh.shape["bis"], mesh.shape["dom"])
    return jax.shard_map(body, mesh=mesh, in_specs=in_specs, out_specs=out_specs, check_vma=False)
```

```python
import functools

import jax
import jax.numpy as jnp
from jax import lax
from jax.experimental import pallas as pl
from jax.experimental.pallas import tpu as pltpu
from jax.sharding import PartitionSpec as P

G = 4
SUBSTEPS = 2
BLK = 128

STIFFNESS = 5.0
DAMPING = 1.0
TIME_STEP = 0.05
EPS_DIST = 0.0001
RADIUS_REF = 0.1
FLUID_GAIN = 0.2

F32 = jnp.float32
BF16 = jnp.bfloat16
MESH = pl.DeviceIdType.MESH


def row_ids():
    return lax.broadcasted_iota(jnp.int32, (8, BLK), 0)


def stack_rows(rows):
    row = row_ids()
    out = jnp.zeros((8, BLK), F32)
    for k, value in enumerate(rows):
        out = jnp.where(row == k, value, out)
    return out


def split(x, parts=3):
    out = []
    for _ in range(parts):
        piece = x.astype(BF16).astype(F32)
        out.append(piece)
        x = x - piece
    return out


def centered(blk):
    return jnp.where(row_ids() < 3, blk - 0.5, blk)


def partner_features(blk):
    row = row_ids()
    y = centered(blk)
    sq = jnp.sum(y[0:3] * y[0:3], axis=0, keepdims=True)
    sv = jnp.sum(y[0:3] * y[3:6], axis=0, keepdims=True)
    base = jnp.where(row < 6, y, jnp.where(row == 6, 1.0, y[6:7]))
    s1, s2, s3 = split(base)
    e = stack_rows(split(sq) + split(sv))
    zero = jnp.zeros((8, BLK), F32)
    return jnp.concatenate([zero, s1, s1, s1, s2, s2, s3, e], axis=0)


def local_features(blk):
    row = row_ids()
    zero = jnp.zeros((8, BLK), F32)
    y = centered(blk)
    sq = jnp.sum(y[0:3] * y[0:3], axis=0, keepdims=True) + EPS_DIST
    sv = jnp.sum(y[0:3] * y[3:6], axis=0, keepdims=True)
    wd = jnp.where(row < 3, -2.0 * y, jnp.where(row == 6, sq, 0.0))
    wv = jnp.concatenate([-y[3:6], -y[0:3], sv, jnp.zeros((1, BLK), F32)], axis=0)
    p1, p2, p3 = split(wd)
    v1, v2, v3 = split(wv)
    ed = jnp.where(row < 3, 1.0, 0.0)
    ev = jnp.where((row >= 3) & (row < 6), 1.0, 0.0)
    d = jnp.concatenate([zero, p1, p2, p3, p1, p2, p1, ed], axis=0)
    v = jnp.concatenate([zero, v1, v2, v3, v1, v2, v1, ev], axis=0)
    return jnp.concatenate([d, v], axis=1).astype(BF16)


def kernel(
    bis, dom, pmax,
    pos_hbm, vel_hbm, rad_hbm, drag_hbm, slots_hbm, moved_hbm, pairs_hbm, cnt_hbm, left_hbm, own_hbm, w_hbm, fluid_hbm,
    pos_hbm_out, vel_hbm_out, fluid_hbm_out, void_hbm_out,
    slots_ref, moved_ref, pairs_ref, cnt_ref,
    pos_out, vel_out, fluid_out, void_out, pos_ref, vel_ref, rad_ref, drag_ref, left_ref, own_ref, fluid_ref, inv_v, inv_ref,
    st0, st1, mig_s, mig_r, from_s, from_near, from_far, halo_r, own_s, own_r, fl_s, fl_r, w_v, flrow, samp,
    a_ref, xb_ref, b_ref, f_ref, sel_ref, oh_ref, dep, mass_s, mass_r, da, db,
    in_sem, inv_sem, out_sem, w_sem, mig_ss, mig_rs, halo_ss, halo_rs, own_ss, own_rs, fl_ss, fl_rs, mass_ss, mass_rs, dep_ss, dep_rs,
):
    nb = st0.shape[0]
    per = BLK // nb
    tiles = bis // per
    me = lax.axis_index("bis")
    mine = lax.axis_index("dom")
    right, left = lax.rem(mine + 1, dom), lax.rem(mine + dom - 1, dom)

    barrier = pltpu.get_barrier_semaphore()

    def greet(r, _):
        pl.semaphore_signal(barrier, inc=1, device_id={"bis": lax.rem(me + r, bis)}, device_id_type=MESH)
        return 0

    lax.fori_loop(1, bis, greet, 0)
    for side in (left, right):
        pl.semaphore_signal(barrier, inc=1, device_id={"dom": side}, device_id_type=MESH)

    inputs = [
        pltpu.make_async_copy(src, dst, in_sem.at[k])
        for k, (src, dst) in enumerate((
            (pos_hbm, pos_ref), (vel_hbm, vel_ref), (rad_hbm, rad_ref), (drag_hbm, drag_ref),
            (own_hbm, own_ref), (left_hbm, left_ref), (fluid_hbm, fluid_ref),
            (slots_hbm, slots_ref), (moved_hbm, moved_ref), (pairs_hbm, pairs_ref), (cnt_hbm, cnt_ref),
        ))
    ]
    for copy in inputs:
        copy.start()
    weights_copy = pltpu.make_async_copy(w_hbm, w_v, w_sem)
    weights_copy.start()

    def to_peer(r, source, target, ss, rs):
        peer = lax.rem(me + r, bis)
        return pltpu.make_async_remote_copy(
            src_ref=source(peer), dst_ref=target.at[me], send_sem=ss.at[r], recv_sem=rs.at[r],
            device_id={"bis": peer}, device_id_type=MESH,
        )

    def start_all(source, target, ss, rs):
        def step(r, _):
            to_peer(r, source, target, ss, rs).start()
            return 0

        lax.fori_loop(1, bis, step, 0)

    def wait_all(source, target, ss, rs):
        def step(r, _):
            to_peer(r, source, target, ss, rs).wait()
            return 0

        lax.fori_loop(1, bis, step, 0)

    for copy in inputs[7:]:
        copy.wait()
    lane8 = lax.broadcasted_iota(jnp.int32, (8, BLK), 1)
    capacity = slots_ref.shape[2]
    places = jnp.full((8, BLK), -1, jnp.int32)
    for level in range(slots_ref.shape[0]):
        for j in range(capacity):
            here = (lane8 == slots_ref[level, 0, j]) & (row_ids() == level) & (moved_ref[0, level] > j)
            places = jnp.where(here, j, places)
    inv_v[...] = places
    inv_copy = pltpu.make_async_copy(inv_v, inv_ref, inv_sem)
    inv_copy.start()
    for copy in inputs[:6]:
        copy.wait()
    own_s[...] = jnp.zeros((8, BLK), jnp.int32)
    own_s[:, 0:nb] = jnp.broadcast_to(own_ref[...], (8, nb))
    quarter = lax.rem(me, per)
    half = nb // 2
    owners = own_s[...]
    low = pltpu.roll(jnp.where(lane8 < half, owners, 0), half * quarter, 1)
    high = pltpu.roll(jnp.where((lane8 >= half) & (lane8 < nb), owners, 0), BLK // 2 - half + half * quarter, 1)
    own_s[...] = low + high
    for k in range(3):
        st0[:, k, :] = pos_ref[k]
        st0[:, 3 + k, :] = vel_ref[k]
    st0[:, 6, :] = rad_ref[...]
    st0[:, 7, :] = drag_ref[...]
    own_r[me] = own_s[...]

    def gather(level, target):
        def step(j, _):
            target[j] = st0[slots_ref[level, 0, j]]
            return 0

        lax.fori_loop(0, capacity, step, 0, unroll=16)

    def flip(level):
        stride = 2**level
        return stride - 2 * stride * lax.rem(me // stride, 2)

    def migrate_copy(k, source, target, partner):
        return pltpu.make_async_remote_copy(
            src_ref=source, dst_ref=target, send_sem=mig_ss.at[k], recv_sem=mig_rs.at[k],
            device_id={"bis": partner}, device_id_type=MESH,
        )

    def scatter(level, arrived):
        def step(n, _):
            j = inv_ref[level, n]
            st0[n] = jnp.where(j >= 0, arrived[jnp.maximum(j, 0)], st0[n])
            return 0

        lax.fori_loop(0, nb, step, 0, unroll=16)

    near, far = me + flip(1), me + flip(2)
    both = far + flip(1)
    level0 = migrate_copy(0, mig_s[0], mig_r[0], me + flip(0))
    table_near = migrate_copy(1, from_s, from_near, near)
    table_far = migrate_copy(2, from_s, from_far, far)
    level1 = migrate_copy(3, mig_s[1], mig_r[1], near)
    level2 = migrate_copy(4, mig_s[2], mig_r[2], far)
    level12 = migrate_copy(5, mig_s[3], mig_r[3], both)

    def make_table():
        row = lax.broadcasted_iota(jnp.int32, (capacity, BLK), 0)
        table = jnp.zeros((capacity, BLK), jnp.int32)
        for j in range(capacity):
            table = jnp.where(row == j, inv_ref[1, slots_ref[2, 0, j]], table)
        from_s[...] = table

    def pick_for_both():
        def step(j, _):
            want = from_near[pl.ds(j, 1), :]
            block = jnp.zeros((8, BLK), F32)
            for k in range(capacity):
                block = jnp.where(want == k, mig_s[1][k], block)
            mig_s[3][j] = block
            return 0

        lax.fori_loop(0, capacity, step, 0, unroll=16)

    def merge_level2():
        def step(j, _):
            mig_r[2][j] = jnp.where(from_far[pl.ds(j, 1), :] >= 0, mig_r[3][j], mig_r[2][j])
            return 0

        lax.fori_loop(0, capacity, step, 0, unroll=16)

    gather(0, mig_s[0])
    inv_copy.wait()
    make_table()
    pl.semaphore_wait(barrier, bis - 1 + 2)
    level0.start()
    table_near.start()
    table_far.start()
    own_source = lambda peer: own_s
    start_all(own_source, own_r, own_ss, own_rs)
    srow = lax.broadcasted_iota(jnp.int32, (64, BLK), 0)
    part = (srow >= 8) & (srow < 56)
    first = (srow // 8 == 1) | (srow // 8 == 4) | (srow // 8 == 6)
    for c, ch in enumerate((0, 1, 2, 7)):
        sel_ref[:, c * BLK:(c + 1) * BLK] = jnp.where(first & part & (lax.rem(srow, 8) == ch), 1.0, 0.0).astype(BF16)
    level0.wait()
    scatter(0, mig_r[0])
    gather(1, mig_s[1])
    level1.start()
    gather(2, mig_s[2])
    level2.start()
    table_near.wait()
    pick_for_both()
    level12.start()

    wait_all(own_source, own_r, own_ss, own_rs)
    inputs[6].wait()
    fluid_bf = jnp.concatenate([fluid_ref[k].astype(BF16) for k in range(3)], axis=1)
    rows = []
    for t in range(tiles):
        row = own_r[per * t, 0:1, :]
        for i in range(1, per):
            row = row + own_r[per * t + i, 0:1, :]
        rows.append(row - BLK * me)
    sub = lax.broadcasted_iota(jnp.int32, (BLK, BLK), 0)
    for t in range(tiles):
        hot = jnp.where(sub == rows[t], 1.0, 0.0)
        oh_ref[t] = hot.astype(BF16)
        chosen = jnp.dot(hot.T.astype(BF16), fluid_bf, preferred_element_type=F32).astype(BF16)
        for i in range(per):
            for h in range(2):
                first_row = BLK // 2 * h + half * i
                fl_s[per * t + i, half * h:half * (h + 1)] = chosen[first_row:first_row + half]
    fl_r[me] = fl_s[me]
    fl_source = lambda peer: fl_s.at[peer]

    level1.wait()
    scatter(1, mig_r[1])
    table_far.wait()
    level2.wait()
    level12.wait()
    merge_level2()
    scatter(2, mig_r[2])

    def halo_copies(step, state):
        return [
            pltpu.make_async_remote_copy(
                src_ref=state.at[pl.ds(nb - G, G)], dst_ref=halo_r.at[step, pl.ds(0, G)],
                send_sem=halo_ss.at[step, 0], recv_sem=halo_rs.at[step, 0],
                device_id={"dom": right}, device_id_type=MESH,
            ),
            pltpu.make_async_remote_copy(
                src_ref=state.at[pl.ds(0, G)], dst_ref=halo_r.at[step, pl.ds(G, G)],
                send_sem=halo_ss.at[step, 1], recv_sem=halo_rs.at[step, 1],
                device_id={"dom": left}, device_id_type=MESH,
            ),
        ]


    def prepare(step, blk, j):
        t = partner_features(blk).T.astype(BF16)
        a_ref[j] = t
        count = 4 - step
        wide = jnp.dot(t, sel_ref[:, 0:count * BLK], preferred_element_type=F32)
        for c in range(count):
            xb_ref[j, c] = wide[:, c * BLK:(c + 1) * BLK]

    mass_source = lambda peer: mass_s

    def deposit(n, _):
        dep[n] = jnp.dot(flrow[n].astype(BF16), w_v[n], preferred_element_type=F32)
        return 0

    def load_mass():
        flrow[...] = jnp.zeros(flrow.shape, F32)
        flrow[:, 0, :] = (st0[:, 6, :] / RADIUS_REF) ** 3
        weights_copy.wait()

    def send_mass():
        mass_s[...] = dep[:, 0, :]
        mass_r[me] = mass_s[...]
        start_all(mass_source, mass_r, mass_ss, mass_rs)

    def solid_volume():
        wait_all(mass_source, mass_r, mass_ss, mass_rs)
        solid = jnp.zeros((BLK, BLK), F32)
        for t in range(tiles):
            values = jnp.concatenate([
                mass_r[per * t:per * (t + 1), half * h:half * (h + 1)].reshape(BLK // 2, BLK) for h in range(2)
            ], axis=0)
            for piece in split(values, 2)[::-1]:
                solid = solid + jnp.dot(oh_ref[t], piece.astype(BF16), preferred_element_type=F32)
        void_out[...] = 1.0 / (1.0 + solid)

    def gather_fluid():
        wait_all(fl_source, fl_r, fl_ss, fl_rs)
        total = fl_r[0].astype(F32)
        for g in range(1, bis):
            total = total + fl_r[g].astype(F32)
        for k in range(3):
            flrow[:, k, :] = total[:, k * BLK:(k + 1) * BLK]

    def sample(n, _):
        samp[n] = lax.dot_general(
            flrow[n].astype(BF16), w_v[n], (((1,), (1,)), ((), ())), preferred_element_type=F32
        )

    def contacts(step, state):
        for copy in halo_copies(step, state):
            copy.start()
        if step == 0:
            start_all(fl_source, fl_r, fl_ss, fl_rs)

        def own_blocks(n, _):
            blk = state[n]
            prepare(step, blk, n + G)
            b_ref[n] = local_features(blk)
            return 0

        lax.fori_loop(0, nb, own_blocks, 0, unroll=8)
        if step == 1:
            solid_volume()
        for copy in halo_copies(step, state):
            copy.wait()

        def rim(n, _):
            prepare(step, halo_r[step, n], n)
            prepare(step, halo_r[step, n + G], n + nb + G)
            return 0

        lax.fori_loop(0, G, rim, 0, unroll=4)

        def pair(i, _):
            a = jnp.minimum(pairs_ref[0, i], nb - 1)
            b = pairs_ref[1, i]
            blk = centered(state[a])
            z = jnp.dot(a_ref[b], b_ref[a], preferred_element_type=F32)
            inv = lax.rsqrt(jnp.maximum(z[:, :BLK], EPS_DIST))
            depth = jnp.maximum((xb_ref[b, 3] + blk[6:7]) * inv - 1.0, 0.0)
            f = depth * (STIFFNESS - DAMPING * z[:, BLK:] * inv)
            total = jnp.sum(f, axis=0, keepdims=True)
            f_ref[i] = stack_rows([
                blk[k:k + 1] * total - jnp.sum(f * xb_ref[b, k], axis=0, keepdims=True) for k in range(3)
            ])
            return 0

        def beside(begin, end, turns, extra):
            pairs_each, blocks_each = (end - begin) // turns, nb // turns

            def mixed(turn, _):
                for u in range(pairs_each):
                    pair(begin + turn * pairs_each + u, 0)
                    for v in range(blocks_each * u // pairs_each, blocks_each * (u + 1) // pairs_each):
                        extra(turn * blocks_each + v, 0)
                return 0

            lax.fori_loop(0, turns, mixed, 0)

        if step == 0:
            first = pmax * 2 // 3
            load_mass()
            beside(0, first, 4 if first % 4 == 0 else 2, deposit)
            send_mass()
            gather_fluid()
            beside(first, pmax, 2, sample)
        else:
            lax.fori_loop(0, pmax, pair, 0, unroll=min(48, pmax))
        lane = lax.broadcasted_iota(jnp.int32, (nb, pmax), 1)
        blk_id = lax.broadcasted_iota(jnp.int32, (nb, pmax), 0)
        hot = jnp.where((left_ref[0:1] == blk_id) & (lane < cnt_ref[0, 0]), 1.0, 0.0).astype(BF16)
        out = []
        for k in range(3):
            acc = jnp.zeros((nb, BLK), F32)
            for piece in split(f_ref[:, k, :], 2)[::-1]:
                acc = acc + jnp.dot(hot, piece.astype(BF16), preferred_element_type=F32)
            out.append(acc)
        return out

    radius, beta = None, None
    for substep in range(SUBSTEPS):
        state = (st0, st1)[substep]
        contact = contacts(substep, state)
        if substep == 0:
            sampled = [samp[:, k, :] for k in range(3)]
            radius, beta = st0[:, 6, :], st0[:, 7, :]
            masses = (radius / RADIUS_REF) ** 3
        speed, place = [], []
        for k in range(3):
            v = state[:, 3 + k, :]
            v = v + TIME_STEP * (contact[k] / masses + beta * (sampled[k] - v))
            speed.append(v)
            place.append(state[:, k, :] + TIME_STEP * v)
        if substep + 1 < SUBSTEPS:
            for k in range(3):
                st1[:, k, :] = place[k]
                st1[:, 3 + k, :] = speed[k]
            st1[:, 6, :] = radius
            st1[:, 7, :] = beta
    for k in range(3):
        pos_out[k] = place[k]
        vel_out[k] = speed[k]
    results = [
        pltpu.make_async_copy(src, dst, out_sem.at[k])
        for k, (src, dst) in enumerate(
            [(pos_out, pos_hbm_out), (vel_out, vel_hbm_out), (void_out, void_hbm_out)]
            + [(fluid_out.at[k], fluid_hbm_out.at[k]) for k in range(3)]
        )
    ]
    for copy in results[:3]:
        copy.start()

    ring = 4
    cols = bis // ring
    my_y, my_z = me // ring, lax.rem(me, ring)
    steps_z = (1, 3, 2)
    steps_y = (1, 3, 2)[:cols - 1] if cols > 2 else (1,)
    along_z = lambda i: my_y * ring + lax.rem(my_z + i, ring)
    along_y = lambda i: lax.rem(my_y + i, cols) * ring + my_z

    def relay(h, slot, sem, peer):
        buffer = (da, db)[h]
        return pltpu.make_async_remote_copy(
            src_ref=buffer.at[slot], dst_ref=buffer.at[slot], send_sem=dep_ss.at[h, sem], recv_sem=dep_rs.at[h, slot],
            device_id={"bis": peer}, device_id_type=MESH,
        )

    for k in range(3):
        flrow[:, k, :] = (masses * beta) * (sampled[k] - speed[k])
    sent = []

    def send(h, slot, peer):
        copy = relay(h, slot, sum(1 for g, _ in sent if g == h), peer)
        copy.start()
        sent.append((h, copy))

    routes = ((along_z, steps_z, along_y, steps_y), (along_y, steps_y, along_z, steps_z))
    for h in range(2):
        lax.fori_loop(half * h, half * (h + 1), deposit, 0, unroll=16)
        buffer = (da, db)[h]
        for k in range(3):
            buffer[me, k] = dep[half * h:half * (h + 1), k, :]
        first, steps, _, _ = routes[h]
        for i in steps:
            send(h, me, first(i))
    for h in range(2):
        _, _, second, steps = routes[h]
        for i in steps:
            send(h, me, second(i))
    for h, i in [(h, i) for i in range(3) for h in range(2)]:
        first, steps, second, others = routes[h]
        if i >= len(steps):
            continue
        slot = first(-steps[i] + (ring if h == 0 else cols))
        relay(h, slot, 0, lax.rem(me + 1, bis)).wait_recv()
        for i in others:
            send(h, slot, second(i))
    for y in range(1, cols):
        for z in range(ring):
            relay(0, lax.rem(my_y + y, cols) * ring + z, 0, lax.rem(me + 1, bis)).wait_recv()
    for y in range(cols):
        for z in range(1, ring):
            relay(1, y * ring + lax.rem(my_z + z, ring), 0, lax.rem(me + 1, bis)).wait_recv()

    def reduce(values_of):
        acc = jnp.zeros((BLK, BLK), F32)
        for t in range(tiles):
            values = jnp.concatenate([values_of(t, h).reshape(BLK // 2, BLK) for h in range(2)], axis=0)
            for piece in split(values, 2)[::-1]:
                acc = acc + jnp.dot(oh_ref[t], piece.astype(BF16), preferred_element_type=F32)
        return acc

    void = void_out[...]
    for k in range(3):
        total = reduce(lambda t, h: (da, db)[h][per * t:per * (t + 1), k])
        fluid_out[k] = fluid_ref[k] - FLUID_GAIN * total * void
        results[3 + k].start()
    for _, copy in sent:
        copy.wait_send()
    for copy in results:
        copy.wait()


def copy_out(*refs):
    sem = refs[-1]
    count = len(refs) // 2
    copies = [pltpu.make_async_copy(refs[k], refs[count + k], sem.at[k]) for k in range(count)]
    for copy in copies:
        copy.start()
    for copy in copies:
        copy.wait()


def local(
    bis, dom, positions, velocities, radii, drag_rates, mig_slots, mig_counts, pair_lists, pair_counts, owners, dep_weights, fluid_velocity,
):
    nb = positions.shape[1]
    levels, capacity = mig_slots.shape[1:]
    pmax = pair_lists.shape[2]
    fb = fluid_velocity.shape[1]
    vmem = pl.BlockSpec(memory_space=pltpu.VMEM)
    smem = pl.BlockSpec(memory_space=pltpu.SMEM)
    hbm = pl.BlockSpec(memory_space=pltpu.HBM)
    dma = pltpu.SemaphoreType.DMA
    tiles = bis * nb // BLK
    outs = pl.pallas_call(
        functools.partial(kernel, bis, dom, pmax),
        out_shape=(
            jax.ShapeDtypeStruct((3, nb, BLK), F32),
            jax.ShapeDtypeStruct((3, nb, BLK), F32),
            jax.ShapeDtypeStruct((3, fb, BLK), F32),
            jax.ShapeDtypeStruct((fb, BLK), F32),
        ),
        in_specs=[hbm] * 12,
        out_specs=(hbm,) * 4,
        scratch_shapes=[
            pltpu.SMEM((levels, 1, capacity), jnp.int32),
            pltpu.SMEM((1, levels), jnp.int32),
            pltpu.SMEM((2, pmax), jnp.int32),
            pltpu.SMEM((1, 1), jnp.int32),
            pltpu.VMEM((3, nb, BLK), F32),
            pltpu.VMEM((3, nb, BLK), F32),
            pltpu.VMEM((3, fb, BLK), F32),
            pltpu.VMEM((fb, BLK), F32),
            pltpu.VMEM((3, nb, BLK), F32),
            pltpu.VMEM((3, nb, BLK), F32),
            pltpu.VMEM((nb, BLK), F32),
            pltpu.VMEM((nb, BLK), F32),
            pltpu.VMEM((2, pmax), jnp.int32),
            pltpu.VMEM((1, nb), jnp.int32),
            pltpu.VMEM((3, fb, BLK), F32),
            pltpu.VMEM((8, BLK), jnp.int32),
            pltpu.SMEM((8, BLK), jnp.int32),
            pltpu.VMEM((nb, 8, BLK), F32),
            pltpu.VMEM((nb, 8, BLK), F32),
            [pltpu.VMEM((capacity, 8, BLK), F32)] * (levels + 1),
            [pltpu.VMEM((capacity, 8, BLK), F32)] * (levels + 1),
            pltpu.VMEM((capacity, BLK), jnp.int32),
            pltpu.VMEM((capacity, BLK), jnp.int32),
            pltpu.VMEM((capacity, BLK), jnp.int32),
            pltpu.VMEM((SUBSTEPS, 2 * G, 8, BLK), F32),
            pltpu.VMEM((8, BLK), jnp.int32),
            pltpu.VMEM((bis, 8, BLK), jnp.int32),
            pltpu.VMEM((bis, nb, 3 * BLK), BF16),
            pltpu.VMEM((bis, nb, 3 * BLK), BF16),
            pltpu.VMEM((nb, BLK, BLK), BF16),
            pltpu.VMEM((nb, 8, BLK), F32),
            pltpu.VMEM((nb, 8, BLK), F32),
            pltpu.VMEM((nb + 2 * G, BLK, 64), BF16),
            pltpu.VMEM((nb + 2 * G, 4, BLK, BLK), F32),
            pltpu.VMEM((nb, 64, 2 * BLK), BF16),
            pltpu.VMEM((pmax, 8, BLK), F32),
            pltpu.VMEM((64, 4 * BLK), BF16),
            pltpu.VMEM((tiles, BLK, BLK), BF16),
            pltpu.VMEM((nb, 8, BLK), F32),
            pltpu.VMEM((nb, BLK), F32),
            pltpu.VMEM((bis, nb, BLK), F32),
            pltpu.VMEM((bis, 3, nb // 2, BLK), F32),
            pltpu.VMEM((bis, 3, nb // 2, BLK), F32),
            dma((11,)),
            dma,
            dma((6,)),
            dma,
            dma((6,)),
            dma((6,)),
            dma((SUBSTEPS, 2)),
            dma((SUBSTEPS, 2)),
            dma((bis,)),
            dma((bis,)),
            dma((bis,)),
            dma((bis,)),
            dma((bis,)),
            dma((bis,)),
            dma((2, bis)),
            dma((2, bis)),
        ],
        compiler_params=pltpu.CompilerParams(
            collective_id=0, has_side_effects=True, vmem_limit_bytes=64 * 1024 * 1024
        ),
    )(
        jnp.transpose(positions[0], (1, 0, 2)),
        jnp.transpose(velocities[0], (1, 0, 2)),
        radii[0],
        drag_rates[0],
        jnp.transpose(mig_slots, (1, 0, 2)),
        mig_counts,
        pair_lists[0],
        pair_counts,
        pair_lists[0],
        owners,
        dep_weights[0],
        jnp.transpose(fluid_velocity[0], (1, 0, 2)),
    )
    pos, vel, fluid, void = pl.pallas_call(
        copy_out,
        out_shape=tuple(jax.ShapeDtypeStruct(out.shape, out.dtype) for out in outs),
        in_specs=[vmem] * 4,
        out_specs=(hbm,) * 4,
        scratch_shapes=[dma((4,))],
        compiler_params=pltpu.CompilerParams(vmem_limit_bytes=64 * 1024 * 1024),
    )(*outs)
    return (
        jnp.transpose(pos, (1, 0, 2))[None],
        jnp.transpose(vel, (1, 0, 2))[None],
        jnp.transpose(fluid, (1, 0, 2))[None],
        void[None],
    )


def solution(mesh):
    in_specs = (
        P("bis", "dom", None, None),
        P("bis", "dom", None, None),
        P("bis", "dom", None),
        P("bis", "dom", None),
        P("bis", "dom", None),
        P("bis", "dom"),
        P("bis", None, "dom"),
        P("bis", "dom"),
        P("bis", "dom"),
        P("bis", "dom", None, None),
        P("dom", "bis", None, None),
    )
    out_specs = (
        P("bis", "dom", None, None),
        P("bis", "dom", None, None),
        P("dom", "bis", None, None),
        P("dom", "bis", None),
    )
    body = functools.partial(local, mesh.shape["bis"], mesh.shape["dom"])
    return jax.shard_map(body, mesh=mesh, in_specs=in_specs, out_specs=out_specs, check_vma=False)
```

```python
import functools

import jax
import jax.numpy as jnp
from jax import lax
from jax.experimental import pallas as pl
from jax.experimental.pallas import tpu as pltpu
from jax.sharding import PartitionSpec as P

G = 4
SUBSTEPS = 2
BLK = 128

STIFFNESS = 5.0
DAMPING = 1.0
TIME_STEP = 0.05
EPS_DIST = 0.0001
RADIUS_REF = 0.1
FLUID_GAIN = 0.2

F32 = jnp.float32
BF16 = jnp.bfloat16
MESH = pl.DeviceIdType.MESH


def row_ids():
    return lax.broadcasted_iota(jnp.int32, (8, BLK), 0)


def stack_rows(rows):
    row = row_ids()
    out = jnp.zeros((8, BLK), F32)
    for k, value in enumerate(rows):
        out = jnp.where(row == k, value, out)
    return out


def split(x, parts=3):
    out = []
    for _ in range(parts):
        piece = x.astype(BF16).astype(F32)
        out.append(piece)
        x = x - piece
    return out


def centered(blk):
    return jnp.where(row_ids() < 3, blk - 0.5, blk)


def partner_features(blk):
    row = row_ids()
    y = centered(blk)
    sq = jnp.sum(y[0:3] * y[0:3], axis=0, keepdims=True)
    sv = jnp.sum(y[0:3] * y[3:6], axis=0, keepdims=True)
    base = jnp.where(row < 6, y, jnp.where(row == 6, 1.0, y[6:7]))
    s1, s2, s3 = split(base)
    e = stack_rows(split(sq) + split(sv))
    zero = jnp.zeros((8, BLK), F32)
    return jnp.concatenate([zero, s1, s1, s1, s2, s2, s3, e], axis=0)


def local_features(blk):
    row = row_ids()
    zero = jnp.zeros((8, BLK), F32)
    y = centered(blk)
    sq = jnp.sum(y[0:3] * y[0:3], axis=0, keepdims=True) + EPS_DIST
    sv = jnp.sum(y[0:3] * y[3:6], axis=0, keepdims=True)
    wd = jnp.where(row < 3, -2.0 * y, jnp.where(row == 6, sq, 0.0))
    wv = jnp.concatenate([-y[3:6], -y[0:3], sv, jnp.zeros((1, BLK), F32)], axis=0)
    p1, p2, p3 = split(wd)
    v1, v2, v3 = split(wv)
    ed = jnp.where(row < 3, 1.0, 0.0)
    ev = jnp.where((row >= 3) & (row < 6), 1.0, 0.0)
    d = jnp.concatenate([zero, p1, p2, p3, p1, p2, p1, ed], axis=0)
    v = jnp.concatenate([zero, v1, v2, v3, v1, v2, v1, ev], axis=0)
    return jnp.concatenate([d, v], axis=1).astype(BF16)


def kernel(
    bis, dom, pmax,
    pos_hbm, vel_hbm, rad_hbm, drag_hbm, slots_hbm, moved_hbm, pairs_hbm, cnt_hbm, left_hbm, own_hbm, w_hbm, fluid_hbm,
    pos_hbm_out, vel_hbm_out, fluid_hbm_out, void_hbm_out,
    slots_ref, moved_ref, pairs_ref, cnt_ref,
    pos_out, vel_out, fluid_out, void_out, pos_ref, vel_ref, rad_ref, drag_ref, left_ref, own_ref, fluid_ref, inv_v, inv_ref,
    st0, st1, mig_s, mig_r, from_s, from_near, from_far, halo_r, own_s, own_r, fl_s, fl_r, w_v, flrow, samp,
    a_ref, xb_ref, b_ref, f_ref, sel_ref, oh_ref, dep, mass_s, mass_r, da, db,
    in_sem, inv_sem, out_sem, w_sem, mig_ss, mig_rs, halo_ss, halo_rs, own_ss, own_rs, fl_ss, fl_rs, mass_ss, mass_rs, dep_ss, dep_rs,
):
    nb = st0.shape[0]
    per = BLK // nb
    tiles = bis // per
    me = lax.axis_index("bis")
    mine = lax.axis_index("dom")
    right, left = lax.rem(mine + 1, dom), lax.rem(mine + dom - 1, dom)

    barrier = pltpu.get_barrier_semaphore()

    def greet(r, _):
        pl.semaphore_signal(barrier, inc=1, device_id={"bis": lax.rem(me + r, bis)}, device_id_type=MESH)
        return 0

    lax.fori_loop(1, bis, greet, 0)
    for side in (left, right):
        pl.semaphore_signal(barrier, inc=1, device_id={"dom": side}, device_id_type=MESH)

    inputs = [
        pltpu.make_async_copy(src, dst, in_sem.at[k])
        for k, (src, dst) in enumerate((
            (pos_hbm, pos_ref), (vel_hbm, vel_ref), (rad_hbm, rad_ref), (drag_hbm, drag_ref),
            (own_hbm, own_ref), (left_hbm, left_ref), (fluid_hbm, fluid_ref),
            (slots_hbm, slots_ref), (moved_hbm, moved_ref), (pairs_hbm, pairs_ref), (cnt_hbm, cnt_ref),
        ))
    ]
    for copy in inputs:
        copy.start()
    weights_copy = pltpu.make_async_copy(w_hbm, w_v, w_sem)
    weights_copy.start()

    def to_peer(r, source, target, ss, rs):
        peer = lax.rem(me + r, bis)
        return pltpu.make_async_remote_copy(
            src_ref=source(peer), dst_ref=target.at[me], send_sem=ss.at[r], recv_sem=rs.at[r],
            device_id={"bis": peer}, device_id_type=MESH,
        )

    def start_all(source, target, ss, rs):
        def step(r, _):
            to_peer(r, source, target, ss, rs).start()
            return 0

        lax.fori_loop(1, bis, step, 0)

    def wait_all(source, target, ss, rs):
        def step(r, _):
            to_peer(r, source, target, ss, rs).wait()
            return 0

        lax.fori_loop(1, bis, step, 0)

    for copy in inputs[7:]:
        copy.wait()
    lane8 = lax.broadcasted_iota(jnp.int32, (8, BLK), 1)
    capacity = slots_ref.shape[2]
    places = jnp.full((8, BLK), -1, jnp.int32)
    for level in range(slots_ref.shape[0]):
        for j in range(capacity):
            here = (lane8 == slots_ref[level, 0, j]) & (row_ids() == level) & (moved_ref[0, level] > j)
            places = jnp.where(here, j, places)
    inv_v[...] = places
    inv_copy = pltpu.make_async_copy(inv_v, inv_ref, inv_sem)
    inv_copy.start()
    for copy in inputs[:6]:
        copy.wait()
    own_s[...] = jnp.zeros((8, BLK), jnp.int32)
    own_s[:, 0:nb] = jnp.broadcast_to(own_ref[...], (8, nb))
    quarter = lax.rem(me, per)
    half = nb // 2
    owners = own_s[...]
    low = pltpu.roll(jnp.where(lane8 < half, owners, 0), half * quarter, 1)
    high = pltpu.roll(jnp.where((lane8 >= half) & (lane8 < nb), owners, 0), BLK // 2 - half + half * quarter, 1)
    own_s[...] = low + high
    for k in range(3):
        st0[:, k, :] = pos_ref[k]
        st0[:, 3 + k, :] = vel_ref[k]
    st0[:, 6, :] = rad_ref[...]
    st0[:, 7, :] = drag_ref[...]
    own_r[me] = own_s[...]

    def gather(level, target):
        def step(j, _):
            target[j] = st0[slots_ref[level, 0, j]]
            return 0

        lax.fori_loop(0, capacity, step, 0, unroll=16)

    def flip(level):
        stride = 2**level
        return stride - 2 * stride * lax.rem(me // stride, 2)

    def migrate_copy(k, source, target, partner):
        return pltpu.make_async_remote_copy(
            src_ref=source, dst_ref=target, send_sem=mig_ss.at[k], recv_sem=mig_rs.at[k],
            device_id={"bis": partner}, device_id_type=MESH,
        )

    def scatter(level, arrived):
        def step(n, _):
            j = inv_ref[level, n]
            st0[n] = jnp.where(j >= 0, arrived[jnp.maximum(j, 0)], st0[n])
            return 0

        lax.fori_loop(0, nb, step, 0, unroll=16)

    near, far = me + flip(1), me + flip(2)
    both = far + flip(1)
    level0 = migrate_copy(0, mig_s[0], mig_r[0], me + flip(0))
    table_near = migrate_copy(1, from_s, from_near, near)
    table_far = migrate_copy(2, from_s, from_far, far)
    level1 = migrate_copy(3, mig_s[1], mig_r[1], near)
    level2 = migrate_copy(4, mig_s[2], mig_r[2], far)
    level12 = migrate_copy(5, mig_s[3], mig_r[3], both)

    def make_table():
        row = lax.broadcasted_iota(jnp.int32, (capacity, BLK), 0)
        table = jnp.zeros((capacity, BLK), jnp.int32)
        for j in range(capacity):
            table = jnp.where(row == j, inv_ref[1, slots_ref[2, 0, j]], table)
        from_s[...] = table

    def pick_for_both():
        def step(j, _):
            want = from_near[pl.ds(j, 1), :]
            block = jnp.zeros((8, BLK), F32)
            for k in range(capacity):
                block = jnp.where(want == k, mig_s[1][k], block)
            mig_s[3][j] = block
            return 0

        lax.fori_loop(0, capacity, step, 0, unroll=16)

    def merge_level2():
        def step(j, _):
            mig_r[2][j] = jnp.where(from_far[pl.ds(j, 1), :] >= 0, mig_r[3][j], mig_r[2][j])
            return 0

        lax.fori_loop(0, capacity, step, 0, unroll=16)

    gather(0, mig_s[0])
    inv_copy.wait()
    make_table()
    pl.semaphore_wait(barrier, bis - 1 + 2)
    level0.start()
    table_near.start()
    table_far.start()
    own_source = lambda peer: own_s
    start_all(own_source, own_r, own_ss, own_rs)
    srow = lax.broadcasted_iota(jnp.int32, (64, BLK), 0)
    part = (srow >= 8) & (srow < 56)
    first = (srow // 8 == 1) | (srow // 8 == 4) | (srow // 8 == 6)
    for c, ch in enumerate((0, 1, 2, 7)):
        sel_ref[:, c * BLK:(c + 1) * BLK] = jnp.where(first & part & (lax.rem(srow, 8) == ch), 1.0, 0.0).astype(BF16)
    level0.wait()
    scatter(0, mig_r[0])
    gather(1, mig_s[1])
    level1.start()
    gather(2, mig_s[2])
    level2.start()
    table_near.wait()
    pick_for_both()
    level12.start()

    wait_all(own_source, own_r, own_ss, own_rs)
    inputs[6].wait()
    fluid_bf = jnp.concatenate([fluid_ref[k].astype(BF16) for k in range(3)], axis=1)
    rows = []
    for t in range(tiles):
        row = own_r[per * t, 0:1, :]
        for i in range(1, per):
            row = row + own_r[per * t + i, 0:1, :]
        rows.append(row - BLK * me)
    sub = lax.broadcasted_iota(jnp.int32, (BLK, BLK), 0)
    for t in range(tiles):
        hot = jnp.where(sub == rows[t], 1.0, 0.0)
        oh_ref[t] = hot.astype(BF16)
        chosen = jnp.dot(hot.T.astype(BF16), fluid_bf, preferred_element_type=F32).astype(BF16)
        for i in range(per):
            for h in range(2):
                first_row = BLK // 2 * h + half * i
                fl_s[per * t + i, half * h:half * (h + 1)] = chosen[first_row:first_row + half]
    fl_r[me] = fl_s[me]
    fl_source = lambda peer: fl_s.at[peer]

    level1.wait()
    scatter(1, mig_r[1])
    table_far.wait()
    level2.wait()
    level12.wait()
    merge_level2()
    scatter(2, mig_r[2])

    def halo_copies(step, state):
        return [
            pltpu.make_async_remote_copy(
                src_ref=state.at[pl.ds(nb - G, G)], dst_ref=halo_r.at[step, pl.ds(0, G)],
                send_sem=halo_ss.at[step, 0], recv_sem=halo_rs.at[step, 0],
                device_id={"dom": right}, device_id_type=MESH,
            ),
            pltpu.make_async_remote_copy(
                src_ref=state.at[pl.ds(0, G)], dst_ref=halo_r.at[step, pl.ds(G, G)],
                send_sem=halo_ss.at[step, 1], recv_sem=halo_rs.at[step, 1],
                device_id={"dom": left}, device_id_type=MESH,
            ),
        ]


    def prepare(step, blk, j):
        t = partner_features(blk).T.astype(BF16)
        a_ref[j] = t
        count = 4 - step
        wide = jnp.dot(t, sel_ref[:, 0:count * BLK], preferred_element_type=F32)
        for c in range(count):
            xb_ref[j, c] = wide[:, c * BLK:(c + 1) * BLK]

    mass_source = lambda peer: mass_s

    def deposit(n, _):
        dep[n] = jnp.dot(flrow[n].astype(BF16), w_v[n], preferred_element_type=F32)
        return 0

    def load_mass():
        flrow[...] = jnp.zeros(flrow.shape, F32)
        flrow[:, 0, :] = (st0[:, 6, :] / RADIUS_REF) ** 3
        weights_copy.wait()

    def send_mass():
        mass_s[...] = dep[:, 0, :]
        mass_r[me] = mass_s[...]
        start_all(mass_source, mass_r, mass_ss, mass_rs)

    def solid_volume():
        wait_all(mass_source, mass_r, mass_ss, mass_rs)
        solid = jnp.zeros((BLK, BLK), F32)
        for t in range(tiles):
            values = jnp.concatenate([
                mass_r[per * t:per * (t + 1), half * h:half * (h + 1)].reshape(BLK // 2, BLK) for h in range(2)
            ], axis=0)
            for piece in split(values, 2)[::-1]:
                solid = solid + jnp.dot(oh_ref[t], piece.astype(BF16), preferred_element_type=F32)
        void_out[...] = 1.0 / (1.0 + solid)

    def gather_fluid():
        wait_all(fl_source, fl_r, fl_ss, fl_rs)
        total = fl_r[0].astype(F32)
        for g in range(1, bis):
            total = total + fl_r[g].astype(F32)
        for k in range(3):
            flrow[:, k, :] = total[:, k * BLK:(k + 1) * BLK]

    def sample(n, _):
        samp[n] = lax.dot_general(
            flrow[n].astype(BF16), w_v[n], (((1,), (1,)), ((), ())), preferred_element_type=F32
        )

    def contacts(step, state):
        for copy in halo_copies(step, state):
            copy.start()
        if step == 0:
            start_all(fl_source, fl_r, fl_ss, fl_rs)

        def own_blocks(n, _):
            blk = state[n]
            prepare(step, blk, n + G)
            b_ref[n] = local_features(blk)
            return 0

        lax.fori_loop(0, nb, own_blocks, 0, unroll=8)
        if step == 1:
            solid_volume()
        for copy in halo_copies(step, state):
            copy.wait()

        def rim(n, _):
            prepare(step, halo_r[step, n], n)
            prepare(step, halo_r[step, n + G], n + nb + G)
            return 0

        lax.fori_loop(0, G, rim, 0, unroll=4)

        def pair(i, _):
            a = jnp.minimum(pairs_ref[0, i], nb - 1)
            b = pairs_ref[1, i]
            blk = centered(state[a])
            z = jnp.dot(a_ref[b], b_ref[a], preferred_element_type=F32)
            inv = lax.rsqrt(jnp.maximum(z[:, :BLK], EPS_DIST))
            depth = jnp.maximum((xb_ref[b, 3] + blk[6:7]) * inv - 1.0, 0.0)
            f = depth * (STIFFNESS - DAMPING * z[:, BLK:] * inv)
            total = jnp.sum(f, axis=0, keepdims=True)
            f_ref[i] = stack_rows([
                blk[k:k + 1] * total - jnp.sum(f * xb_ref[b, k], axis=0, keepdims=True) for k in range(3)
            ])
            return 0

        def beside(begin, end, turns, extra):
            pairs_each, blocks_each = (end - begin) // turns, nb // turns

            def mixed(turn, _):
                for u in range(pairs_each):
                    pair(begin + turn * pairs_each + u, 0)
                    for v in range(blocks_each * u // pairs_each, blocks_each * (u + 1) // pairs_each):
                        extra(turn * blocks_each + v, 0)
                return 0

            lax.fori_loop(0, turns, mixed, 0)

        if step == 0:
            first = pmax * 2 // 3
            load_mass()
            beside(0, first, 4 if first % 4 == 0 else 2, deposit)
            send_mass()
            gather_fluid()
            beside(first, pmax, 2, sample)
        else:
            lax.fori_loop(0, pmax, pair, 0, unroll=min(48, pmax))
        lane = lax.broadcasted_iota(jnp.int32, (nb, pmax), 1)
        blk_id = lax.broadcasted_iota(jnp.int32, (nb, pmax), 0)
        hot = jnp.where((left_ref[0:1] == blk_id) & (lane < cnt_ref[0, 0]), 1.0, 0.0).astype(BF16)
        hi, lo = split(jnp.concatenate([f_ref[:, k, :] for k in range(3)], axis=1), 2)
        acc = jnp.dot(hot, lo.astype(BF16), preferred_element_type=F32)
        acc = acc + jnp.dot(hot, hi.astype(BF16), preferred_element_type=F32)
        return [acc[:, k * BLK:(k + 1) * BLK] for k in range(3)]

    radius, beta = None, None
    for substep in range(SUBSTEPS):
        state = (st0, st1)[substep]
        contact = contacts(substep, state)
        if substep == 0:
            sampled = [samp[:, k, :] for k in range(3)]
            radius, beta = st0[:, 6, :], st0[:, 7, :]
            masses = (radius / RADIUS_REF) ** 3
        speed, place = [], []
        for k in range(3):
            v = state[:, 3 + k, :]
            v = v + TIME_STEP * (contact[k] / masses + beta * (sampled[k] - v))
            speed.append(v)
            place.append(state[:, k, :] + TIME_STEP * v)
        if substep + 1 < SUBSTEPS:
            for k in range(3):
                st1[:, k, :] = place[k]
                st1[:, 3 + k, :] = speed[k]
            st1[:, 6, :] = radius
            st1[:, 7, :] = beta
    for k in range(3):
        pos_out[k] = place[k]
        vel_out[k] = speed[k]
    results = [
        pltpu.make_async_copy(src, dst, out_sem.at[k])
        for k, (src, dst) in enumerate(
            [(pos_out, pos_hbm_out), (vel_out, vel_hbm_out), (void_out, void_hbm_out)]
            + [(fluid_out.at[k], fluid_hbm_out.at[k]) for k in range(3)]
        )
    ]
    for copy in results[:3]:
        copy.start()

    ring = 4
    cols = bis // ring
    my_y, my_z = me // ring, lax.rem(me, ring)
    steps_z = (1, 3, 2)
    steps_y = (1, 3, 2)[:cols - 1] if cols > 2 else (1,)
    along_z = lambda i: my_y * ring + lax.rem(my_z + i, ring)
    along_y = lambda i: lax.rem(my_y + i, cols) * ring + my_z

    def relay(h, slot, sem, peer):
        buffer = (da, db)[h]
        return pltpu.make_async_remote_copy(
            src_ref=buffer.at[slot], dst_ref=buffer.at[slot], send_sem=dep_ss.at[h, sem], recv_sem=dep_rs.at[h, slot],
            device_id={"bis": peer}, device_id_type=MESH,
        )

    for k in range(3):
        flrow[:, k, :] = (masses * beta) * (sampled[k] - speed[k])
    sent = []

    def send(h, slot, peer):
        copy = relay(h, slot, sum(1 for g, _ in sent if g == h), peer)
        copy.start()
        sent.append((h, copy))

    routes = ((along_z, steps_z, along_y, steps_y), (along_y, steps_y, along_z, steps_z))
    for h in range(2):
        lax.fori_loop(half * h, half * (h + 1), deposit, 0, unroll=16)
        buffer = (da, db)[h]
        for k in range(3):
            buffer[me, k] = dep[half * h:half * (h + 1), k, :]
        first, steps, _, _ = routes[h]
        for i in steps:
            send(h, me, first(i))
    for h in range(2):
        _, _, second, steps = routes[h]
        for i in steps:
            send(h, me, second(i))
    for h, i in [(h, i) for i in range(3) for h in range(2)]:
        first, steps, second, others = routes[h]
        if i >= len(steps):
            continue
        slot = first(-steps[i] + (ring if h == 0 else cols))
        relay(h, slot, 0, lax.rem(me + 1, bis)).wait_recv()
        for i in others:
            send(h, slot, second(i))
    for y in range(1, cols):
        for z in range(ring):
            relay(0, lax.rem(my_y + y, cols) * ring + z, 0, lax.rem(me + 1, bis)).wait_recv()
    for y in range(cols):
        for z in range(1, ring):
            relay(1, y * ring + lax.rem(my_z + z, ring), 0, lax.rem(me + 1, bis)).wait_recv()

    def reduce(values_of):
        acc = jnp.zeros((BLK, BLK), F32)
        for t in range(tiles):
            values = jnp.concatenate([values_of(t, h).reshape(BLK // 2, BLK) for h in range(2)], axis=0)
            hi, lo = split(values, 2)
            both = jnp.concatenate([hi, lo], axis=0).astype(BF16)
            hot = jnp.concatenate([oh_ref[t], oh_ref[t]], axis=1)
            acc = acc + jnp.dot(hot, both, preferred_element_type=F32)
        return acc

    void = void_out[...]
    for k in range(3):
        total = reduce(lambda t, h: (da, db)[h][per * t:per * (t + 1), k])
        fluid_out[k] = fluid_ref[k] - FLUID_GAIN * total * void
        results[3 + k].start()
    for _, copy in sent:
        copy.wait_send()
    for copy in results:
        copy.wait()


def copy_out(*refs):
    sem = refs[-1]
    count = len(refs) // 2
    copies = [pltpu.make_async_copy(refs[k], refs[count + k], sem.at[k]) for k in range(count)]
    for copy in copies:
        copy.start()
    for copy in copies:
        copy.wait()


def local(
    bis, dom, positions, velocities, radii, drag_rates, mig_slots, mig_counts, pair_lists, pair_counts, owners, dep_weights, fluid_velocity,
):
    nb = positions.shape[1]
    levels, capacity = mig_slots.shape[1:]
    pmax = pair_lists.shape[2]
    fb = fluid_velocity.shape[1]
    vmem = pl.BlockSpec(memory_space=pltpu.VMEM)
    smem = pl.BlockSpec(memory_space=pltpu.SMEM)
    hbm = pl.BlockSpec(memory_space=pltpu.HBM)
    dma = pltpu.SemaphoreType.DMA
    tiles = bis * nb // BLK
    outs = pl.pallas_call(
        functools.partial(kernel, bis, dom, pmax),
        out_shape=(
            jax.ShapeDtypeStruct((3, nb, BLK), F32),
            jax.ShapeDtypeStruct((3, nb, BLK), F32),
            jax.ShapeDtypeStruct((3, fb, BLK), F32),
            jax.ShapeDtypeStruct((fb, BLK), F32),
        ),
        in_specs=[hbm] * 12,
        out_specs=(hbm,) * 4,
        scratch_shapes=[
            pltpu.SMEM((levels, 1, capacity), jnp.int32),
            pltpu.SMEM((1, levels), jnp.int32),
            pltpu.SMEM((2, pmax), jnp.int32),
            pltpu.SMEM((1, 1), jnp.int32),
            pltpu.VMEM((3, nb, BLK), F32),
            pltpu.VMEM((3, nb, BLK), F32),
            pltpu.VMEM((3, fb, BLK), F32),
            pltpu.VMEM((fb, BLK), F32),
            pltpu.VMEM((3, nb, BLK), F32),
            pltpu.VMEM((3, nb, BLK), F32),
            pltpu.VMEM((nb, BLK), F32),
            pltpu.VMEM((nb, BLK), F32),
            pltpu.VMEM((2, pmax), jnp.int32),
            pltpu.VMEM((1, nb), jnp.int32),
            pltpu.VMEM((3, fb, BLK), F32),
            pltpu.VMEM((8, BLK), jnp.int32),
            pltpu.SMEM((8, BLK), jnp.int32),
            pltpu.VMEM((nb, 8, BLK), F32),
            pltpu.VMEM((nb, 8, BLK), F32),
            [pltpu.VMEM((capacity, 8, BLK), F32)] * (levels + 1),
            [pltpu.VMEM((capacity, 8, BLK), F32)] * (levels + 1),
            pltpu.VMEM((capacity, BLK), jnp.int32),
            pltpu.VMEM((capacity, BLK), jnp.int32),
            pltpu.VMEM((capacity, BLK), jnp.int32),
            pltpu.VMEM((SUBSTEPS, 2 * G, 8, BLK), F32),
            pltpu.VMEM((8, BLK), jnp.int32),
            pltpu.VMEM((bis, 8, BLK), jnp.int32),
            pltpu.VMEM((bis, nb, 3 * BLK), BF16),
            pltpu.VMEM((bis, nb, 3 * BLK), BF16),
            pltpu.VMEM((nb, BLK, BLK), BF16),
            pltpu.VMEM((nb, 8, BLK), F32),
            pltpu.VMEM((nb, 8, BLK), F32),
            pltpu.VMEM((nb + 2 * G, BLK, 64), BF16),
            pltpu.VMEM((nb + 2 * G, 4, BLK, BLK), F32),
            pltpu.VMEM((nb, 64, 2 * BLK), BF16),
            pltpu.VMEM((pmax, 8, BLK), F32),
            pltpu.VMEM((64, 4 * BLK), BF16),
            pltpu.VMEM((tiles, BLK, BLK), BF16),
            pltpu.VMEM((nb, 8, BLK), F32),
            pltpu.VMEM((nb, BLK), F32),
            pltpu.VMEM((bis, nb, BLK), F32),
            pltpu.VMEM((bis, 3, nb // 2, BLK), F32),
            pltpu.VMEM((bis, 3, nb // 2, BLK), F32),
            dma((11,)),
            dma,
            dma((6,)),
            dma,
            dma((6,)),
            dma((6,)),
            dma((SUBSTEPS, 2)),
            dma((SUBSTEPS, 2)),
            dma((bis,)),
            dma((bis,)),
            dma((bis,)),
            dma((bis,)),
            dma((bis,)),
            dma((bis,)),
            dma((2, bis)),
            dma((2, bis)),
        ],
        compiler_params=pltpu.CompilerParams(
            collective_id=0, has_side_effects=True, vmem_limit_bytes=64 * 1024 * 1024
        ),
    )(
        jnp.transpose(positions[0], (1, 0, 2)),
        jnp.transpose(velocities[0], (1, 0, 2)),
        radii[0],
        drag_rates[0],
        jnp.transpose(mig_slots, (1, 0, 2)),
        mig_counts,
        pair_lists[0],
        pair_counts,
        pair_lists[0],
        owners,
        dep_weights[0],
        jnp.transpose(fluid_velocity[0], (1, 0, 2)),
    )
    pos, vel, fluid, void = pl.pallas_call(
        copy_out,
        out_shape=tuple(jax.ShapeDtypeStruct(out.shape, out.dtype) for out in outs),
        in_specs=[vmem] * 4,
        out_specs=(hbm,) * 4,
        scratch_shapes=[dma((4,))],
        compiler_params=pltpu.CompilerParams(vmem_limit_bytes=64 * 1024 * 1024),
    )(*outs)
    return (
        jnp.transpose(pos, (1, 0, 2))[None],
        jnp.transpose(vel, (1, 0, 2))[None],
        jnp.transpose(fluid, (1, 0, 2))[None],
        void[None],
    )


def solution(mesh):
    in_specs = (
        P("bis", "dom", None, None),
        P("bis", "dom", None, None),
        P("bis", "dom", None),
        P("bis", "dom", None),
        P("bis", "dom", None),
        P("bis", "dom"),
        P("bis", None, "dom"),
        P("bis", "dom"),
        P("bis", "dom"),
        P("bis", "dom", None, None),
        P("dom", "bis", None, None),
    )
    out_specs = (
        P("bis", "dom", None, None),
        P("bis", "dom", None, None),
        P("dom", "bis", None, None),
        P("dom", "bis", None),
    )
    body = functools.partial(local, mesh.shape["bis"], mesh.shape["dom"])
    return jax.shard_map(body, mesh=mesh, in_specs=in_specs, out_specs=out_specs, check_vma=False)
```
